128 devices in a mesh: dp: 4 (over y_hi, core), fsdp: 32 (over x, z, y_lo).
Axes of the slice: x: 4, y: 4 (y_hi: 2, y_lo: 2; y = y_hi * 2 + y_lo), z: 4, core: 2. Of those that a mesh axis runs over, the one named last changes fastest.
Arguments:
- tokens: bfloat16 [2048, 4096], P('dp', 'fsdp'), may hold values from -6 to 6
- gate_weight: bfloat16 [4096, 16384], P(None, 'fsdp'), may hold values from -0.09375 to 0.09375
- up_weight: bfloat16 [4096, 16384], P(None, 'fsdp'), may hold values from -0.09375 to 0.09375
- down_weight: bfloat16 [16384, 4096], P('fsdp'), may hold values from -0.09375 to 0.09375
- curvature: float32 [2048, 4096], P('dp', 'fsdp'), may hold values from 0.5 to 4
- start: float32 [4096, 16384], P('dp', 'fsdp'), may hold values from -18 to 18
Outputs:
- coefficients: float32 [4], replicated
- next_vector: float32 [4096, 16384], P('dp', 'fsdp')
The draws below stay inside these ranges and needn't reach their ends.
All inputs are finite; a program needn't handle non-finite values.
Results may differ from the reference program's by a relative error of at most 0.039.
Values may be sent and summed in bfloat16 or wider, within the bound.
No kernel may reach another device: no remote copies, remote signals or barrier semaphores. Data moves between devices by JAX's collectives and lax.ppermute only.
A program may use at most 128 MiB of HBM per device.

```python
import math
import jax
import jax.numpy as jnp
from jax import lax

D = 4096
FF = 16384
TOKENS = 2048
N_FSDP = 32


def rising_rows(ratio):
    position = jax.lax.broadcasted_iota(jnp.float32, (D, FF), 0) / (D - 1)
    return jnp.exp(math.log(ratio) * position)


def draw_start(key, part):
    key = jax.random.fold_in(key, 11)
    base = jnp.clip(jax.random.normal(key, (D, FF), jnp.float32), -6.0, 6.0)
    values = base * rising_rows(3.0)
    return values.astype(jnp.float32)


def strengthened(array, key, source, target, shards_of, factor):
    owner, partner = [(jnp.arange(array.shape[dim]) // (array.shape[dim] // shards_of)).reshape([-1 if axis == dim else 1 for axis in range(array.ndim)]) for dim in (source, target)]
    chosen = jax.random.permutation(key, shards_of)[partner]
    strong = (owner == chosen) | (owner == (partner + shards_of // 2) % shards_of)
    return jnp.where(strong, factor * array, array)


def block_scale(rng, shape, split, smallest, largest):
    loudness, own = 1.0, jax.random.fold_in(rng, 6)
    for dim, blocks in split:
        heights = jnp.exp(jax.random.uniform(jax.random.fold_in(own, dim), (blocks,), jnp.float32, smallest / len(split), largest / len(split)))
        loudness = loudness * jnp.repeat(heights, shape[dim] // blocks).reshape([-1 if axis == dim else 1 for axis in range(len(shape))])
    return loudness


def scatter_about(rng, dims, deviation, most, pieces=(), kind=jnp.bfloat16):
    factor_of = block_scale(rng, dims, pieces, -0.22, 0.18) if pieces else 1.0
    values = jax.random.normal(rng, dims, jnp.float32) * deviation * factor_of
    return jnp.minimum(jnp.maximum(values, -most), most).astype(kind)


def noise_with(rng, dims, scale, most, pieces, heavy, kind=jnp.bfloat16):
    entries = scale * jax.random.normal(rng, dims, jnp.float32)
    if pieces:
        entries = entries * block_scale(rng, dims, pieces, -0.22, 0.18)
    return jnp.clip(strengthened(entries, jax.random.fold_in(rng, 3), *heavy), -most, most).astype(kind)


def setup_inputs(seed: int = 0) -> dict:
    key_of = jax.random.split(jax.random.key(seed), 7)
    tokens = scatter_about(key_of[0], (TOKENS, D), 1.0, 6.0, ((0, 4), (1, 32)))
    gate_weight = scatter_about(key_of[1], (D, FF), D ** -0.5, 0.09375, ((1, 32),))
    up_weight = scatter_about(key_of[2], (D, FF), D ** -0.5, 0.09375, ((1, 32),))
    down_weight = noise_with(key_of[3], (FF, D), FF ** -0.5, 0.09375, ((0, 32),), (0, 1, 32, 2.75))
    curvature = jnp.clip(jnp.exp(math.log(4.0) - 2.0794415 * jax.random.uniform(key_of[4], (TOKENS, D), jnp.float32) ** block_scale(key_of[4], (TOKENS, D), ((0, 4), (1, 32)), -0.2, 0.2)), 0.5, 4.0)
    start = draw_start(jax.random.fold_in(key_of[6], 71), 0)
    return dict(tokens=tokens, gate_weight=gate_weight, up_weight=up_weight, down_weight=down_weight, curvature=curvature, start=start)


EPS = 1e-06

def down_sum(pushed, down_weight):
    width = FF // N_FSDP

    def step(running, block):
        begin = (block * width).astype(jnp.int32)
        left = lax.dynamic_slice_in_dim(pushed, begin, width, 1)
        right = lax.dynamic_slice_in_dim(down_weight, begin, width, 0)
        partial_sum = jnp.dot(left, right, preferred_element_type=jnp.float32).astype(jnp.bfloat16)
        partial_sum = lax.optimization_barrier(partial_sum)
        return (running + partial_sum.astype(jnp.float32), None)
    init = jnp.zeros((pushed.shape[0], down_weight.shape[1]), jnp.float32)
    result, _ = lax.scan(step, init, jnp.arange(N_FSDP, dtype=jnp.int32))
    return result

def reference(tokens, gate_weight, up_weight, down_weight, curvature, start):
    gate = jnp.dot(tokens, gate_weight, preferred_element_type=jnp.float32)
    up = jnp.dot(tokens, up_weight, preferred_element_type=jnp.float32)
    sigma = jax.nn.sigmoid(gate)
    slope = sigma * (1.0 + gate * (1.0 - sigma)) * up
    scale_inv = 1.0 / (D * FF)

    def inner(left, right):
        return jnp.sum(left * right) * scale_inv

    def curvature_product(vector):
        vector_b = vector.astype(jnp.bfloat16)
        tangent = jnp.dot(tokens, vector_b, preferred_element_type=jnp.float32)
        pushed = (slope * tangent).astype(jnp.bfloat16)
        moved = down_sum(pushed, down_weight)
        weighted = (curvature * moved / TOKENS).astype(jnp.bfloat16)
        back = jnp.dot(weighted, down_weight.T, preferred_element_type=jnp.float32)
        delta = (back * slope).astype(jnp.bfloat16)
        return jnp.dot(tokens.T, delta, preferred_element_type=jnp.float32)
    first = start / jnp.sqrt(inner(start, start) + EPS)
    image_one = curvature_product(first)
    alpha_one = inner(first, image_one)
    resid_one = image_one - alpha_one * first
    beta_one = jnp.sqrt(inner(resid_one, resid_one) + EPS)
    second = resid_one / beta_one
    image_two = curvature_product(second)
    alpha_two = inner(second, image_two)
    back_coef = inner(first, image_two)
    resid_two = image_two - alpha_two * second - back_coef * first
    beta_two = jnp.sqrt(inner(resid_two, resid_two) + EPS)
    next_vector = resid_two / beta_two
    coefficients = jnp.stack([alpha_one, beta_one, alpha_two, beta_two]).astype(jnp.float32)
    return (coefficients, next_vector)
```

```python
import functools
import jax
import jax.numpy as jnp
from jax import lax
from jax.experimental import pallas as pl
from jax.experimental.pallas import tpu as pltpu
from jax.sharding import Mesh
from jax.sharding import PartitionSpec as P

D = 4096
FF = 16384
EPS = 1e-06
SCALE_INV = 1.0 / (D * FF)
AXES = (("yh", 2), ("c", 2), ("x", 4), ("z", 4), ("yl", 2))
NAMES = tuple(name for name, _ in AXES)
SIZES = dict(AXES)
BF = jnp.bfloat16
F32 = jnp.float32
PARAMS = pltpu.CompilerParams(vmem_limit_bytes=40 * 1024 * 1024)
VM = pl.BlockSpec(memory_space=pltpu.VMEM)
SM = pl.BlockSpec(memory_space=pltpu.SMEM)


def shift(value, axis, by):
    n = SIZES[axis]
    return lax.ppermute(value, axis, [((i + by) % n, i) for i in range(n)])


def ring_pair(jobs):
    up = [shift(v, a, 1) for v, a in jobs]
    down = [shift(v, a, -1) for v, a in jobs]
    out = []
    for (v, a), p, m in zip(jobs, up, down):
        h = v.shape[-2] // 2
        far = [shift(p[..., :h, :], a, 1), shift(m[..., h:, :], a, -1)]
        out.append([v, p, jnp.concatenate(far, axis=-2), m])
    return out


def ring_direct(v, a):
    return [v, shift(v, a, 1), shift(v, a, 2), shift(v, a, 3)]


def assemble_tokens_kernel(pos, *refs):
    a, b, out = refs[:4], refs[4:8], refs[8]
    x, z = pos[0], pos[1]
    h = out.shape[0] // 2
    for i in range(4):
        for j in range(4):
            col = (lax.rem(x + j, 4) * 4 + lax.rem(z + i, 4)) * 256
            out[:h, pl.ds(pl.multiple_of(col, 256), 256)] = a[i][j]
            col = (lax.rem(x + i, 4) * 4 + lax.rem(z + j, 4)) * 256
            out[h:, pl.ds(pl.multiple_of(col, 256), 256)] = b[i][j]


def gather_tokens(pair, pos):
    h = pair.shape[0] // 2
    a, b = ring_pair([(pair[:h], "x"), (pair[h:], "z")])
    a, b = ring_pair([(jnp.stack(a), "z"), (jnp.stack(b), "x")])
    return pl.pallas_call(
        assemble_tokens_kernel,
        out_shape=jax.ShapeDtypeStruct((2 * h, D), BF),
        in_specs=[SM] + [VM] * 8,
        out_specs=VM,
        compiler_params=PARAMS,
        name="assemble",
    )(pos, *a, *b)


def nt(a, b):
    return lax.dot_general(a, b, (((1,), (1,)), ((), ())), preferred_element_type=F32)


def tn(a, b):
    return lax.dot_general(a, b, (((0,), (0,)), ((), ())), preferred_element_type=F32)


def nn(a, b):
    return jnp.dot(a, b, preferred_element_type=F32)


def split_kernel(pos, down, keep, send):
    yl = pos[2]
    for b in range(16):
        keep[:, b * 128:(b + 1) * 128] = down[:, pl.ds(pl.multiple_of((2 * b + yl) * 128, 128), 128)]
        send[:, b * 128:(b + 1) * 128] = down[:, pl.ds(pl.multiple_of((2 * b + 1 - yl) * 128, 128), 128)]


def tangent_kernel(pos, feats, *refs):
    out = refs[4]
    acc = jnp.zeros(out.shape, F32)
    for k in range(4):
        rows = pl.multiple_of(pos[4 + k] * 1024, 1024)
        acc = acc + nn(feats[:, pl.ds(rows, 1024)], refs[k][...])
    out[...] = acc


def partial_kernel(own, other, keep, recv, extra, out):
    h = own.shape[0]
    r = nn(own[...], keep[...]) + nn(other[...], recv[...])
    r = r.astype(BF)
    for i in range(2):
        out[i, :h, :] = r[:, i * 128:(i + 1) * 128]
        if out.shape[1] > h:
            out[i, h:, :] = extra[...]


def push_down(own, other, keep, recv, extra, with_extra):
    rows = own.shape[0] + (16 if with_extra else 0)
    whole = lambda s: pl.BlockSpec(s, lambda i: (0, 0))
    return pl.pallas_call(
        partial_kernel,
        grid=(8,),
        out_shape=jax.ShapeDtypeStruct((16, rows, 128), BF),
        in_specs=[
            whole(own.shape),
            whole(other.shape),
            pl.BlockSpec((keep.shape[0], 256), lambda i: (0, i)),
            pl.BlockSpec((recv.shape[0], 256), lambda i: (0, i)),
            whole(extra.shape),
        ],
        out_specs=pl.BlockSpec((2, rows, 128), lambda i: (i, 0, 0)),
        compiler_params=PARAMS,
        name="push_down",
    )(own, other, keep, recv, extra)


def back_kernel(pos, p0, p1, p2, p3, recv, full, send):
    x, z = pos[0], pos[1]
    for i, p in enumerate((p0, p1, p2, p3)):
        for j in range(4):
            col = (lax.rem(x + j, 4) * 4 + lax.rem(z + i, 4)) * 128
            full[:, pl.ds(pl.multiple_of(col, 128), 128)] = p[j]
    send[...] = nt(full[...], recv[...]).astype(BF)


def pull_back(weighted, pos, keep, recv):
    pieces = ring_direct(jnp.stack(ring_direct(weighted, "x")), "z")
    rows, hid = weighted.shape[0], recv.shape[0]
    full, send = pl.pallas_call(
        back_kernel,
        out_shape=(jax.ShapeDtypeStruct((rows, 2048), BF), jax.ShapeDtypeStruct((rows, hid), BF)),
        in_specs=[SM] + [VM] * 5,
        out_specs=(VM, VM),
        compiler_params=PARAMS,
        name="back_other",
    )(pos, *pieces, recv)
    got = shift(send, "yl", 1)
    return nt(full, keep) + got.astype(F32)


def round_bf(v):
    return lax.reduce_precision(v, 8, 7)


def sum_all(values):
    block = jnp.concatenate([jnp.broadcast_to(v, (1, 128)) for v in values] + [jnp.zeros((8 - len(values), 128), F32)])
    block = jnp.broadcast_to(block[None], (128, 8, 128))
    got = lax.all_to_all(block, NAMES, 0, 0, tiled=True)
    total = jnp.sum(got, axis=0)
    return [total[i, 0] for i in range(len(values))]


def shards(tokens, gate_weight, up_weight, down_weight, curvature, start):
    yh, c, x, z, yl = [lax.axis_index(n).astype(jnp.int32) for n in NAMES]
    dp = yh * 2 + c
    order = [dp, yh * 2 + 1 - c, (1 - yh) * 2 + c, (1 - yh) * 2 + 1 - c]
    pos = jnp.stack([x, z, yl, dp] + order)
    total_tokens = tokens.shape[0] * 4

    def over_dp(v):
        far = shift(v, "yh", 1)
        return [v, shift(v, "c", 1), far, shift(far, "c", 1)]

    other = shift(tokens, "yl", 1)
    pair = jnp.where(
        yl == 0, jnp.concatenate([tokens, other], axis=1), jnp.concatenate([other, tokens], axis=1)
    )
    start_b = over_dp(start.astype(BF))
    keep, send = pl.pallas_call(
        split_kernel,
        out_shape=(jax.ShapeDtypeStruct((512, 2048), BF),) * 2,
        in_specs=[SM, VM],
        out_specs=(VM, VM),
        compiler_params=PARAMS,
        name="split_down",
    )(pos, down_weight)
    recv = shift(send, "yl", 1)
    feats = gather_tokens(pair, pos)

    gate = nn(feats, gate_weight)
    up = nn(feats, up_weight)
    sigma = jax.nn.sigmoid(gate)
    slope = sigma * (1.0 + gate * (1.0 - sigma)) * up
    tan_start = pl.pallas_call(
        tangent_kernel,
        out_shape=jax.ShapeDtypeStruct((512, 512), F32),
        in_specs=[SM] + [VM] * 5,
        out_specs=VM,
        compiler_params=PARAMS,
        name="tangent",
    )(pos, feats, *start_b)
    start_squares = jnp.sum(start * start)

    def spread(tangent, extra, with_extra):
        pushed = (slope * tangent).astype(BF)
        parts = push_down(pushed, shift(pushed, "yl", 1), keep, recv, extra, with_extra)
        got = lax.all_to_all(parts, ("x", "z"), 0, 0, tiled=True)
        return jnp.sum(got.astype(F32), axis=0)

    moved_one = spread(tan_start, jnp.zeros((16, 128), BF), False)
    weighted = (curvature * moved_one / total_tokens).astype(BF)
    delta = (pull_back(weighted, pos, keep, recv) * slope).astype(BF)
    deltas_one = over_dp(delta)

    feats_all = over_dp(feats)
    tan_image = 0.0
    for f, d in zip(feats_all, deltas_one):
        gram = nt(feats, f)
        high = round_bf(gram)
        low = round_bf(gram - high)
        tan_image = tan_image + nn(high.astype(BF), d) + nn(low.astype(BF), d)
    rows_all = [lax.dynamic_slice_in_dim(f, dp * 1024, 1024, axis=1) for f in feats_all]

    def image_of(deltas):
        out = tn(rows_all[0], deltas[0])
        for r, d in zip(rows_all[1:], deltas[1:]):
            out = out + tn(r, d)
        return out

    sums = [start_squares, jnp.sum(tan_start * delta.astype(F32)), jnp.sum(tan_image * delta.astype(F32))]
    sums = jnp.stack([jnp.broadcast_to(v * SCALE_INV, (128,)) for v in sums] + [jnp.zeros((128,), F32)] * 5)
    for axis in ("c", "yh", "yl"):
        sums = sums + shift(sums, axis, 1)
    digits = []
    rest = sums[:4]
    for _ in range(3):
        digit = round_bf(rest)
        digits.append(digit)
        rest = rest - digit
    extra = jnp.concatenate(digits + [jnp.zeros((4, 128), F32)]).astype(BF)

    moved = spread(tan_image, extra, True)
    moved_two = moved[:512]
    tail = moved[512:, 0]
    ss, sw, ww = [tail[i] + tail[4 + i] + tail[8 + i] for i in range(3)]
    norm_sq = ss + EPS
    inv_norm = lax.rsqrt(norm_sq)
    alpha_one = sw / norm_sq
    one_one = ss / norm_sq
    resid_sq = jnp.maximum(ww / norm_sq - alpha_one * alpha_one * (2.0 - one_one), 0.0)
    beta_one = jnp.sqrt(resid_sq + EPS)
    scale_two = inv_norm / beta_one

    weighted = (curvature * ((moved_two - alpha_one * moved_one) * scale_two) / total_tokens).astype(BF)
    delta = (pull_back(weighted, pos, keep, recv) * slope).astype(BF)
    deltas_two = over_dp(delta)
    image_one = image_of(deltas_one)
    image_two = image_of(deltas_two)
    delta_f = delta.astype(F32)
    tan_two = (tan_image - alpha_one * tan_start) * scale_two
    alpha_two, cross, image_sq = [
        v * SCALE_INV
        for v in sum_all(
            [jnp.sum(tan_two * delta_f), jnp.sum(tan_start * delta_f) * inv_norm, jnp.sum(image_two * image_two)]
        )
    ]
    two_two = resid_sq / (resid_sq + EPS)
    one_two = alpha_one * (1.0 - one_one) / beta_one
    resid_two_sq = (
        image_sq
        - alpha_two * alpha_two * (2.0 - two_two)
        - cross * cross * (2.0 - one_one)
        + 2.0 * alpha_two * cross * one_two
    )
    beta_two = jnp.sqrt(jnp.maximum(resid_two_sq, 0.0) + EPS)
    first = start * inv_norm
    second = image_one * scale_two - (alpha_one / beta_one) * first
    next_vector = (image_two - alpha_two * second - cross * first) / beta_two
    coefficients = jnp.stack([alpha_one, beta_one, alpha_two, beta_two])
    return (coefficients, next_vector)


def solution(mesh):
    inner = Mesh(mesh.devices.reshape([n for _, n in AXES]), NAMES)
    dp, fsdp = ("yh", "c"), ("x", "z", "yl")
    in_specs = (P(dp, fsdp), P(None, fsdp), P(None, fsdp), P(fsdp, None), P(dp, fsdp), P(dp, fsdp))
    out_specs = (P(), P(dp, fsdp))
    return jax.shard_map(shards, mesh=inner, in_specs=in_specs, out_specs=out_specs, check_vma=False)
```

```python
import jax
import jax.numpy as jnp
from jax import lax
from jax.experimental import pallas as pl
from jax.experimental.pallas import tpu as pltpu
from jax.sharding import Mesh
from jax.sharding import PartitionSpec as P

D = 4096
FF = 16384
EPS = 1e-06
TOKENS = 2048
SCALE_INV = 1.0 / (D * FF)
AXES = (("yh", 2), ("c", 2), ("x", 4), ("z", 4), ("yl", 2))
NAMES = tuple(name for name, _ in AXES)
SIZES = dict(AXES)
BF = jnp.bfloat16
F32 = jnp.float32
MIB = 1024 * 1024
VM = pl.BlockSpec(memory_space=pltpu.VMEM)
SM = pl.BlockSpec(memory_space=pltpu.SMEM)


def shift(value, axis, by):
    n = SIZES[axis]
    return lax.ppermute(value, axis, [((i + by) % n, i) for i in range(n)])


def ring_pair(jobs):
    up = [shift(v, a, 1) for v, a in jobs]
    down = [shift(v, a, -1) for v, a in jobs]
    out = []
    for (v, a), p, m in zip(jobs, up, down):
        h = v.shape[-2] // 2
        far = [shift(p[..., :h, :], a, 1), shift(m[..., h:, :], a, -1)]
        out.append([v, p, jnp.concatenate(far, axis=-2), m])
    return out


def ring_direct(v, a):
    return [v, shift(v, a, 1), shift(v, a, 2), shift(v, a, 3)]


def after(value, *others):
    return lax.optimization_barrier((value, *others))[0]


def call(kernel, name, out, *operands, mib=16):
    specs = [SM if v.dtype == jnp.int32 else VM for v in operands]
    shapes = [jax.ShapeDtypeStruct(s, t) for s, t in out]
    got = pl.pallas_call(
        kernel,
        out_shape=shapes,
        in_specs=specs,
        out_specs=[VM] * len(shapes),
        compiler_params=pltpu.CompilerParams(vmem_limit_bytes=mib * MIB),
        name=name,
    )(*operands)
    return got if len(got) > 1 else got[0]


def nt(a, b):
    return lax.dot_general(a, b, (((1,), (1,)), ((), ())), preferred_element_type=F32)


def nn(a, b):
    return jnp.dot(a, b, preferred_element_type=F32)


def place(pos, i, j, width):
    return pl.multiple_of((lax.rem(pos[0] + i, 4) * 4 + lax.rem(pos[1] + j, 4)) * width, width)


def total(v):
    return jnp.sum(v, axis=(0, 1), keepdims=True) * SCALE_INV


def row_of(values, rows, width):
    index = lax.broadcasted_iota(jnp.int32, (rows, width), 0)
    out = jnp.zeros((rows, width), F32)
    for i, v in enumerate(values):
        out = jnp.where(index == i, jnp.broadcast_to(v, (rows, width)), out)
    return out


def digits(values, width):
    rows = []
    for v in values:
        for _ in range(3):
            d = v.astype(BF).astype(F32)
            rows.append(d)
            v = v - d
    return row_of(rows, 16, width).astype(BF)


def undigit(rows):
    return [rows[3 * i:3 * i + 1] + rows[3 * i + 1:3 * i + 2] + rows[3 * i + 2:3 * i + 3] for i in range(3)]


def cast_kernel(start, out, squares):
    acc = jnp.zeros((8, 512), F32)
    for i in range(0, 1024, 8):
        v = start[i:i + 8, :]
        acc = acc + v * v
    out[...] = start[...].astype(BF)
    squares[...] = acc


def split_kernel(pos, down, keep, send):
    yl = pos[2]
    for b in range(16):
        keep[:, b * 128:(b + 1) * 128] = down[:, pl.ds(pl.multiple_of((2 * b + yl) * 128, 128), 128)]
        send[:, b * 128:(b + 1) * 128] = down[:, pl.ds(pl.multiple_of((2 * b + 1 - yl) * 128, 128), 128)]


def front_kernel(pos, *refs):
    a, b = refs[:4], refs[4:8]
    gate_w, up_w = refs[8:10]
    rows = refs[10:14]
    feats, slope, tangent, pushed = refs[14:]
    h = feats.shape[0] // 2
    for i in range(4):
        for j in range(4):
            feats[:h, pl.ds(place(pos, j, i, 256), 256)] = a[i][j]
            feats[h:, pl.ds(place(pos, i, j, 256), 256)] = b[i][j]
    gate = nn(feats[...], gate_w[...])
    sigma = 1.0 / (1.0 + jnp.exp(-gate))
    slope[...] = sigma * (1.0 + gate * (1.0 - sigma)) * nn(feats[...], up_w[...])
    acc = jnp.zeros(tangent.shape, F32)
    for k in range(4):
        cols = pl.multiple_of(pos[4 + k] * 1024, 1024)
        acc = acc + nn(feats[:, pl.ds(cols, 1024)], rows[k][...])
    tangent[...] = acc
    pushed[...] = (slope[...] * acc).astype(BF)


def push_kernel(own, other, keep, recv, out):
    for b in range(0, 16, 4):
        cols = slice(b * 128, (b + 4) * 128)
        r = (nn(own[:512], keep[:, cols]) + nn(other[:512], recv[:, cols])).astype(BF)
        for i in range(4):
            out[b + i, :512, :] = r[:, i * 128:(i + 1) * 128]
    if out.shape[1] > 512:
        sums = undigit(own[512:].astype(F32) + other[512:].astype(F32))
        extra = digits(sums, 512)[:, :128]
        for b in range(16):
            out[b, 512:, :] = extra


def weigh_first_kernel(got, curvature, moved, weighted):
    acc = got[0].astype(F32)
    for i in range(1, 16):
        acc = acc + got[i].astype(F32)
    moved[...] = acc
    weighted[...] = (curvature[...] * acc / TOKENS).astype(BF)


def weigh_second_kernel(got, curvature, moved, weighted, scalars):
    acc = got[0, :512, :].astype(F32)
    tail = got[0, 512:, :].astype(F32)
    for i in range(1, 16):
        acc = acc + got[i, :512, :].astype(F32)
        tail = tail + got[i, 512:, :].astype(F32)
    ss, sw, dd = undigit(tail)
    alpha = sw / (ss + EPS)
    scale = lax.rsqrt(dd + 1e-30) * (1.0 / 1024.0)
    weighted[...] = (curvature[...] * ((acc - alpha * moved[...]) * scale) / TOKENS).astype(BF)
    scalars[...] = row_of([ss, sw, scale], 8, 128)


def back_kernel(pos, p0, p1, p2, p3, recv, full, send):
    for i, p in enumerate((p0, p1, p2, p3)):
        for j in range(4):
            full[:, pl.ds(place(pos, j, i, 128), 128)] = p[j]
    send[...] = nt(full[...], recv[...]).astype(BF)


def own_back_kernel(full, keep, out):
    out[...] = nt(full[...], keep[...])


def delta_first_kernel(own, got, slope, tangent, squares, out):
    delta = ((own[...] + got[...].astype(F32)) * slope[...]).astype(BF)
    out[:512, :] = delta
    delta = delta.astype(F32)
    sums = [total(squares[...]), total(tangent[...] * delta), total(delta * (delta * 1.0))]
    out[512:, :] = digits([jnp.broadcast_to(v, (1, 512)) for v in sums], 512)


def delta_second_kernel(own, got, slope, tan_start, tan_image, delta_one, out, sums):
    delta = ((own[...] + got[...].astype(F32)) * slope[...]).astype(BF)
    out[...] = delta
    delta = delta.astype(F32)
    ww = total(tan_image[...] * delta_one[:512].astype(F32))
    sums[...] = row_of([ww, total(tan_start[...] * delta), total(tan_image[...] * delta)], 8, 128)


def gram_kernel(feats, others, out):
    out[...] = nt(feats[...], others[...])


def gram_split_kernel(pos, near, p0, p1, p2, p3, high, low):
    def put(cols, v):
        top = v.astype(BF)
        high[:, cols] = top
        low[:, cols] = (v - top.astype(F32)).astype(BF)

    put(slice(0, 1024), near[...])
    for i, p in enumerate((p0, p1, p2, p3)):
        q = lax.rem(pos[0] + i, 4) * 128
        put(pl.ds(pl.multiple_of(1024 + q, 128), 128), p[:, :128])
        put(pl.ds(pl.multiple_of(1536 + q, 128), 128), p[:, 128:])


def near_tangent_kernel(high, low, d0, d1, out):
    acc = nn(high[:, :512], d0[:512]) + nn(low[:, :512], d0[:512])
    out[...] = acc + nn(high[:, 512:1024], d1[:512]) + nn(low[:, 512:1024], d1[:512])


def far_tangent_kernel(near, high, low, d0, d1, d2, d3, slope, tangent, pushed):
    acc = near[...] + nn(high[:, 1024:1536], d2[:512]) + nn(low[:, 1024:1536], d2[:512])
    acc = acc + nn(high[:, 1536:], d3[:512]) + nn(low[:, 1536:], d3[:512])
    tangent[...] = acc
    pushed[:512, :] = (slope[...] * acc).astype(BF)
    rows = d0[512:].astype(F32) + d1[512:].astype(F32) + d2[512:].astype(F32) + d3[512:].astype(F32)
    pushed[512:, :] = digits(undigit(rows), 512)


def near_image_kernel(r0, r1, d0, d1, out):
    out[...] = nn(r0[...], d0[:512]) + nn(r1[...], d1[:512])


def far_image_kernel(near, r2, r3, d2, d3, out):
    out[...] = near[...] + nn(r2[...], d2[:512]) + nn(r3[...], d3[:512])


def last_image_kernel(near, r2, r3, d2, d3, sums, out, block):
    acc = near[...] + nn(r2[...], d2[...]) + nn(r3[...], d3[...])
    out[...] = acc
    index = lax.broadcasted_iota(jnp.int32, (8, 128), 0)
    block[...] = jnp.where(index == 3, jnp.broadcast_to(total(acc * acc), (8, 128)), sums[...])


def final_kernel(got, scalars, start, image_one, image_two, out, coefficients):
    acc = got[0]
    for i in range(1, 128):
        acc = acc + got[i]
    ss, sw, scale = scalars[0:1], scalars[1:2], scalars[2:3]
    ww, uz, wz, zz = acc[0:1], acc[1:2], acc[2:3], acc[3:4]
    norm_sq = ss + EPS
    norm = jnp.sqrt(norm_sq)
    alpha_one = sw / norm_sq
    one_one = ss / norm_sq
    resid_sq = jnp.maximum(ww / norm_sq - alpha_one * alpha_one * (2.0 - one_one), 0.0)
    beta_one = jnp.sqrt(resid_sq + EPS)
    second = 1.0 / (norm * beta_one)
    image = second / scale
    alpha_two = image * second * (wz - alpha_one * uz)
    cross = image * uz / norm
    two_two = resid_sq / (resid_sq + EPS)
    one_two = alpha_one * (1.0 - one_one) / beta_one
    last_sq = (
        image * image * zz
        - alpha_two * alpha_two * (2.0 - two_two)
        - cross * cross * (2.0 - one_one)
        + 2.0 * alpha_two * cross * one_two
    )
    beta_two = jnp.sqrt(jnp.maximum(last_sq, 0.0) + EPS)
    index = lax.broadcasted_iota(jnp.int32, (1, 128), 1)
    row = jnp.zeros((1, 128), F32)
    for i, v in enumerate((alpha_one, beta_one, alpha_two, beta_two)):
        row = jnp.where(index == i, v, row)
    coefficients[...] = row
    f_two = image / beta_two
    f_one = -alpha_two * second / beta_two
    f_start = (alpha_two * alpha_one / beta_one - cross) / (norm * beta_two)
    for k in range(4):
        cols = slice(k * 128, (k + 1) * 128)
        out[:, cols] = f_two * image_two[:, cols] + f_one * image_one[:, cols] + f_start * start[:, cols]


def pull_back(weighted, pos, keep, recv):
    pieces = ring_direct(jnp.stack(ring_direct(weighted, "x")), "z")
    full, send = call(back_kernel, "back_other", [((512, 2048), BF), ((512, 512), BF)], pos, *pieces, recv)
    got = shift(send, "yl", 1)
    own = call(own_back_kernel, "back_own", [((512, 512), F32)], full, keep)
    return own, got, full


def over_dp(v):
    far = shift(v, "yh", 1)
    return [v, shift(v, "c", 1), far, shift(far, "c", 1)]


def shards(tokens, gate_weight, up_weight, down_weight, curvature, start):
    yh, c, x, z, yl = [lax.axis_index(n).astype(jnp.int32) for n in NAMES]
    dp = yh * 2 + c
    pos = jnp.stack([x, z, yl, dp, dp, yh * 2 + 1 - c, (1 - yh) * 2 + c, (1 - yh) * 2 + 1 - c])

    other = shift(tokens, "yl", 1)
    start_b, squares = call(cast_kernel, "cast_start", [((1024, 512), BF), ((8, 512), F32)], start)
    pair = jnp.where(
        yl == 0, jnp.concatenate([tokens, other], axis=1), jnp.concatenate([other, tokens], axis=1)
    )
    keep, send = call(split_kernel, "split_down", [((512, 2048), BF)] * 2, pos, down_weight)
    a, b = ring_pair([(pair[:256], "x"), (pair[256:], "z")])
    starts = over_dp(start_b)
    recv = shift(after(send, starts[2]), "yl", 1)
    a, b = ring_pair([(jnp.stack(a), "z"), (jnp.stack(b), "x")])
    feats, slope, tan_start, pushed = call(
        front_kernel,
        "front",
        [((512, D), BF), ((512, 512), F32), ((512, 512), F32), ((512, 512), BF)],
        pos, *a, *b, gate_weight, up_weight, *starts,
        mib=32,
    )

    other = shift(pushed, "yl", 1)
    feats_c = shift(feats, "c", 1)
    near_gram = call(
        gram_kernel, "near_gram", [((512, 1024), F32)], after(feats, pushed), jnp.concatenate([feats, feats_c])
    )
    other, near_gram = lax.optimization_barrier((other, near_gram))
    parts = call(push_kernel, "push", [((16, 512, 128), BF)], pushed, other, keep, recv)
    quarter = lax.dynamic_slice_in_dim(feats, x * 128, 128, axis=0)
    quarter = shift(after(quarter, other), "yh", 1)
    quarter_c = shift(quarter, "c", 1)
    got = lax.all_to_all(parts, ("x", "z"), 0, 0, tiled=True)
    moved, weighted = call(weigh_first_kernel, "weigh", [((512, 128), F32), ((512, 128), BF)], got, curvature)
    own, got, full = pull_back(weighted, pos, keep, recv)
    far_gram = call(
        gram_kernel, "far_gram", [((512, 256), F32)], after(feats, own), jnp.concatenate([quarter, quarter_c])
    )
    delta = call(
        delta_first_kernel, "delta", [((528, 512), BF)], own, got, slope, tan_start, squares
    )
    deltas = over_dp(delta)
    high, low = call(
        gram_split_kernel, "gram_split", [((512, 2048), BF)] * 2, pos, near_gram, *ring_direct(far_gram, "x")
    )
    near = call(near_tangent_kernel, "near_tangent", [((512, 512), F32)], high, low, *deltas[:2])
    tan_image, pushed = call(
        far_tangent_kernel,
        "far_tangent",
        [((512, 512), F32), ((528, 512), BF)],
        near, high, low, *deltas, slope,
    )

    other = shift(pushed, "yl", 1)
    parts = call(push_kernel, "push", [((16, 528, 128), BF)], pushed, other, keep, recv)
    theirs = lax.dynamic_slice_in_dim(feats, (1 - yh) * 2048, 2048, axis=1)
    far_rows = shift(after(theirs, other), "yh", 1)
    got = lax.all_to_all(parts, ("x", "z"), 0, 0, tiled=True)
    weighted, scalars = call(
        weigh_second_kernel, "weigh", [((512, 128), BF), ((8, 128), F32)], got, curvature, moved
    )
    own, got, full = pull_back(weighted, pos, keep, recv)
    mine = lambda v, at: lax.dynamic_slice_in_dim(v, at * 1024, 1024, axis=1)
    rows = [mine(feats, dp), mine(feats_c, dp), mine(far_rows, c), shift(mine(far_rows, 1 - c), "c", 1)]
    rows = [after(r, own).T for r in rows]
    first_deltas = deltas
    near = call(near_image_kernel, "near_image", [((1024, 512), F32)], *rows[:2], *first_deltas[:2])
    image_one = call(far_image_kernel, "far_image", [((1024, 512), F32)], near, *rows[2:], *first_deltas[2:])
    delta, sums = call(
        delta_second_kernel,
        "delta",
        [((512, 512), BF), ((8, 128), F32)],
        own, got, slope, tan_start, tan_image, delta,
    )
    deltas = over_dp(delta)
    near = call(near_image_kernel, "near_image", [((1024, 512), F32)], *rows[:2], *deltas[:2])
    image_two, block = call(
        last_image_kernel, "last_image", [((1024, 512), F32), ((8, 128), F32)], near, *rows[2:], *deltas[2:], sums
    )
    got = lax.all_to_all(jnp.broadcast_to(block[None], (128, 8, 128)), NAMES, 0, 0, tiled=True)
    whole = lambda *s: pl.BlockSpec(s, lambda i: (0,) * len(s))
    band = pl.BlockSpec((256, 512), lambda i: (i, 0))
    next_vector, coefficients = pl.pallas_call(
        final_kernel,
        grid=(4,),
        out_shape=[jax.ShapeDtypeStruct((1024, 512), F32), jax.ShapeDtypeStruct((1, 128), F32)],
        in_specs=[whole(128, 8, 128), whole(8, 128), band, band, band],
        out_specs=[band, whole(1, 128)],
        compiler_params=pltpu.CompilerParams(vmem_limit_bytes=16 * MIB),
        name="final",
    )(got, scalars, start, image_one, image_two)
    return (coefficients[0, :4], next_vector)


def solution(mesh):
    inner = Mesh(mesh.devices.reshape([n for _, n in AXES]), NAMES)
    dp, fsdp = ("yh", "c"), ("x", "z", "yl")
    in_specs = (P(dp, fsdp), P(None, fsdp), P(None, fsdp), P(fsdp, None), P(dp, fsdp), P(dp, fsdp))
    out_specs = (P(), P(dp, fsdp))
    return jax.shard_map(shards, mesh=inner, in_specs=in_specs, out_specs=out_specs, check_vma=False)
```

```python
import jax
import jax.numpy as jnp
from jax import lax
from jax.experimental import pallas as pl
from jax.experimental.pallas import tpu as pltpu
from jax.sharding import Mesh
from jax.sharding import PartitionSpec as P

D = 4096
FF = 16384
EPS = 1e-06
TOKENS = 2048
SCALE_INV = 1.0 / (D * FF)
AXES = (("yh", 2), ("c", 2), ("x", 4), ("z", 4), ("yl", 2))
NAMES = tuple(name for name, _ in AXES)
SIZES = dict(AXES)
BF = jnp.bfloat16
F32 = jnp.float32
MIB = 1024 * 1024
VM = pl.BlockSpec(memory_space=pltpu.VMEM)
SM = pl.BlockSpec(memory_space=pltpu.SMEM)


def shift(value, axis, by):
    n = SIZES[axis]
    return lax.ppermute(value, axis, [((i + by) % n, i) for i in range(n)])


def line(v, a):
    return [v, shift(v, a, 1), shift(v, a, 2), shift(v, a, 3)]


def after(value, *others):
    return lax.optimization_barrier((value, *others))[0]


def call(kernel, name, out, *operands, mib=16):
    specs = [SM if v.dtype == jnp.int32 else VM for v in operands]
    shapes = [jax.ShapeDtypeStruct(s, t) for s, t in out]
    got = pl.pallas_call(
        kernel,
        out_shape=shapes,
        in_specs=specs,
        out_specs=[VM] * len(shapes),
        compiler_params=pltpu.CompilerParams(vmem_limit_bytes=mib * MIB),
        name=name,
    )(*operands)
    return got if len(got) > 1 else got[0]


def gather(v):
    here, far = lax.optimization_barrier((line(v, "x"), shift(v, "z", 2)))
    here = jnp.stack(here)
    return [here, shift(here, "z", 1), *line(far, "x"), shift(here, "z", 3)]


def blocks(pos, refs, width):
    here, nxt, f0, f1, f2, f3, prev = refs
    for i, f in enumerate((f0, f1, f2, f3)):
        yield place(pos, i, 0, width), here[i]
        yield place(pos, i, 1, width), nxt[i]
        yield place(pos, i, 2, width), f[...]
        yield place(pos, i, 3, width), prev[i]


def nt(a, b):
    return lax.dot_general(a, b, (((1,), (1,)), ((), ())), preferred_element_type=F32)


def nn(a, b):
    return jnp.dot(a, b, preferred_element_type=F32)


def place(pos, i, j, width):
    return pl.multiple_of((lax.rem(pos[0] + i, 4) * 4 + lax.rem(pos[1] + j, 4)) * width, width)


def total(v):
    return jnp.sum(v, axis=(0, 1), keepdims=True) * SCALE_INV


def row_of(values, rows, width):
    index = lax.broadcasted_iota(jnp.int32, (rows, width), 0)
    out = jnp.zeros((rows, width), F32)
    for i, v in enumerate(values):
        out = jnp.where(index == i, jnp.broadcast_to(v, (rows, width)), out)
    return out


def digits(values, width):
    rows = []
    for v in values:
        for _ in range(3):
            d = v.astype(BF).astype(F32)
            rows.append(d)
            v = v - d
    return row_of(rows, 16, width).astype(BF)


def undigit(rows):
    return [rows[3 * i:3 * i + 1] + rows[3 * i + 1:3 * i + 2] + rows[3 * i + 2:3 * i + 3] for i in range(3)]


def cast_kernel(start, out, squares):
    acc = jnp.zeros((8, 512), F32)
    for i in range(0, 1024, 8):
        v = start[i:i + 8, :]
        acc = acc + v * v
    out[...] = start[...].astype(BF)
    squares[...] = acc


def split_kernel(pos, down, keep, send):
    yl = pos[2]
    for b in range(16):
        keep[:, b * 128:(b + 1) * 128] = down[:, pl.ds(pl.multiple_of((2 * b + yl) * 128, 128), 128)]
        send[:, b * 128:(b + 1) * 128] = down[:, pl.ds(pl.multiple_of((2 * b + 1 - yl) * 128, 128), 128)]


def front_kernel(pos, *refs):
    gate_w, up_w = refs[7:9]
    rows = refs[9:13]
    feats, slope, tangent, pushed = refs[13:]
    for col, block in blocks(pos, refs[:7], 256):
        feats[:, pl.ds(col, 256)] = block
    gate = nn(feats[...], gate_w[...])
    sigma = 1.0 / (1.0 + jnp.exp(-gate))
    slope[...] = sigma * (1.0 + gate * (1.0 - sigma)) * nn(feats[...], up_w[...])
    acc = jnp.zeros(tangent.shape, F32)
    for k in range(4):
        cols = pl.multiple_of(pos[4 + k] * 1024, 1024)
        acc = acc + nn(feats[:, pl.ds(cols, 1024)], rows[k][...])
    tangent[...] = acc
    pushed[...] = (slope[...] * acc).astype(BF)


def push_kernel(own, other, keep, recv, out):
    for b in range(0, 16, 4):
        cols = slice(b * 128, (b + 4) * 128)
        r = (nn(own[:512], keep[:, cols]) + nn(other[:512], recv[:, cols])).astype(BF)
        for i in range(4):
            out[b + i, :512, :] = r[:, i * 128:(i + 1) * 128]
    if out.shape[1] > 512:
        sums = undigit(own[512:].astype(F32) + other[512:].astype(F32))
        extra = digits(sums, 512)[:, :128]
        for b in range(16):
            out[b, 512:, :] = extra


def weigh_first_kernel(got, curvature, moved, weighted):
    acc = got[0].astype(F32)
    for i in range(1, 16):
        acc = acc + got[i].astype(F32)
    moved[...] = acc
    weighted[...] = (curvature[...] * acc / TOKENS).astype(BF)


def weigh_second_kernel(got, curvature, moved, weighted, scalars):
    acc = got[0, :512, :].astype(F32)
    tail = got[0, 512:, :].astype(F32)
    for i in range(1, 16):
        acc = acc + got[i, :512, :].astype(F32)
        tail = tail + got[i, 512:, :].astype(F32)
    ss, sw, dd = undigit(tail)
    alpha = sw / (ss + EPS)
    scale = lax.rsqrt(dd + 1e-30) * (1.0 / 1024.0)
    weighted[...] = (curvature[...] * ((acc - alpha * moved[...]) * scale) / TOKENS).astype(BF)
    scalars[...] = row_of([ss, sw, scale], 8, 128)


def back_kernel(pos, *refs):
    recv, full, send = refs[7:]
    for col, block in blocks(pos, refs[:7], 128):
        full[:, pl.ds(col, 128)] = block
    send[...] = nt(full[...], recv[...]).astype(BF)


def own_back_kernel(full, keep, out):
    out[...] = nt(full[...], keep[...])


def delta_first_kernel(own, got, slope, tangent, squares, out):
    delta = ((own[...] + got[...].astype(F32)) * slope[...]).astype(BF)
    out[:512, :] = delta
    delta = delta.astype(F32)
    sums = [total(squares[...]), total(tangent[...] * delta), total(delta * (delta * 1.0))]
    out[512:, :] = digits([jnp.broadcast_to(v, (1, 512)) for v in sums], 512)


def delta_second_kernel(own, got, slope, tan_start, tan_image, delta_one, out, sums):
    delta = ((own[...] + got[...].astype(F32)) * slope[...]).astype(BF)
    out[...] = delta
    delta = delta.astype(F32)
    ww = total(tan_image[...] * delta_one[:512].astype(F32))
    sums[...] = row_of([ww, total(tan_start[...] * delta), total(tan_image[...] * delta)], 8, 128)


def gram_kernel(feats, one, two, out):
    n = one.shape[0]
    out[:, :n] = nt(feats[...], one[...])
    out[:, n:] = nt(feats[...], two[...])


def rows_kernel(pos, feats, out):
    out[...] = feats[:, pl.ds(pl.multiple_of(pos[3] * 1024, 1024), 1024)].T


def far_rows_kernel(pos, feats, out, other):
    c = pos[8]
    out[...] = feats[:, pl.ds(pl.multiple_of(c * 1024, 1024), 1024)].T
    other[...] = feats[:, pl.ds(pl.multiple_of((1 - c) * 1024, 1024), 1024)].T


def gram_split_kernel(pos, near, p0, p1, p2, p3, high, low):
    def put(cols, v):
        top = v.astype(BF)
        high[:, cols] = top
        low[:, cols] = (v - top.astype(F32)).astype(BF)

    put(slice(0, 1024), near[...])
    for i, p in enumerate((p0, p1, p2, p3)):
        q = lax.rem(pos[0] + i, 4) * 128
        put(pl.ds(pl.multiple_of(1024 + q, 128), 128), p[:, :128])
        put(pl.ds(pl.multiple_of(1536 + q, 128), 128), p[:, 128:])


def near_tangent_kernel(high, low, d0, d1, out):
    acc = nn(high[:, :512], d0[:512]) + nn(low[:, :512], d0[:512])
    out[...] = acc + nn(high[:, 512:1024], d1[:512]) + nn(low[:, 512:1024], d1[:512])


def far_tangent_kernel(near, high, low, d0, d1, d2, d3, slope, tangent, pushed):
    acc = near[...] + nn(high[:, 1024:1536], d2[:512]) + nn(low[:, 1024:1536], d2[:512])
    acc = acc + nn(high[:, 1536:], d3[:512]) + nn(low[:, 1536:], d3[:512])
    tangent[...] = acc
    pushed[:512, :] = (slope[...] * acc).astype(BF)
    rows = d0[512:].astype(F32) + d1[512:].astype(F32) + d2[512:].astype(F32) + d3[512:].astype(F32)
    pushed[512:, :] = digits(undigit(rows), 512)


def near_image_kernel(r0, r1, d0, d1, out):
    out[...] = nn(r0[...], d0[:512]) + nn(r1[...], d1[:512])


def far_image_kernel(near, r2, r3, d2, d3, out):
    out[...] = near[...] + nn(r2[...], d2[:512]) + nn(r3[...], d3[:512])


def last_image_kernel(near, r2, r3, d2, d3, sums, out, block):
    acc = near[...] + nn(r2[...], d2[...]) + nn(r3[...], d3[...])
    out[...] = acc
    index = lax.broadcasted_iota(jnp.int32, (8, 128), 0)
    block[...] = jnp.where(index == 3, jnp.broadcast_to(total(acc * acc), (8, 128)), sums[...])


def final_kernel(got, scalars, start, image_one, image_two, out, coefficients):
    acc = got[0]
    for i in range(1, 128):
        acc = acc + got[i]
    ss, sw, scale = scalars[0:1], scalars[1:2], scalars[2:3]
    ww, uz, wz, zz = acc[0:1], acc[1:2], acc[2:3], acc[3:4]
    norm_sq = ss + EPS
    norm = jnp.sqrt(norm_sq)
    alpha_one = sw / norm_sq
    one_one = ss / norm_sq
    resid_sq = jnp.maximum(ww / norm_sq - alpha_one * alpha_one * (2.0 - one_one), 0.0)
    beta_one = jnp.sqrt(resid_sq + EPS)
    second = 1.0 / (norm * beta_one)
    image = second / scale
    alpha_two = image * second * (wz - alpha_one * uz)
    cross = image * uz / norm
    two_two = resid_sq / (resid_sq + EPS)
    one_two = alpha_one * (1.0 - one_one) / beta_one
    last_sq = (
        image * image * zz
        - alpha_two * alpha_two * (2.0 - two_two)
        - cross * cross * (2.0 - one_one)
        + 2.0 * alpha_two * cross * one_two
    )
    beta_two = jnp.sqrt(jnp.maximum(last_sq, 0.0) + EPS)
    index = lax.broadcasted_iota(jnp.int32, (1, 128), 1)
    row = jnp.zeros((1, 128), F32)
    for i, v in enumerate((alpha_one, beta_one, alpha_two, beta_two)):
        row = jnp.where(index == i, v, row)
    coefficients[...] = row
    f_two = image / beta_two
    f_one = -alpha_two * second / beta_two
    f_start = (alpha_two * alpha_one / beta_one - cross) / (norm * beta_two)
    for k in range(4):
        cols = slice(k * 128, (k + 1) * 128)
        out[:, cols] = f_two * image_two[:, cols] + f_one * image_one[:, cols] + f_start * start[:, cols]


def over_dp(v):
    far = shift(v, "yh", 1)
    return [v, shift(v, "c", 1), far, shift(far, "c", 1)]


def shards(tokens, gate_weight, up_weight, down_weight, curvature, start):
    yh, c, x, z, yl = [lax.axis_index(n).astype(jnp.int32) for n in NAMES]
    dp = yh * 2 + c
    pos = jnp.stack([x, z, yl, dp, dp, yh * 2 + 1 - c, (1 - yh) * 2 + c, (1 - yh) * 2 + 1 - c, c])

    other = shift(tokens, "yl", 1)
    start_b, squares = call(cast_kernel, "cast_start", [((1024, 512), BF), ((8, 512), F32)], start)
    keep, send = call(
        split_kernel, "split_down", [((512, 2048), BF)] * 2, pos, after(down_weight, squares)
    )
    pair = jnp.where(
        yl == 0, jnp.concatenate([tokens, other], axis=1), jnp.concatenate([other, tokens], axis=1)
    )
    start_b, send = lax.optimization_barrier((start_b, send))
    starts = over_dp(start_b)
    recv = shift(send, "yl", 1)
    feats, slope, tan_start, pushed = call(
        front_kernel,
        "front",
        [((512, D), BF), ((512, 512), F32), ((512, 512), F32), ((512, 512), BF)],
        pos, *gather(pair), gate_weight, up_weight, *starts,
        mib=32,
    )

    other = shift(pushed, "yl", 1)
    feats_c = shift(feats, "c", 1)
    near_gram = call(gram_kernel, "near_gram", [((512, 1024), F32)], feats, feats, feats_c)
    other, near_gram = lax.optimization_barrier((other, near_gram))
    parts = call(push_kernel, "push", [((16, 512, 128), BF)], pushed, other, keep, recv)
    quarter = lax.dynamic_slice_in_dim(feats, x * 128, 128, axis=0)
    quarter = shift(after(quarter, parts), "yh", 1)
    quarter_c = shift(quarter, "c", 1)
    got = lax.all_to_all(parts, ("x", "z"), 0, 0, tiled=True)
    rows = [call(rows_kernel, "rows", [((1024, 512), BF)], pos, after(f, parts)) for f in (feats, feats_c)]
    got, rows = lax.optimization_barrier((got, rows))
    moved, weighted = call(weigh_first_kernel, "weigh", [((512, 128), F32), ((512, 128), BF)], got, curvature)
    pieces = gather(weighted)
    far_gram = call(gram_kernel, "far_gram", [((512, 256), F32)], after(feats, pieces[0]), quarter, quarter_c)
    recv_one, far_gram = lax.optimization_barrier((recv, far_gram))
    full, send = call(back_kernel, "back_other", [((512, 2048), BF), ((512, 512), BF)], pos, *pieces, recv_one)
    got = shift(send, "yl", 1)
    own = call(own_back_kernel, "back_own", [((512, 512), F32)], full, keep)
    far_grams = line(after(far_gram, send), "x")
    delta = call(delta_first_kernel, "delta", [((528, 512), BF)], own, got, slope, tan_start, squares)
    deltas = over_dp(delta)
    high, low = call(gram_split_kernel, "gram_split", [((512, 2048), BF)] * 2, pos, near_gram, *far_grams)
    near = call(near_tangent_kernel, "near_tangent", [((512, 512), F32)], high, low, *deltas[:2])
    tan_image, pushed = call(
        far_tangent_kernel,
        "far_tangent",
        [((512, 512), F32), ((528, 512), BF)],
        near, high, low, *deltas, slope,
    )

    other = shift(pushed, "yl", 1)
    parts = call(push_kernel, "push", [((16, 528, 128), BF)], pushed, other, keep, recv)
    theirs = lax.dynamic_slice_in_dim(feats, (1 - yh) * 2048, 2048, axis=1)
    far_rows = shift(after(theirs, parts), "yh", 1)
    got = lax.all_to_all(parts, ("x", "z"), 0, 0, tiled=True)
    first_deltas = deltas
    near_one = call(
        near_image_kernel, "near_image", [((1024, 512), F32)], *rows, after(first_deltas[0], parts), first_deltas[1]
    )
    got, near_one = lax.optimization_barrier((got, near_one))
    weighted, scalars = call(
        weigh_second_kernel, "weigh", [((512, 128), BF), ((8, 128), F32)], got, curvature, moved
    )
    full, send = call(
        back_kernel, "back_other", [((512, 2048), BF), ((512, 512), BF)], pos, *gather(weighted), recv
    )
    got = shift(send, "yl", 1)
    own = call(own_back_kernel, "back_own", [((512, 512), F32)], full, keep)
    mine, theirs = call(far_rows_kernel, "far_rows", [((1024, 512), BF)] * 2, pos, after(far_rows, send))
    got, mine, theirs = lax.optimization_barrier((got, mine, theirs))
    rows += [mine, shift(theirs, "c", 1)]
    delta, sums = call(
        delta_second_kernel,
        "delta",
        [((512, 512), BF), ((8, 128), F32)],
        own, got, slope, tan_start, tan_image, delta,
    )
    deltas = over_dp(delta)
    image_one = call(
        far_image_kernel, "far_image", [((1024, 512), F32)], after(near_one, delta), *rows[2:], *first_deltas[2:]
    )
    near = call(near_image_kernel, "near_image", [((1024, 512), F32)], *rows[:2], *deltas[:2])
    near, image_one = lax.optimization_barrier((near, image_one))
    image_two, block = call(
        last_image_kernel, "last_image", [((1024, 512), F32), ((8, 128), F32)], near, *rows[2:], *deltas[2:], sums
    )
    got = lax.all_to_all(jnp.broadcast_to(block[None], (128, 8, 128)), NAMES, 0, 0, tiled=True)
    whole = lambda *s: pl.BlockSpec(s, lambda i: (0,) * len(s))
    band = pl.BlockSpec((256, 512), lambda i: (i, 0))
    next_vector, coefficients = pl.pallas_call(
        final_kernel,
        grid=(4,),
        out_shape=[jax.ShapeDtypeStruct((1024, 512), F32), jax.ShapeDtypeStruct((1, 128), F32)],
        in_specs=[whole(128, 8, 128), whole(8, 128), band, band, band],
        out_specs=[band, whole(1, 128)],
        compiler_params=pltpu.CompilerParams(vmem_limit_bytes=16 * MIB),
        name="final",
    )(got, scalars, start, image_one, image_two)
    return (coefficients[0, :4], next_vector)


def solution(mesh):
    inner = Mesh(mesh.devices.reshape([n for _, n in AXES]), NAMES)
    dp, fsdp = ("yh", "c"), ("x", "z", "yl")
    in_specs = (P(dp, fsdp), P(None, fsdp), P(None, fsdp), P(fsdp, None), P(dp, fsdp), P(dp, fsdp))
    out_specs = (P(), P(dp, fsdp))
    return jax.shard_map(shards, mesh=inner, in_specs=in_specs, out_specs=out_specs, check_vma=False)
```

```python
import jax
import jax.numpy as jnp
from jax import lax
from jax.experimental import pallas as pl
from jax.experimental.pallas import tpu as pltpu
from jax.sharding import Mesh
from jax.sharding import PartitionSpec as P

D = 4096
FF = 16384
EPS = 1e-06
TOKENS = 2048
SCALE_INV = 1.0 / (D * FF)
AXES = (("yh", 2), ("c", 2), ("x", 4), ("z", 4), ("yl", 2))
NAMES = tuple(name for name, _ in AXES)
SIZES = dict(AXES)
BF = jnp.bfloat16
F32 = jnp.float32
MIB = 1024 * 1024
VM = pl.BlockSpec(memory_space=pltpu.VMEM)
SM = pl.BlockSpec(memory_space=pltpu.SMEM)


def shift(value, axis, by):
    n = SIZES[axis]
    return lax.ppermute(value, axis, [((i + by) % n, i) for i in range(n)])


def line(v, a):
    return [v, shift(v, a, 1), shift(v, a, 2), shift(v, a, 3)]


def after(value, *others):
    return lax.optimization_barrier((value, *others))[0]


def call(kernel, name, out, *operands, mib=16):
    specs = [SM if v.dtype == jnp.int32 else VM for v in operands]
    shapes = [jax.ShapeDtypeStruct(s, t) for s, t in out]
    got = pl.pallas_call(
        kernel,
        out_shape=shapes,
        in_specs=specs,
        out_specs=[VM] * len(shapes),
        compiler_params=pltpu.CompilerParams(vmem_limit_bytes=mib * MIB),
        name=name,
    )(*operands)
    return got if len(got) > 1 else got[0]


def gather(v):
    here, far = lax.optimization_barrier((line(v, "x"), shift(v, "z", 2)))
    here = jnp.stack(here)
    return [here, shift(here, "z", 1), *line(far, "x"), shift(here, "z", 3)]


def blocks(pos, refs, width):
    here, nxt, f0, f1, f2, f3, prev = refs
    for i, f in enumerate((f0, f1, f2, f3)):
        yield place(pos, i, 0, width), here[i]
        yield place(pos, i, 1, width), nxt[i]
        yield place(pos, i, 2, width), f[...]
        yield place(pos, i, 3, width), prev[i]


def nt(a, b):
    return lax.dot_general(a, b, (((1,), (1,)), ((), ())), preferred_element_type=F32)


def nn(a, b):
    return jnp.dot(a, b, preferred_element_type=F32)


def place(pos, i, j, width):
    return pl.multiple_of((lax.rem(pos[0] + i, 4) * 4 + lax.rem(pos[1] + j, 4)) * width, width)


def total(v):
    return jnp.sum(v, axis=(0, 1), keepdims=True) * SCALE_INV


def row_of(values, rows, width):
    index = lax.broadcasted_iota(jnp.int32, (rows, width), 0)
    out = jnp.zeros((rows, width), F32)
    for i, v in enumerate(values):
        out = jnp.where(index == i, jnp.broadcast_to(v, (rows, width)), out)
    return out


def digits(values, width):
    rows = []
    for v in values:
        for _ in range(3):
            d = v.astype(BF).astype(F32)
            rows.append(d)
            v = v - d
    return row_of(rows, 16, width).astype(BF)


def undigit(rows):
    return [rows[3 * i:3 * i + 1] + rows[3 * i + 1:3 * i + 2] + rows[3 * i + 2:3 * i + 3] for i in range(3)]


def cast_kernel(start, out, squares):
    acc = jnp.zeros((8, 512), F32)
    for i in range(0, 1024, 8):
        v = start[i:i + 8, :]
        acc = acc + v * v
    out[...] = start[...].astype(BF)
    squares[...] = acc


def split_kernel(pos, down, keep, send):
    yl = pos[2]
    mine = pl.ds(pl.multiple_of(pos[8] * 256, 256), 256)
    for b in range(16):
        keep[:, b * 128:(b + 1) * 128] = down[:, pl.ds(pl.multiple_of((2 * b + yl) * 128, 128), 128)]
        send[:, b * 128:(b + 1) * 128] = down[mine, pl.ds(pl.multiple_of((2 * b + 1 - yl) * 128, 128), 128)]


def join_kernel(pos, mine, theirs, out):
    out[pl.ds(pl.multiple_of(pos[8] * 256, 256), 256), :] = mine[...]
    out[pl.ds(pl.multiple_of((1 - pos[8]) * 256, 256), 256), :] = theirs[...]


def front_kernel(pos, *refs):
    gate_w, up_w = refs[7:9]
    rows = refs[9]
    feats, slope, tangent, pushed = refs[10:]
    for col, block in blocks(pos, refs[:7], 256):
        feats[:, pl.ds(col, 256)] = block
    gate = nn(feats[...], gate_w[...])
    sigma = 1.0 / (1.0 + jnp.exp(-gate))
    slope[...] = sigma * (1.0 + gate * (1.0 - sigma)) * nn(feats[...], up_w[...])
    acc = nn(feats[...], rows[...])
    tangent[...] = acc
    pushed[...] = (slope[...] * acc).astype(BF)


def push_kernel(own, other, keep, recv, out):
    for b in range(0, 16, 4):
        cols = slice(b * 128, (b + 4) * 128)
        r = (nn(own[:512], keep[:, cols]) + nn(other[:512], recv[:, cols])).astype(BF)
        for i in range(4):
            out[b + i, :512, :] = r[:, i * 128:(i + 1) * 128]
    if out.shape[1] > 512:
        sums = undigit(own[512:].astype(F32) + other[512:].astype(F32))
        extra = digits(sums, 512)[:, :128]
        for b in range(16):
            out[b, 512:, :] = extra


def weigh_first_kernel(got, curvature, moved, weighted):
    acc = got[0].astype(F32)
    for i in range(1, 16):
        acc = acc + got[i].astype(F32)
    moved[...] = acc
    weighted[...] = (curvature[...] * acc / TOKENS).astype(BF)


def weigh_second_kernel(got, curvature, moved, weighted, scalars):
    acc = got[0, :512, :].astype(F32)
    tail = got[0, 512:, :].astype(F32)
    for i in range(1, 16):
        acc = acc + got[i, :512, :].astype(F32)
        tail = tail + got[i, 512:, :].astype(F32)
    ss, sw, dd = undigit(tail)
    alpha = sw / (ss + EPS)
    scale = lax.rsqrt(dd + 1e-30) * (1.0 / 1024.0)
    weighted[...] = (curvature[...] * ((acc - alpha * moved[...]) * scale) / TOKENS).astype(BF)
    scalars[...] = row_of([ss, sw, scale], 8, 128)


def back_kernel(pos, *refs):
    recv, full, send = refs[7:]
    for col, block in blocks(pos, refs[:7], 128):
        full[:, pl.ds(col, 128)] = block
    send[...] = nt(full[...], recv[...]).astype(BF)


def own_back_kernel(full, keep, out):
    out[...] = nt(full[...], keep[...])


def delta_first_kernel(own, got, slope, tangent, squares, out):
    delta = ((own[...] + got[...].astype(F32)) * slope[...]).astype(BF)
    out[:512, :] = delta
    delta = delta.astype(F32)
    sums = [total(squares[...]), total(tangent[...] * delta), total(delta * (delta * 1.0))]
    out[512:, :] = digits([jnp.broadcast_to(v, (1, 512)) for v in sums], 512)


def delta_second_kernel(own, got, slope, tan_start, tan_image, delta_one, out, sums):
    delta = ((own[...] + got[...].astype(F32)) * slope[...]).astype(BF)
    out[...] = delta
    delta = delta.astype(F32)
    ww = total(tan_image[...] * delta_one[:512].astype(F32))
    sums[...] = row_of([ww, total(tan_start[...] * delta), total(tan_image[...] * delta)], 8, 128)


def gram_kernel(feats, one, two, out):
    n = one.shape[0]
    out[:, :n] = nt(feats[...], one[...])
    out[:, n:] = nt(feats[...], two[...])


def rows_kernel(pos, feats, out):
    out[...] = feats[:, pl.ds(pl.multiple_of(pos[3] * 1024, 1024), 1024)].T


def far_rows_kernel(pos, feats, out, other):
    c = pos[8]
    out[...] = feats[:, pl.ds(pl.multiple_of(c * 1024, 1024), 1024)].T
    other[...] = feats[:, pl.ds(pl.multiple_of((1 - c) * 1024, 1024), 1024)].T


def gram_split_kernel(pos, near, p0, p1, p2, p3, high, low):
    def put(cols, v):
        top = v.astype(BF)
        high[:, cols] = top
        low[:, cols] = (v - top.astype(F32)).astype(BF)

    put(slice(0, 1024), near[...])
    for i, p in enumerate((p0, p1, p2, p3)):
        q = lax.rem(pos[0] + i, 4) * 128
        put(pl.ds(pl.multiple_of(1024 + q, 128), 128), p[:, :128])
        put(pl.ds(pl.multiple_of(1536 + q, 128), 128), p[:, 128:])


def near_tangent_kernel(high, low, d0, d1, out):
    acc = nn(high[:, :512], d0[:512]) + nn(low[:, :512], d0[:512])
    out[...] = acc + nn(high[:, 512:1024], d1[:512]) + nn(low[:, 512:1024], d1[:512])


def far_tangent_kernel(near, high, low, d0, d1, d2, d3, slope, tangent, pushed):
    acc = near[...] + nn(high[:, 1024:1536], d2[:512]) + nn(low[:, 1024:1536], d2[:512])
    acc = acc + nn(high[:, 1536:], d3[:512]) + nn(low[:, 1536:], d3[:512])
    tangent[...] = acc
    pushed[:512, :] = (slope[...] * acc).astype(BF)
    rows = d0[512:].astype(F32) + d1[512:].astype(F32) + d2[512:].astype(F32) + d3[512:].astype(F32)
    pushed[512:, :] = digits(undigit(rows), 512)


def near_image_kernel(r0, r1, d0, d1, out):
    out[...] = nn(r0[...], d0[:512]) + nn(r1[...], d1[:512])


def far_image_kernel(near, r2, r3, d2, d3, out):
    out[...] = near[...] + nn(r2[...], d2[:512]) + nn(r3[...], d3[:512])


def last_image_kernel(near, r2, r3, d2, d3, sums, out, block):
    acc = near[...] + nn(r2[...], d2[...]) + nn(r3[...], d3[...])
    out[...] = acc
    index = lax.broadcasted_iota(jnp.int32, (8, 128), 0)
    block[...] = jnp.where(index == 3, jnp.broadcast_to(total(acc * acc), (8, 128)), sums[...])


def final_kernel(got, scalars, start, image_one, image_two, out, coefficients):
    acc = got[0]
    for i in range(1, 128):
        acc = acc + got[i]
    ss, sw, scale = scalars[0:1], scalars[1:2], scalars[2:3]
    ww, uz, wz, zz = acc[0:1], acc[1:2], acc[2:3], acc[3:4]
    norm_sq = ss + EPS
    norm = jnp.sqrt(norm_sq)
    alpha_one = sw / norm_sq
    one_one = ss / norm_sq
    resid_sq = jnp.maximum(ww / norm_sq - alpha_one * alpha_one * (2.0 - one_one), 0.0)
    beta_one = jnp.sqrt(resid_sq + EPS)
    second = 1.0 / (norm * beta_one)
    image = second / scale
    alpha_two = image * second * (wz - alpha_one * uz)
    cross = image * uz / norm
    two_two = resid_sq / (resid_sq + EPS)
    one_two = alpha_one * (1.0 - one_one) / beta_one
    last_sq = (
        image * image * zz
        - alpha_two * alpha_two * (2.0 - two_two)
        - cross * cross * (2.0 - one_one)
        + 2.0 * alpha_two * cross * one_two
    )
    beta_two = jnp.sqrt(jnp.maximum(last_sq, 0.0) + EPS)
    index = lax.broadcasted_iota(jnp.int32, (1, 128), 1)
    row = jnp.zeros((1, 128), F32)
    for i, v in enumerate((alpha_one, beta_one, alpha_two, beta_two)):
        row = jnp.where(index == i, v, row)
    coefficients[...] = row
    f_two = image / beta_two
    f_one = -alpha_two * second / beta_two
    f_start = (alpha_two * alpha_one / beta_one - cross) / (norm * beta_two)
    for k in range(4):
        cols = slice(k * 128, (k + 1) * 128)
        out[:, cols] = f_two * image_two[:, cols] + f_one * image_one[:, cols] + f_start * start[:, cols]


def over_dp(v):
    far = shift(v, "yh", 1)
    return [v, shift(v, "c", 1), far, shift(far, "c", 1)]


def shards(tokens, gate_weight, up_weight, down_weight, curvature, start):
    yh, c, x, z, yl = [lax.axis_index(n).astype(jnp.int32) for n in NAMES]
    dp = yh * 2 + c
    pos = jnp.stack([x, z, yl, dp, dp, dp, dp, dp, c])

    start_b, squares = call(cast_kernel, "cast_start", [((1024, 512), BF), ((8, 512), F32)], start)
    start_all = lax.all_gather(start_b, ("yh", "c"), axis=0, tiled=True)
    other = shift(tokens, "yl", 1)
    keep, send = call(
        split_kernel,
        "split_down",
        [((512, 2048), BF), ((256, 2048), BF)],
        pos, down_weight,
    )
    other, send = lax.optimization_barrier((other, send))
    pair = jnp.where(
        yl == 0, jnp.concatenate([tokens, other], axis=1), jnp.concatenate([other, tokens], axis=1)
    )
    recv = shift(send, "yl", 1)
    pieces = gather(pair)
    recv, pieces = lax.optimization_barrier((recv, pieces))
    feats, slope, tan_start, pushed = call(
        front_kernel,
        "front",
        [((512, D), BF), ((512, 512), F32), ((512, 512), F32), ((512, 512), BF)],
        pos, *pieces, gate_weight, up_weight, start_all,
        mib=32,
    )
    recv = call(join_kernel, "join", [((512, 2048), BF)], pos, recv, shift(recv, "c", 1))

    other = shift(pushed, "yl", 1)
    feats_c = shift(feats, "c", 1)
    near_gram = call(gram_kernel, "near_gram", [((512, 1024), F32)], feats, feats, feats_c)
    other, near_gram = lax.optimization_barrier((other, near_gram))
    parts = call(push_kernel, "push", [((16, 512, 128), BF)], pushed, other, keep, recv)
    quarter = lax.dynamic_slice_in_dim(feats, x * 128, 128, axis=0)
    quarter = shift(after(quarter, parts), "yh", 1)
    quarter_c = shift(quarter, "c", 1)
    got = lax.all_to_all(parts, ("x", "z"), 0, 0, tiled=True)
    moved, weighted = call(weigh_first_kernel, "weigh", [((512, 128), F32), ((512, 128), BF)], got, curvature)
    pieces = gather(weighted)
    far_gram = call(gram_kernel, "far_gram", [((512, 256), F32)], after(feats, pieces[0]), quarter, quarter_c)
    recv_one, far_gram = lax.optimization_barrier((recv, far_gram))
    full, send = call(back_kernel, "back_other", [((512, 2048), BF), ((512, 512), BF)], pos, *pieces, recv_one)
    got = shift(send, "yl", 1)
    own = call(own_back_kernel, "back_own", [((512, 512), F32)], full, keep)
    far_gram = after(far_gram, send)
    far_one, far_three = shift(far_gram, "x", 1), shift(far_gram, "x", 3)
    got, far_one, far_three = lax.optimization_barrier((got, far_one, far_three))
    far_grams = [far_gram, far_one, shift(after(far_gram, got), "x", 2), far_three]
    delta = call(delta_first_kernel, "delta", [((528, 512), BF)], own, got, slope, tan_start, squares)
    deltas = over_dp(delta)
    high, low = call(gram_split_kernel, "gram_split", [((512, 2048), BF)] * 2, pos, near_gram, *far_grams)
    near = call(near_tangent_kernel, "near_tangent", [((512, 512), F32)], high, low, *deltas[:2])
    tan_image, pushed = call(
        far_tangent_kernel,
        "far_tangent",
        [((512, 512), F32), ((528, 512), BF)],
        near, high, low, *deltas, slope,
    )

    other = shift(pushed, "yl", 1)
    parts = call(push_kernel, "push", [((16, 528, 128), BF)], pushed, other, keep, recv)
    theirs = lax.dynamic_slice_in_dim(feats, (1 - yh) * 2048, 2048, axis=1)
    far_rows = shift(after(theirs, parts), "yh", 1)
    got = lax.all_to_all(parts, ("x", "z"), 0, 0, tiled=True)
    first_deltas = deltas
    rows = [call(rows_kernel, "rows", [((1024, 512), BF)], pos, after(f, parts)) for f in (feats, feats_c)]
    near_one = call(
        near_image_kernel, "near_image", [((1024, 512), F32)], *rows, after(first_deltas[0], parts), first_deltas[1]
    )
    got, near_one = lax.optimization_barrier((got, near_one))
    weighted, scalars = call(
        weigh_second_kernel, "weigh", [((512, 128), BF), ((8, 128), F32)], got, curvature, moved
    )
    full, send = call(
        back_kernel, "back_other", [((512, 2048), BF), ((512, 512), BF)], pos, *gather(weighted), recv
    )
    got = shift(send, "yl", 1)
    own = call(own_back_kernel, "back_own", [((512, 512), F32)], full, keep)
    mine, theirs = call(far_rows_kernel, "far_rows", [((1024, 512), BF)] * 2, pos, after(far_rows, send))
    got, mine, theirs = lax.optimization_barrier((got, mine, theirs))
    rows += [mine, shift(theirs, "c", 1)]
    delta, sums = call(
        delta_second_kernel,
        "delta",
        [((512, 512), BF), ((8, 128), F32)],
        own, got, slope, tan_start, tan_image, delta,
    )
    deltas = over_dp(delta)
    image_one = call(
        far_image_kernel, "far_image", [((1024, 512), F32)], after(near_one, delta), *rows[2:], *first_deltas[2:]
    )
    near = call(near_image_kernel, "near_image", [((1024, 512), F32)], *rows[:2], *deltas[:2])
    near, image_one = lax.optimization_barrier((near, image_one))
    image_two, block = call(
        last_image_kernel, "last_image", [((1024, 512), F32), ((8, 128), F32)], near, *rows[2:], *deltas[2:], sums
    )
    got = lax.all_to_all(jnp.broadcast_to(block[None], (128, 8, 128)), NAMES, 0, 0, tiled=True)
    whole = lambda *s: pl.BlockSpec(s, lambda i: (0,) * len(s))
    band = pl.BlockSpec((256, 512), lambda i: (i, 0))
    next_vector, coefficients = pl.pallas_call(
        final_kernel,
        grid=(4,),
        out_shape=[jax.ShapeDtypeStruct((1024, 512), F32), jax.ShapeDtypeStruct((1, 128), F32)],
        in_specs=[whole(128, 8, 128), whole(8, 128), band, band, band],
        out_specs=[band, whole(1, 128)],
        compiler_params=pltpu.CompilerParams(vmem_limit_bytes=16 * MIB),
        name="final",
    )(got, scalars, start, image_one, image_two)
    return (coefficients[0, :4], next_vector)


def solution(mesh):
    inner = Mesh(mesh.devices.reshape([n for _, n in AXES]), NAMES)
    dp, fsdp = ("yh", "c"), ("x", "z", "yl")
    in_specs = (P(dp, fsdp), P(None, fsdp), P(None, fsdp), P(fsdp, None), P(dp, fsdp), P(dp, fsdp))
    out_specs = (P(), P(dp, fsdp))
    return jax.shard_map(shards, mesh=inner, in_specs=in_specs, out_specs=out_specs, check_vma=False)
```

```python
import jax
import jax.numpy as jnp
from jax import lax
from jax.experimental import pallas as pl
from jax.experimental.pallas import tpu as pltpu
from jax.sharding import Mesh
from jax.sharding import PartitionSpec as P

D = 4096
FF = 16384
EPS = 1e-06
TOKENS = 2048
SCALE_INV = 1.0 / (D * FF)
AXES = (("yh", 2), ("c", 2), ("x", 4), ("z", 4), ("yl", 2))
NAMES = tuple(name for name, _ in AXES)
SIZES = dict(AXES)
BF = jnp.bfloat16
F32 = jnp.float32
MIB = 1024 * 1024
VM = pl.BlockSpec(memory_space=pltpu.VMEM)
SM = pl.BlockSpec(memory_space=pltpu.SMEM)


def shift(value, axis, by):
    n = SIZES[axis]
    return lax.ppermute(value, axis, [((i + by) % n, i) for i in range(n)])


def line(v, a):
    return [v, shift(v, a, 1), shift(v, a, 2), shift(v, a, 3)]


def after(value, *others):
    return lax.optimization_barrier((value, *others))[0]


def call(kernel, name, out, *operands, mib=16, scratch=()):
    specs = [SM if v.dtype == jnp.int32 else VM for v in operands]
    shapes = [jax.ShapeDtypeStruct(s, t) for s, t in out]
    got = pl.pallas_call(
        kernel,
        out_shape=shapes,
        in_specs=specs,
        out_specs=[VM] * len(shapes),
        scratch_shapes=[pltpu.VMEM(s, t) for s, t in scratch],
        compiler_params=pltpu.CompilerParams(vmem_limit_bytes=mib * MIB),
        name=name,
    )(*operands)
    return got if len(got) > 1 else got[0]


def gather(v, later=()):
    here, far, later = lax.optimization_barrier((line(v, "x"), shift(v, "z", 2), later))
    here = jnp.stack(here)
    return [here, shift(here, "z", 1), *line(far, "x"), shift(here, "z", 3)], later


def scatter(parts):
    row0, row1, row3, f0, f1, f2, f3 = parts
    up, down = shift(row1, "z", 3), shift(row3, "z", 1)
    far = [f0, shift(f1, "x", 3), shift(f2, "x", 2), shift(f3, "x", 1)]
    block = (f0.shape, BF)
    r0, r1, r2, r3, far = call(add_kernel, "add", [block] * 5, row0, up, down, *far)
    return [r0, shift(r1, "x", 3), shift(r2, "x", 2), shift(r3, "x", 1), shift(far, "z", 2)]


def add_up(*blocks):
    acc = blocks[0].astype(F32)
    for b in blocks[1:]:
        acc = acc + b.astype(F32)
    return acc[:512], undigit(acc[512:]) if acc.shape[0] > 512 else None


def add_kernel(row0, up, down, f0, f1, f2, f3, r0, r1, r2, r3, far):
    def put(out, *blocks):
        acc, sums = add_up(*blocks)
        out[:512, :] = acc.astype(BF)
        if sums is not None:
            out[512:, :] = digits(sums, 128)

    put(far, f0[...], f1[...], f2[...], f3[...])
    for i, r in enumerate((r0, r1, r2, r3)):
        put(r, row0[i], up[i], down[i])


def blocks(pos, refs, width):
    here, nxt, f0, f1, f2, f3, prev = refs
    for i, f in enumerate((f0, f1, f2, f3)):
        yield place(pos, i, 0, width), here[i]
        yield place(pos, i, 1, width), nxt[i]
        yield place(pos, i, 2, width), f[...]
        yield place(pos, i, 3, width), prev[i]


def nt(a, b):
    return lax.dot_general(a, b, (((1,), (1,)), ((), ())), preferred_element_type=F32)


def nn(a, b):
    return jnp.dot(a, b, preferred_element_type=F32)


def place(pos, i, j, width):
    return pl.multiple_of((lax.rem(pos[0] + i, 4) * 4 + lax.rem(pos[1] + j, 4)) * width, width)


def total(v):
    return jnp.sum(v, axis=(0, 1), keepdims=True) * SCALE_INV


def row_of(values, rows, width):
    index = lax.broadcasted_iota(jnp.int32, (rows, width), 0)
    out = jnp.zeros((rows, width), F32)
    for i, v in enumerate(values):
        out = jnp.where(index == i, jnp.broadcast_to(v, (rows, width)), out)
    return out


def digits(values, width):
    rows = []
    for v in values:
        for _ in range(3):
            d = v.astype(BF).astype(F32)
            rows.append(d)
            v = v - d
    return row_of(rows, 16, width).astype(BF)


def undigit(rows):
    return [rows[3 * i:3 * i + 1] + rows[3 * i + 1:3 * i + 2] + rows[3 * i + 2:3 * i + 3] for i in range(3)]


def cast_kernel(start, out, squares):
    acc = jnp.zeros((8, 512), F32)
    for i in range(0, 1024, 8):
        v = start[i:i + 8, :]
        acc = acc + v * v
    out[...] = start[...].astype(BF)
    squares[...] = acc


def split_kernel(pos, down, keep, send):
    yl = pos[2]
    mine = pl.ds(pl.multiple_of(pos[8] * 256, 256), 256)
    for b in range(16):
        keep[:, b * 128:(b + 1) * 128] = down[:, pl.ds(pl.multiple_of((2 * b + yl) * 128, 128), 128)]
        send[:, b * 128:(b + 1) * 128] = down[mine, pl.ds(pl.multiple_of((2 * b + 1 - yl) * 128, 128), 128)]


def join_kernel(pos, mine, theirs, out):
    out[pl.ds(pl.multiple_of(pos[8] * 256, 256), 256), :] = mine[...]
    out[pl.ds(pl.multiple_of((1 - pos[8]) * 256, 256), 256), :] = theirs[...]


def front_kernel(pos, *refs):
    gate_w, up_w = refs[7:9]
    rows = refs[9:13]
    feats, slope, tangent, pushed = refs[13:]
    for col, block in blocks(pos, refs[:7], 256):
        feats[:, pl.ds(col, 256)] = block
    gate = nn(feats[...], gate_w[...])
    sigma = 1.0 / (1.0 + jnp.exp(-gate))
    slope[...] = sigma * (1.0 + gate * (1.0 - sigma)) * nn(feats[...], up_w[...])
    acc = jnp.zeros(tangent.shape, F32)
    for k in range(4):
        cols = pl.multiple_of(pos[4 + k] * 1024, 1024)
        acc = acc + nn(feats[:, pl.ds(cols, 1024)], rows[k][...])
    tangent[...] = acc
    pushed[...] = (slope[...] * acc).astype(BF)


def push_kernel(pos, own, other, keep, recv, row0, row1, row3, f0, f1, f2, f3, strip):
    x, z = pos[0], pos[1]
    extra = None
    if own.shape[0] > 512:
        extra = digits(undigit(own[512:].astype(F32) + other[512:].astype(F32)), 512)[:, :128]

    def put(out, block):
        out[:512] = block
        if extra is not None:
            out[512:] = extra

    for i, f in enumerate((f0, f1, f2, f3)):
        cols = pl.ds(pl.multiple_of(lax.rem(x + i, 4) * 512, 512), 512)
        strip[...] = (nn(own[:512], keep[:, cols]) + nn(other[:512], recv[:, cols])).astype(BF)
        for j, out in enumerate((row0.at[i], row1.at[i], f, row3.at[i])):
            put(out, strip[:, pl.ds(pl.multiple_of(lax.rem(z + j, 4) * 128, 128), 128)])


def weigh_first_kernel(b0, b1, b2, b3, b4, curvature, moved, weighted):
    acc, _ = add_up(b0[...], b1[...], b2[...], b3[...], b4[...])
    moved[...] = acc
    weighted[...] = (curvature[...] * acc / TOKENS).astype(BF)


def weigh_second_kernel(b0, b1, b2, b3, b4, curvature, moved, weighted, scalars):
    acc, (ss, sw, dd) = add_up(b0[...], b1[...], b2[...], b3[...], b4[...])
    alpha = sw / (ss + EPS)
    scale = lax.rsqrt(dd + 1e-30) * (1.0 / 1024.0)
    weighted[...] = (curvature[...] * ((acc - alpha * moved[...]) * scale) / TOKENS).astype(BF)
    scalars[...] = row_of([ss, sw, scale], 8, 128)


def back_kernel(pos, *refs):
    recv, full, send = refs[7:]
    for col, block in blocks(pos, refs[:7], 128):
        full[:, pl.ds(col, 128)] = block
    send[...] = nt(full[...], recv[...]).astype(BF)


def own_back_kernel(full, keep, out):
    out[...] = nt(full[...], keep[...])


def delta_first_kernel(own, got, slope, tangent, squares, out):
    delta = ((own[...] + got[...].astype(F32)) * slope[...]).astype(BF)
    out[:512, :] = delta
    delta = delta.astype(F32)
    sums = [total(squares[...]), total(tangent[...] * delta), total(delta * (delta * 1.0))]
    out[512:, :] = digits([jnp.broadcast_to(v, (1, 512)) for v in sums], 512)


def delta_second_kernel(own, got, slope, tan_start, tan_image, delta_one, out, sums):
    delta = ((own[...] + got[...].astype(F32)) * slope[...]).astype(BF)
    out[...] = delta
    delta = delta.astype(F32)
    ww = total(tan_image[...] * delta_one[:512].astype(F32))
    sums[...] = row_of([ww, total(tan_start[...] * delta), total(tan_image[...] * delta)], 8, 128)


def gram_kernel(feats, one, out):
    out[...] = nt(feats[...], one[...])


def far_gram_kernel(feats, one, two, out):
    out[:, :128] = nt(feats[...], one[...])
    out[:, 128:] = nt(feats[...], two[...])


def rows_kernel(pos, feats, out):
    out[...] = feats[:, pl.ds(pl.multiple_of(pos[3] * 1024, 1024), 1024)].T


def far_rows_kernel(pos, feats, out, other):
    c = pos[8]
    out[...] = feats[:, pl.ds(pl.multiple_of(c * 1024, 1024), 1024)].T
    other[...] = feats[:, pl.ds(pl.multiple_of((1 - c) * 1024, 1024), 1024)].T


def gram_split_kernel(pos, own, core, p0, p1, p2, p3, high, low):
    def put(cols, v):
        top = v.astype(BF)
        high[:, cols] = top
        low[:, cols] = (v - top.astype(F32)).astype(BF)

    put(slice(0, 512), own[...])
    put(slice(512, 1024), core[...])
    for i, p in enumerate((p0, p1, p2, p3)):
        q = lax.rem(pos[9] + i, 4) * 128
        put(pl.ds(pl.multiple_of(1024 + q, 128), 128), p[:, :128])
        put(pl.ds(pl.multiple_of(1536 + q, 128), 128), p[:, 128:])


def near_tangent_kernel(high, low, d0, d1, out):
    acc = nn(high[:, :512], d0[:512]) + nn(low[:, :512], d0[:512])
    out[...] = acc + nn(high[:, 512:1024], d1[:512]) + nn(low[:, 512:1024], d1[:512])


def far_tangent_kernel(near, high, low, d0, d1, d2, d3, slope, tangent, pushed):
    acc = near[...] + nn(high[:, 1024:1536], d2[:512]) + nn(low[:, 1024:1536], d2[:512])
    acc = acc + nn(high[:, 1536:], d3[:512]) + nn(low[:, 1536:], d3[:512])
    tangent[...] = acc
    pushed[:512, :] = (slope[...] * acc).astype(BF)
    rows = d0[512:].astype(F32) + d1[512:].astype(F32) + d2[512:].astype(F32) + d3[512:].astype(F32)
    pushed[512:, :] = digits(undigit(rows), 512)


def near_image_kernel(r0, r1, d0, d1, out):
    out[...] = nn(r0[...], d0[:512]) + nn(r1[...], d1[:512])


def far_image_kernel(near, r2, r3, d2, d3, out):
    out[...] = near[...] + nn(r2[...], d2[:512]) + nn(r3[...], d3[:512])


def last_image_kernel(near, r2, r3, d2, d3, sums, out, block):
    acc = near[...] + nn(r2[...], d2[...]) + nn(r3[...], d3[...])
    out[...] = acc
    index = lax.broadcasted_iota(jnp.int32, (8, 128), 0)
    block[...] = jnp.where(index == 3, jnp.broadcast_to(total(acc * acc), (8, 128)), sums[...])


def final_kernel(got, scalars, start, image_one, image_two, out, coefficients):
    acc = got[0]
    for i in range(1, 128):
        acc = acc + got[i]
    ss, sw, scale = scalars[0:1], scalars[1:2], scalars[2:3]
    ww, uz, wz, zz = acc[0:1], acc[1:2], acc[2:3], acc[3:4]
    norm_sq = ss + EPS
    norm = jnp.sqrt(norm_sq)
    alpha_one = sw / norm_sq
    one_one = ss / norm_sq
    resid_sq = jnp.maximum(ww / norm_sq - alpha_one * alpha_one * (2.0 - one_one), 0.0)
    beta_one = jnp.sqrt(resid_sq + EPS)
    second = 1.0 / (norm * beta_one)
    image = second / scale
    alpha_two = image * second * (wz - alpha_one * uz)
    cross = image * uz / norm
    two_two = resid_sq / (resid_sq + EPS)
    one_two = alpha_one * (1.0 - one_one) / beta_one
    last_sq = (
        image * image * zz
        - alpha_two * alpha_two * (2.0 - two_two)
        - cross * cross * (2.0 - one_one)
        + 2.0 * alpha_two * cross * one_two
    )
    beta_two = jnp.sqrt(jnp.maximum(last_sq, 0.0) + EPS)
    index = lax.broadcasted_iota(jnp.int32, (1, 128), 1)
    row = jnp.zeros((1, 128), F32)
    for i, v in enumerate((alpha_one, beta_one, alpha_two, beta_two)):
        row = jnp.where(index == i, v, row)
    coefficients[...] = row
    f_two = image / beta_two
    f_one = -alpha_two * second / beta_two
    f_start = (alpha_two * alpha_one / beta_one - cross) / (norm * beta_two)
    for k in range(4):
        cols = slice(k * 128, (k + 1) * 128)
        out[:, cols] = f_two * image_two[:, cols] + f_one * image_one[:, cols] + f_start * start[:, cols]


def over_dp(v):
    far = shift(v, "yh", 1)
    return [v, shift(v, "c", 1), far, shift(far, "c", 1)]


def shards(tokens, gate_weight, up_weight, down_weight, curvature, start):
    yh, c, x, z, yl = [lax.axis_index(n).astype(jnp.int32) for n in NAMES]
    dp = yh * 2 + c
    quarter_of = lax.rem(x + 2 * z, 4)
    pos = jnp.stack(
        [x, z, yl, dp, dp, yh * 2 + 1 - c, (1 - yh) * 2 + c, (1 - yh) * 2 + 1 - c, c, quarter_of]
    )

    other = shift(tokens, "yl", 1)
    start_b, squares = call(cast_kernel, "cast_start", [((1024, 512), BF), ((8, 512), F32)], start)
    keep, send = call(
        split_kernel,
        "split_down",
        [((512, 2048), BF), ((256, 2048), BF)],
        pos, down_weight,
    )
    other, start_b, send = lax.optimization_barrier((other, start_b, send))
    starts = over_dp(start_b)
    pair = jnp.where(
        yl == 0, jnp.concatenate([tokens, other], axis=1), jnp.concatenate([other, tokens], axis=1)
    )
    pieces, send = gather(pair, send)
    recv = shift(send, "yl", 1)
    recv, pieces = lax.optimization_barrier((recv, pieces))
    feats, slope, tan_start, pushed = call(
        front_kernel,
        "front",
        [((512, D), BF), ((512, 512), F32), ((512, 512), F32), ((512, 512), BF)],
        pos, *pieces, gate_weight, up_weight, *starts,
        mib=24,
    )
    recv = call(join_kernel, "join", [((512, 2048), BF)], pos, recv, shift(recv, "c", 1))
    row, block = (4, 512, 128), (512, 128)

    other = shift(pushed, "yl", 1)
    feats_c = shift(after(feats, recv), "c", 1)
    own_gram = call(gram_kernel, "own_gram", [((512, 512), F32)], after(feats, pushed), feats)
    other, own_gram = lax.optimization_barrier((other, own_gram))
    parts = call(
        push_kernel,
        "push",
        [(row, BF)] * 3 + [(block, BF)] * 4,
        pos, pushed, other, keep, recv,
        scratch=[((512, 512), BF)],
    )
    quarter = lax.dynamic_slice_in_dim(feats, quarter_of * 128, 128, axis=0)
    quarter = shift(after(quarter, parts[0]), "yh", 1)
    quarter_c = shift(quarter, "c", 1)
    moved, weighted = call(
        weigh_first_kernel, "weigh", [((512, 128), F32), ((512, 128), BF)], *scatter(parts), curvature
    )
    pieces, (quarter, quarter_c) = gather(weighted, (quarter, quarter_c))
    far_gram = call(far_gram_kernel, "far_gram", [((512, 256), F32)], feats, quarter, quarter_c)
    recv_one, far_gram = lax.optimization_barrier((recv, far_gram))
    full, send = call(back_kernel, "back_other", [((512, 2048), BF), ((512, 512), BF)], pos, *pieces, recv_one)
    got = shift(send, "yl", 1)
    far_gram = after(far_gram, send)
    far_grams = [far_gram, shift(far_gram, "x", 1), shift(far_gram, "z", 1), shift(far_gram, "x", 3)]
    own = call(own_back_kernel, "back_own", [((512, 512), F32)], full, keep)
    core_gram = call(gram_kernel, "core_gram", [((512, 512), F32)], after(feats, send), feats_c)
    got, core_gram, far_grams = lax.optimization_barrier((got, core_gram, far_grams))
    delta = call(delta_first_kernel, "delta", [((528, 512), BF)], own, got, slope, tan_start, squares)
    deltas = over_dp(delta)
    high, low = call(
        gram_split_kernel,
        "gram_split",
        [((512, 2048), BF)] * 2,
        pos, after(own_gram, delta), core_gram, *far_grams,
    )
    near = call(near_tangent_kernel, "near_tangent", [((512, 512), F32)], high, low, *deltas[:2])
    deltas, near = lax.optimization_barrier((deltas, near))
    tan_image, pushed = call(
        far_tangent_kernel,
        "far_tangent",
        [((512, 512), F32), ((528, 512), BF)],
        near, high, low, *deltas, slope,
    )

    row, block = (4, 528, 128), (528, 128)
    other = shift(pushed, "yl", 1)
    parts = call(
        push_kernel,
        "push",
        [(row, BF)] * 3 + [(block, BF)] * 4,
        pos, pushed, other, keep, recv,
        scratch=[((512, 512), BF)],
    )
    theirs = lax.dynamic_slice_in_dim(feats, (1 - yh) * 2048, 2048, axis=1)
    far_rows = shift(after(theirs, parts[0]), "yh", 1)
    first_deltas = deltas
    rows = [call(rows_kernel, "rows", [((1024, 512), BF)], pos, after(f, parts[0])) for f in (feats, feats_c)]
    near_one = call(
        near_image_kernel, "near_image", [((1024, 512), F32)], *rows, after(first_deltas[0], parts[0]), first_deltas[1]
    )
    weighted, scalars = call(
        weigh_second_kernel, "weigh", [((512, 128), BF), ((8, 128), F32)], *scatter(parts), curvature, moved
    )
    pieces, near_one = gather(weighted, near_one)
    full, send = call(
        back_kernel, "back_other", [((512, 2048), BF), ((512, 512), BF)], pos, *pieces, recv
    )
    got = shift(send, "yl", 1)
    own = call(own_back_kernel, "back_own", [((512, 512), F32)], full, keep)
    mine, theirs = call(far_rows_kernel, "far_rows", [((1024, 512), BF)] * 2, pos, after(far_rows, send))
    got, mine, theirs = lax.optimization_barrier((got, mine, theirs))
    rows += [mine, shift(theirs, "c", 1)]
    delta, sums = call(
        delta_second_kernel,
        "delta",
        [((512, 512), BF), ((8, 128), F32)],
        own, got, slope, tan_start, tan_image, delta,
    )
    deltas = over_dp(delta)
    image_one = call(
        far_image_kernel, "far_image", [((1024, 512), F32)], after(near_one, delta), *rows[2:], *first_deltas[2:]
    )
    near = call(near_image_kernel, "near_image", [((1024, 512), F32)], *rows[:2], *deltas[:2])
    near, image_one = lax.optimization_barrier((near, image_one))
    image_two, block = call(
        last_image_kernel, "last_image", [((1024, 512), F32), ((8, 128), F32)], near, *rows[2:], *deltas[2:], sums
    )
    got = lax.all_to_all(jnp.broadcast_to(block[None], (128, 8, 128)), NAMES, 0, 0, tiled=True)
    whole = lambda *s: pl.BlockSpec(s, lambda i: (0,) * len(s))
    band = pl.BlockSpec((256, 512), lambda i: (i, 0))
    next_vector, coefficients = pl.pallas_call(
        final_kernel,
        grid=(4,),
        out_shape=[jax.ShapeDtypeStruct((1024, 512), F32), jax.ShapeDtypeStruct((1, 128), F32)],
        in_specs=[whole(128, 8, 128), whole(8, 128), band, band, band],
        out_specs=[band, whole(1, 128)],
        compiler_params=pltpu.CompilerParams(vmem_limit_bytes=16 * MIB),
        name="final",
    )(got, scalars, start, image_one, image_two)
    return (coefficients[0, :4], next_vector)


def solution(mesh):
    inner = Mesh(mesh.devices.reshape([n for _, n in AXES]), NAMES)
    dp, fsdp = ("yh", "c"), ("x", "z", "yl")
    in_specs = (P(dp, fsdp), P(None, fsdp), P(None, fsdp), P(fsdp, None), P(dp, fsdp), P(dp, fsdp))
    out_specs = (P(), P(dp, fsdp))
    return jax.shard_map(shards, mesh=inner, in_specs=in_specs, out_specs=out_specs, check_vma=False)
```

```python
import jax
import jax.numpy as jnp
from jax import lax
from jax.experimental import pallas as pl
from jax.experimental.pallas import tpu as pltpu
from jax.sharding import Mesh
from jax.sharding import PartitionSpec as P

D = 4096
FF = 16384
EPS = 1e-06
TOKENS = 2048
SCALE_INV = 1.0 / (D * FF)
AXES = (("yh", 2), ("c", 2), ("x", 4), ("z", 4), ("yl", 2))
NAMES = tuple(name for name, _ in AXES)
SIZES = dict(AXES)
BF = jnp.bfloat16
F32 = jnp.float32
MIB = 1024 * 1024
VM = pl.BlockSpec(memory_space=pltpu.VMEM)
SM = pl.BlockSpec(memory_space=pltpu.SMEM)


def shift(value, axis, by):
    n = SIZES[axis]
    return lax.ppermute(value, axis, [((i + by) % n, i) for i in range(n)])


def from_y(v):
    pairs = []
    for y in range(4):
        for c in range(2):
            src = (y + (1 if c == 0 else 3)) % 4
            pairs.append(((src // 2 * 2 + c) * 2 + src % 2, (y // 2 * 2 + c) * 2 + y % 2))
    return lax.ppermute(v, ("yh", "c", "yl"), pairs)


def line(v, a):
    return [v, shift(v, a, 1), shift(v, a, 2), shift(v, a, 3)]


def after(value, *others):
    return lax.optimization_barrier((value, *others))[0]


def call(kernel, name, out, *operands, mib=16, scratch=()):
    specs = [SM if v.dtype == jnp.int32 else VM for v in operands]
    shapes = [jax.ShapeDtypeStruct(s, t) for s, t in out]
    got = pl.pallas_call(
        kernel,
        out_shape=shapes,
        in_specs=specs,
        out_specs=[VM] * len(shapes),
        scratch_shapes=[pltpu.VMEM(s, t) for s, t in scratch],
        compiler_params=pltpu.CompilerParams(vmem_limit_bytes=mib * MIB),
        name=name,
    )(*operands)
    return got if len(got) > 1 else got[0]


def gather(v, later=()):
    here, far, later = lax.optimization_barrier((line(v, "x"), shift(v, "z", 2), later))
    here = jnp.stack(here)
    return [here, shift(here, "z", 1), *line(far, "x"), shift(here, "z", 3)], later


def scatter(parts, later):
    row0, row1, row3, f0, f1, f2, f3 = parts
    up, down = shift(row1, "z", 3), shift(row3, "z", 1)
    far = [f0, shift(f1, "x", 3), shift(f2, "x", 2), shift(f3, "x", 1)]
    far, later = lax.optimization_barrier((far, later))
    block = (f0.shape, BF)
    r0, r1, r2, r3, far = call(add_kernel, "add", [block] * 5, row0, up, down, *far)
    return [r0, shift(r1, "x", 3), shift(r2, "x", 2), shift(r3, "x", 1), shift(far, "z", 2)], later


def add_up(*blocks):
    acc = blocks[0].astype(F32)
    for b in blocks[1:]:
        acc = acc + b.astype(F32)
    return acc[:512], undigit(acc[512:]) if acc.shape[0] > 512 else None


def add_kernel(row0, up, down, f0, f1, f2, f3, r0, r1, r2, r3, far):
    def put(out, *blocks):
        acc, sums = add_up(*blocks)
        out[:512, :] = acc.astype(BF)
        if sums is not None:
            out[512:, :] = digits(sums, 128)

    put(far, f0[...], f1[...], f2[...], f3[...])
    for i, r in enumerate((r0, r1, r2, r3)):
        put(r, row0[i], up[i], down[i])


def blocks(pos, refs, width):
    here, nxt, f0, f1, f2, f3, prev = refs
    for i, f in enumerate((f0, f1, f2, f3)):
        yield place(pos, i, 0, width), here[i]
        yield place(pos, i, 1, width), nxt[i]
        yield place(pos, i, 2, width), f[...]
        yield place(pos, i, 3, width), prev[i]


def nt(a, b):
    return lax.dot_general(a, b, (((1,), (1,)), ((), ())), preferred_element_type=F32)


def nn(a, b):
    return jnp.dot(a, b, preferred_element_type=F32)


def place(pos, i, j, width):
    return pl.multiple_of((lax.rem(pos[0] + i, 4) * 4 + lax.rem(pos[1] + j, 4)) * width, width)


def total(v):
    return jnp.sum(v, axis=(0, 1), keepdims=True) * SCALE_INV


def row_of(values, rows, width):
    index = lax.broadcasted_iota(jnp.int32, (rows, width), 0)
    out = jnp.zeros((rows, width), F32)
    for i, v in enumerate(values):
        out = jnp.where(index == i, jnp.broadcast_to(v, (rows, width)), out)
    return out


def digits(values, width):
    rows = []
    for v in values:
        for _ in range(3):
            d = v.astype(BF).astype(F32)
            rows.append(d)
            v = v - d
    return row_of(rows, 16, width).astype(BF)


def undigit(rows):
    return [rows[3 * i:3 * i + 1] + rows[3 * i + 1:3 * i + 2] + rows[3 * i + 2:3 * i + 3] for i in range(3)]


def cast_kernel(start, out, squares):
    acc = jnp.zeros((8, 512), F32)
    for i in range(0, 1024, 8):
        v = start[i:i + 8, :]
        acc = acc + v * v
    out[...] = start[...].astype(BF)
    squares[...] = acc


def split_kernel(pos, down, keep, send):
    yl = pos[2]
    mine = pl.ds(pl.multiple_of(pos[8] * 256, 256), 256)
    for b in range(16):
        keep[:, b * 128:(b + 1) * 128] = down[:, pl.ds(pl.multiple_of((2 * b + yl) * 128, 128), 128)]
        send[:, b * 128:(b + 1) * 128] = down[mine, pl.ds(pl.multiple_of((2 * b + 1 - yl) * 128, 128), 128)]


def join_kernel(pos, mine, theirs, out):
    out[pl.ds(pl.multiple_of(pos[8] * 256, 256), 256), :] = mine[...]
    out[pl.ds(pl.multiple_of((1 - pos[8]) * 256, 256), 256), :] = theirs[...]


def front_kernel(pos, *refs):
    gate_w, up_w = refs[7:9]
    rows = refs[9:13]
    feats, slope, tangent, pushed_a, pushed_b = refs[13:]
    for col, block in blocks(pos, refs[:7], 256):
        feats[:, pl.ds(col, 256)] = block
    gate = nn(feats[...], gate_w[...])
    sigma = 1.0 / (1.0 + jnp.exp(-gate))
    slope[...] = sigma * (1.0 + gate * (1.0 - sigma)) * nn(feats[...], up_w[...])
    acc = jnp.zeros(tangent.shape, F32)
    for k in range(4):
        cols = pl.multiple_of(pos[4 + k] * 1024, 1024)
        acc = acc + nn(feats[:, pl.ds(cols, 1024)], rows[k][...])
    tangent[...] = acc
    pushed_a[...] = (slope[:256] * acc[:256]).astype(BF)
    pushed_b[...] = (slope[256:] * acc[256:]).astype(BF)


def push_kernel(pos, own_a, own_b, other_a, other_b, keep, recv, row0, row1, row3, f0, f1, f2, f3, strip):
    x, z = pos[0], pos[1]
    extra = None
    if own_b.shape[0] > 256:
        extra = digits(undigit(own_b[256:].astype(F32) + other_b[256:].astype(F32)), 512)[:, :128]

    def put(out, block):
        out[:512] = block
        if extra is not None:
            out[512:] = extra

    for i, f in enumerate((f0, f1, f2, f3)):
        cols = pl.ds(pl.multiple_of(lax.rem(x + i, 4) * 512, 512), 512)
        strip[:256] = (nn(own_a[...], keep[:, cols]) + nn(other_a[...], recv[:, cols])).astype(BF)
        strip[256:] = (nn(own_b[:256], keep[:, cols]) + nn(other_b[:256], recv[:, cols])).astype(BF)
        for j, out in enumerate((row0.at[i], row1.at[i], f, row3.at[i])):
            put(out, strip[:, pl.ds(pl.multiple_of(lax.rem(z + j, 4) * 128, 128), 128)])


def weigh_first_kernel(b0, b1, b2, b3, b4, curvature, moved, weighted):
    acc, _ = add_up(b0[...], b1[...], b2[...], b3[...], b4[...])
    moved[...] = acc
    weighted[...] = (curvature[...] * acc / TOKENS).astype(BF)


def weigh_second_kernel(b0, b1, b2, b3, b4, curvature, moved, weighted, scalars):
    acc, (ss, sw, dd) = add_up(b0[...], b1[...], b2[...], b3[...], b4[...])
    alpha = sw / (ss + EPS)
    scale = lax.rsqrt(dd + 1e-30) * (1.0 / 1024.0)
    weighted[...] = (curvature[...] * ((acc - alpha * moved[...]) * scale) / TOKENS).astype(BF)
    scalars[...] = row_of([ss, sw, scale], 8, 128)


def back_kernel(pos, *refs):
    recv, full, send_a, send_b = refs[7:]
    for col, block in blocks(pos, refs[:7], 128):
        full[:, pl.ds(col, 128)] = block
    send = nt(full[...], recv[...]).astype(BF)
    send_a[...] = send[:256]
    send_b[...] = send[256:]


def own_back_kernel(full, keep, out):
    out[...] = nt(full[...], keep[...])


def delta_first_kernel(own, got_a, got_b, slope, tangent, squares, out):
    out[:256, :] = ((own[:256] + got_a[...].astype(F32)) * slope[:256]).astype(BF)
    out[256:512, :] = ((own[256:] + got_b[...].astype(F32)) * slope[256:]).astype(BF)
    delta = out[:512, :].astype(F32)
    sums = [total(squares[...]), total(tangent[...] * delta), total(delta * (delta * 1.0))]
    out[512:, :] = digits([jnp.broadcast_to(v, (1, 512)) for v in sums], 512)


def delta_second_kernel(own, got_a, got_b, slope, tan_start, tan_image, delta_one, out, sums):
    out[:256, :] = ((own[:256] + got_a[...].astype(F32)) * slope[:256]).astype(BF)
    out[256:, :] = ((own[256:] + got_b[...].astype(F32)) * slope[256:]).astype(BF)
    delta = out[...].astype(F32)
    ww = total(tan_image[...] * delta_one[:512].astype(F32))
    sums[...] = row_of([ww, total(tan_start[...] * delta), total(tan_image[...] * delta)], 8, 128)


def own_gram_kernel(feats, out):
    out[...] = nt(feats[...], feats[...])


def core_gram_kernel(feats, one, out):
    out[...] = nt(feats[...], one[...])


def far_gram_kernel(feats, one, two, out):
    out[:, :128] = nt(feats[...], one[...])
    out[:, 128:] = nt(feats[...], two[...])


def rows_kernel(pos, feats, out):
    out[...] = feats[:, pl.ds(pl.multiple_of(pos[3] * 1024, 1024), 1024)].T


def far_rows_kernel(pos, feats, out, other):
    c = pos[8]
    out[...] = feats[:, pl.ds(pl.multiple_of(c * 1024, 1024), 1024)].T
    other[...] = feats[:, pl.ds(pl.multiple_of((1 - c) * 1024, 1024), 1024)].T


def gram_split_kernel(pos, own, core, p0, p1, p2, p3, high, low):
    def put(cols, v):
        top = v.astype(BF)
        high[:, cols] = top
        low[:, cols] = (v - top.astype(F32)).astype(BF)

    put(slice(0, 512), own[...])
    put(slice(512, 1024), core[...])
    for i, p in enumerate((p0, p1, p2, p3)):
        q = lax.rem(pos[9] + i, 4) * 128
        put(pl.ds(pl.multiple_of(1024 + q, 128), 128), p[:, :128])
        put(pl.ds(pl.multiple_of(1536 + q, 128), 128), p[:, 128:])


def near_tangent_kernel(high, low, d0, d1, out):
    acc = nn(high[:, :512], d0[:512]) + nn(low[:, :512], d0[:512])
    out[...] = acc + nn(high[:, 512:1024], d1[:512]) + nn(low[:, 512:1024], d1[:512])


def far_tangent_kernel(near, high, low, d0, d1, d2, d3, slope, tangent, pushed_a, pushed_b):
    acc = near[...] + nn(high[:, 1024:1536], d2[:512]) + nn(low[:, 1024:1536], d2[:512])
    acc = acc + nn(high[:, 1536:], d3[:512]) + nn(low[:, 1536:], d3[:512])
    tangent[...] = acc
    pushed_a[...] = (slope[:256] * acc[:256]).astype(BF)
    pushed_b[:256, :] = (slope[256:] * acc[256:]).astype(BF)
    rows = d0[512:].astype(F32) + d1[512:].astype(F32) + d2[512:].astype(F32) + d3[512:].astype(F32)
    pushed_b[256:, :] = digits(undigit(rows), 512)


def near_image_kernel(r0, r1, d0, d1, out):
    out[...] = nn(r0[...], d0[:512]) + nn(r1[...], d1[:512])


def far_image_kernel(near, r2, r3, d2, d3, out):
    out[...] = near[...] + nn(r2[...], d2[:512]) + nn(r3[...], d3[:512])


def last_image_kernel(near, r2, r3, d2, d3, sums, out, block):
    acc = near[...] + nn(r2[...], d2[...]) + nn(r3[...], d3[...])
    out[...] = acc
    index = lax.broadcasted_iota(jnp.int32, (8, 128), 0)
    block[...] = jnp.where(index == 3, jnp.broadcast_to(total(acc * acc), (8, 128)), sums[...])


def final_kernel(got, scalars, start, image_one, image_two, out, coefficients):
    acc = got[0]
    for i in range(1, 128):
        acc = acc + got[i]
    ss, sw, scale = scalars[0:1], scalars[1:2], scalars[2:3]
    ww, uz, wz, zz = acc[0:1], acc[1:2], acc[2:3], acc[3:4]
    norm_sq = ss + EPS
    norm = jnp.sqrt(norm_sq)
    alpha_one = sw / norm_sq
    one_one = ss / norm_sq
    resid_sq = jnp.maximum(ww / norm_sq - alpha_one * alpha_one * (2.0 - one_one), 0.0)
    beta_one = jnp.sqrt(resid_sq + EPS)
    second = 1.0 / (norm * beta_one)
    image = second / scale
    alpha_two = image * second * (wz - alpha_one * uz)
    cross = image * uz / norm
    two_two = resid_sq / (resid_sq + EPS)
    one_two = alpha_one * (1.0 - one_one) / beta_one
    last_sq = (
        image * image * zz
        - alpha_two * alpha_two * (2.0 - two_two)
        - cross * cross * (2.0 - one_one)
        + 2.0 * alpha_two * cross * one_two
    )
    beta_two = jnp.sqrt(jnp.maximum(last_sq, 0.0) + EPS)
    index = lax.broadcasted_iota(jnp.int32, (1, 128), 1)
    row = jnp.zeros((1, 128), F32)
    for i, v in enumerate((alpha_one, beta_one, alpha_two, beta_two)):
        row = jnp.where(index == i, v, row)
    coefficients[...] = row
    f_two = image / beta_two
    f_one = -alpha_two * second / beta_two
    f_start = (alpha_two * alpha_one / beta_one - cross) / (norm * beta_two)
    for k in range(4):
        cols = slice(k * 128, (k + 1) * 128)
        out[:, cols] = f_two * image_two[:, cols] + f_one * image_one[:, cols] + f_start * start[:, cols]


def over_dp(v):
    far = shift(v, "yh", 1)
    return [v, shift(v, "c", 1), far, shift(far, "c", 1)]


def shards(tokens, gate_weight, up_weight, down_weight, curvature, start):
    yh, c, x, z, yl = [lax.axis_index(n).astype(jnp.int32) for n in NAMES]
    dp = yh * 2 + c
    quarter_of = lax.rem(x + 2 * z, 4)
    pos = jnp.stack(
        [x, z, yl, dp, dp, yh * 2 + 1 - c, (1 - yh) * 2 + c, (1 - yh) * 2 + 1 - c, c, quarter_of]
    )

    other = shift(tokens, "yl", 1)
    start_b, squares = call(cast_kernel, "cast_start", [((1024, 512), BF), ((8, 512), F32)], start)
    keep, send = call(
        split_kernel,
        "split_down",
        [((512, 2048), BF), ((256, 2048), BF)],
        pos, down_weight,
    )
    start_c = shift(start_b, "c", 1)
    other, start_c, send = lax.optimization_barrier((other, start_c, send))
    pair = jnp.where(
        yl == 0, jnp.concatenate([tokens, other], axis=1), jnp.concatenate([other, tokens], axis=1)
    )
    pieces, (recv, start_b) = gather(pair, (from_y(send), start_b))
    far_start = shift(start_b, "yh", 1)
    starts = [start_b, start_c, far_start, shift(far_start, "c", 1)]
    feats, slope, tan_start, *pushed = call(
        front_kernel,
        "front",
        [((512, D), BF), ((512, 512), F32), ((512, 512), F32), ((256, 512), BF), ((256, 512), BF)],
        pos, *pieces, gate_weight, up_weight, *starts,
        mib=24,
    )
    recv = call(join_kernel, "join", [((512, 2048), BF)], pos, recv, shift(recv, "c", 1))
    row, block = (4, 512, 128), (512, 128)

    other = [shift(v, "yl", 1) for v in pushed]
    feats_c = shift(after(feats, recv), "c", 1)
    own_gram = call(own_gram_kernel, "own_gram", [((512, 512), F32)], after(feats, pushed))
    other, own_gram, feats_c = lax.optimization_barrier((other, own_gram, feats_c))
    parts = call(
        push_kernel,
        "push",
        [(row, BF)] * 3 + [(block, BF)] * 4,
        pos, *pushed, *other, keep, recv,
        scratch=[((512, 512), BF)],
    )
    quarter = lax.dynamic_slice_in_dim(feats, quarter_of * 128, 128, axis=0)
    parts, quarter = scatter(parts, quarter)
    quarter = shift(quarter, "yh", 1)
    quarter_c = shift(quarter, "c", 1)
    moved, weighted = call(
        weigh_first_kernel, "weigh", [((512, 128), F32), ((512, 128), BF)], *parts, curvature
    )
    pieces, (quarter, quarter_c) = gather(weighted, (quarter, quarter_c))
    far_gram = call(far_gram_kernel, "far_gram", [((512, 256), F32)], feats, quarter, quarter_c)
    recv_one, far_gram = lax.optimization_barrier((recv, far_gram))
    full, *send = call(
        back_kernel, "back_other", [((512, 2048), BF), ((256, 512), BF), ((256, 512), BF)], pos, *pieces, recv_one
    )
    got = [shift(v, "yl", 1) for v in send]
    far_gram = after(far_gram, *send)
    far_grams = [far_gram, shift(far_gram, "x", 1), shift(far_gram, "z", 1), shift(far_gram, "x", 3)]
    own = call(own_back_kernel, "back_own", [((512, 512), F32)], full, keep)
    got, far_grams = lax.optimization_barrier((got, far_grams))
    delta = call(delta_first_kernel, "delta", [((528, 512), BF)], own, *got, slope, tan_start, squares)
    deltas = over_dp(delta)
    core_gram = call(core_gram_kernel, "core_gram", [((512, 512), F32)], after(feats, delta), feats_c)
    high, low = call(
        gram_split_kernel,
        "gram_split",
        [((512, 2048), BF)] * 2,
        pos, after(own_gram, delta), core_gram, *far_grams,
    )
    near = call(near_tangent_kernel, "near_tangent", [((512, 512), F32)], high, low, *deltas[:2])
    deltas, near = lax.optimization_barrier((deltas, near))
    tan_image, *pushed = call(
        far_tangent_kernel,
        "far_tangent",
        [((512, 512), F32), ((256, 512), BF), ((272, 512), BF)],
        near, high, low, *deltas, slope,
    )

    row, block = (4, 528, 128), (528, 128)
    other = [shift(v, "yl", 1) for v in pushed]
    first_deltas = deltas
    rows = [call(rows_kernel, "rows", [((1024, 512), BF)], pos, after(f, *pushed)) for f in (feats, feats_c)]
    near_one = call(near_image_kernel, "near_image", [((1024, 512), F32)], *rows, *first_deltas[:2])
    other, near_one = lax.optimization_barrier((other, near_one))
    parts = call(
        push_kernel,
        "push",
        [(row, BF)] * 3 + [(block, BF)] * 4,
        pos, *pushed, *other, keep, recv,
        scratch=[((512, 512), BF)],
    )
    theirs = lax.dynamic_slice_in_dim(feats, (1 - yh) * 2048, 2048, axis=1)
    parts, theirs = scatter(parts, theirs)
    far_rows = shift(theirs, "yh", 1)
    weighted, scalars = call(
        weigh_second_kernel, "weigh", [((512, 128), BF), ((8, 128), F32)], *parts, curvature, moved
    )
    pieces, _ = gather(weighted)
    full, *send = call(
        back_kernel, "back_other", [((512, 2048), BF), ((256, 512), BF), ((256, 512), BF)], pos, *pieces, recv
    )
    got = [shift(v, "yl", 1) for v in send]
    own = call(own_back_kernel, "back_own", [((512, 512), F32)], full, keep)
    mine, theirs = call(far_rows_kernel, "far_rows", [((1024, 512), BF)] * 2, pos, after(far_rows, *send))
    got, mine, theirs = lax.optimization_barrier((got, mine, theirs))
    rows += [mine, shift(theirs, "c", 1)]
    delta, sums = call(
        delta_second_kernel,
        "delta",
        [((512, 512), BF), ((8, 128), F32)],
        own, *got, slope, tan_start, tan_image, delta,
    )
    deltas = over_dp(delta)
    image_one = call(
        far_image_kernel, "far_image", [((1024, 512), F32)], after(near_one, delta), *rows[2:], *first_deltas[2:]
    )
    near = call(near_image_kernel, "near_image", [((1024, 512), F32)], *rows[:2], *deltas[:2])
    near, image_one = lax.optimization_barrier((near, image_one))
    image_two, block = call(
        last_image_kernel, "last_image", [((1024, 512), F32), ((8, 128), F32)], near, *rows[2:], *deltas[2:], sums
    )
    got = lax.all_to_all(jnp.broadcast_to(block[None], (128, 8, 128)), NAMES, 0, 0, tiled=True)
    whole = lambda *s: pl.BlockSpec(s, lambda i: (0,) * len(s))
    band = pl.BlockSpec((256, 512), lambda i: (i, 0))
    next_vector, coefficients = pl.pallas_call(
        final_kernel,
        grid=(4,),
        out_shape=[jax.ShapeDtypeStruct((1024, 512), F32), jax.ShapeDtypeStruct((1, 128), F32)],
        in_specs=[whole(128, 8, 128), whole(8, 128), band, band, band],
        out_specs=[band, whole(1, 128)],
        compiler_params=pltpu.CompilerParams(vmem_limit_bytes=16 * MIB),
        name="final",
    )(got, scalars, start, image_one, image_two)
    return (coefficients[0, :4], next_vector)


def solution(mesh):
    inner = Mesh(mesh.devices.reshape([n for _, n in AXES]), NAMES)
    dp, fsdp = ("yh", "c"), ("x", "z", "yl")
    in_specs = (P(dp, fsdp), P(None, fsdp), P(None, fsdp), P(fsdp, None), P(dp, fsdp), P(dp, fsdp))
    out_specs = (P(), P(dp, fsdp))
    return jax.shard_map(shards, mesh=inner, in_specs=in_specs, out_specs=out_specs, check_vma=False)
```

```python
import jax
import jax.numpy as jnp
from jax import lax
from jax.experimental import pallas as pl
from jax.experimental.pallas import tpu as pltpu
from jax.sharding import Mesh
from jax.sharding import PartitionSpec as P

D = 4096
FF = 16384
EPS = 1e-06
TOKENS = 2048
SCALE_INV = 1.0 / (D * FF)
AXES = (("yh", 2), ("c", 2), ("x", 4), ("z", 4), ("yl", 2))
NAMES = tuple(name for name, _ in AXES)
SIZES = dict(AXES)
BF = jnp.bfloat16
F32 = jnp.float32
MIB = 1024 * 1024
VM = pl.BlockSpec(memory_space=pltpu.VMEM)
SM = pl.BlockSpec(memory_space=pltpu.SMEM)


def shift(value, axis, by):
    n = SIZES[axis]
    return lax.ppermute(value, axis, [((i + by) % n, i) for i in range(n)])


def from_y(v):
    pairs = []
    for y in range(4):
        for c in range(2):
            src = (y + (1 if c == 0 else 3)) % 4
            pairs.append(((src // 2 * 2 + c) * 2 + src % 2, (y // 2 * 2 + c) * 2 + y % 2))
    return lax.ppermute(v, ("yh", "c", "yl"), pairs)


def line(v, a):
    return [v, shift(v, a, 1), shift(v, a, 2), shift(v, a, 3)]


def after(value, *others):
    return lax.optimization_barrier((value, *others))[0]


def call(kernel, name, out, *operands, mib=16, scratch=()):
    specs = [SM if v.dtype == jnp.int32 else VM for v in operands]
    shapes = [jax.ShapeDtypeStruct(s, t) for s, t in out]
    got = pl.pallas_call(
        kernel,
        out_shape=shapes,
        in_specs=specs,
        out_specs=[VM] * len(shapes),
        scratch_shapes=[pltpu.VMEM(s, t) for s, t in scratch],
        compiler_params=pltpu.CompilerParams(vmem_limit_bytes=mib * MIB),
        name=name,
    )(*operands)
    return got if len(got) > 1 else got[0]


def gather(v, later=()):
    here, far, later = lax.optimization_barrier((line(v, "x"), shift(v, "z", 2), later))
    here = jnp.stack(here)
    return [here, shift(here, "z", 1), *line(far, "x"), shift(here, "z", 3)], later


def scatter(parts):
    row0, row1, row3, f0, f1, f2, f3 = parts
    up, down = shift(row1, "z", 3), shift(row3, "z", 1)
    far = [f0, shift(f1, "x", 3), shift(f2, "x", 2), shift(f3, "x", 1)]
    block = (f0.shape, BF)
    r0, r1, r2, r3, far = call(add_kernel, "add", [block] * 5, row0, up, down, *far)
    return [r0, shift(r1, "x", 3), shift(r2, "x", 2), shift(r3, "x", 1), shift(far, "z", 2)]


def add_up(*blocks):
    acc = blocks[0].astype(F32)
    for b in blocks[1:]:
        acc = acc + b.astype(F32)
    return acc[:512], undigit(acc[512:]) if acc.shape[0] > 512 else None


def add_kernel(row0, up, down, f0, f1, f2, f3, r0, r1, r2, r3, far):
    def put(out, *blocks):
        acc, sums = add_up(*blocks)
        out[:512, :] = acc.astype(BF)
        if sums is not None:
            out[512:, :] = digits(sums, 128)

    put(far, f0[...], f1[...], f2[...], f3[...])
    for i, r in enumerate((r0, r1, r2, r3)):
        put(r, row0[i], up[i], down[i])


def blocks(pos, refs, width):
    here, nxt, f0, f1, f2, f3, prev = refs
    for i, f in enumerate((f0, f1, f2, f3)):
        yield place(pos, i, 0, width), here[i]
        yield place(pos, i, 1, width), nxt[i]
        yield place(pos, i, 2, width), f[...]
        yield place(pos, i, 3, width), prev[i]


def nt(a, b):
    return lax.dot_general(a, b, (((1,), (1,)), ((), ())), preferred_element_type=F32)


def nn(a, b):
    return jnp.dot(a, b, preferred_element_type=F32)


def place(pos, i, j, width):
    return pl.multiple_of((lax.rem(pos[0] + i, 4) * 4 + lax.rem(pos[1] + j, 4)) * width, width)


def total(v):
    return jnp.sum(v, axis=(0, 1), keepdims=True) * SCALE_INV


def row_of(values, rows, width):
    index = lax.broadcasted_iota(jnp.int32, (rows, width), 0)
    out = jnp.zeros((rows, width), F32)
    for i, v in enumerate(values):
        out = jnp.where(index == i, jnp.broadcast_to(v, (rows, width)), out)
    return out


def digits(values, width):
    rows = []
    for v in values:
        for _ in range(3):
            d = v.astype(BF).astype(F32)
            rows.append(d)
            v = v - d
    return row_of(rows, 16, width).astype(BF)


def undigit(rows):
    return [rows[3 * i:3 * i + 1] + rows[3 * i + 1:3 * i + 2] + rows[3 * i + 2:3 * i + 3] for i in range(3)]


def cast_kernel(start, out, squares):
    acc = jnp.zeros((8, 512), F32)
    for i in range(0, 1024, 8):
        v = start[i:i + 8, :]
        acc = acc + v * v
    out[...] = start[...].astype(BF)
    squares[...] = acc


def split_kernel(pos, down, keep, send):
    yl = pos[2]
    mine = pl.ds(pl.multiple_of(pos[8] * 256, 256), 256)
    for b in range(16):
        keep[:, b * 128:(b + 1) * 128] = down[:, pl.ds(pl.multiple_of((2 * b + yl) * 128, 128), 128)]
        send[:, b * 128:(b + 1) * 128] = down[mine, pl.ds(pl.multiple_of((2 * b + 1 - yl) * 128, 128), 128)]


def join_kernel(pos, mine, theirs, out):
    out[pl.ds(pl.multiple_of(pos[8] * 256, 256), 256), :] = mine[...]
    out[pl.ds(pl.multiple_of((1 - pos[8]) * 256, 256), 256), :] = theirs[...]


def front_kernel(pos, *refs):
    gate_w, up_w = refs[7:9]
    rows = refs[9:13]
    feats, slope, tangent, pushed_a, pushed_b = refs[13:]
    for col, block in blocks(pos, refs[:7], 256):
        feats[:, pl.ds(col, 256)] = block
    gate = nn(feats[...], gate_w[...])
    sigma = 1.0 / (1.0 + jnp.exp(-gate))
    slope[...] = sigma * (1.0 + gate * (1.0 - sigma)) * nn(feats[...], up_w[...])
    acc = jnp.zeros(tangent.shape, F32)
    for k in range(4):
        cols = pl.multiple_of(pos[4 + k] * 1024, 1024)
        acc = acc + nn(feats[:, pl.ds(cols, 1024)], rows[k][...])
    tangent[...] = acc
    pushed_a[...] = (slope[:256] * acc[:256]).astype(BF)
    pushed_b[...] = (slope[256:] * acc[256:]).astype(BF)


def push_kernel(pos, own_a, own_b, other_a, other_b, keep, recv, row0, row1, row3, f0, f1, f2, f3, strip):
    x, z = pos[0], pos[1]
    extra = None
    if own_b.shape[0] > 256:
        extra = digits(undigit(own_b[256:].astype(F32) + other_b[256:].astype(F32)), 512)[:, :128]

    def put(out, block):
        out[:512] = block
        if extra is not None:
            out[512:] = extra

    for i, f in enumerate((f0, f1, f2, f3)):
        cols = pl.ds(pl.multiple_of(lax.rem(x + i, 4) * 512, 512), 512)
        strip[:256] = (nn(own_a[...], keep[:, cols]) + nn(other_a[...], recv[:, cols])).astype(BF)
        strip[256:] = (nn(own_b[:256], keep[:, cols]) + nn(other_b[:256], recv[:, cols])).astype(BF)
        for j, out in enumerate((row0.at[i], row1.at[i], f, row3.at[i])):
            put(out, strip[:, pl.ds(pl.multiple_of(lax.rem(z + j, 4) * 128, 128), 128)])


def weigh_first_kernel(b0, b1, b2, b3, b4, curvature, moved, weighted):
    acc, _ = add_up(b0[...], b1[...], b2[...], b3[...], b4[...])
    moved[...] = acc
    weighted[...] = (curvature[...] * acc / TOKENS).astype(BF)


def weigh_second_kernel(b0, b1, b2, b3, b4, curvature, moved, weighted, scalars):
    acc, (ss, sw, dd) = add_up(b0[...], b1[...], b2[...], b3[...], b4[...])
    alpha = sw / (ss + EPS)
    scale = lax.rsqrt(dd + 1e-30) * (1.0 / 1024.0)
    weighted[...] = (curvature[...] * ((acc - alpha * moved[...]) * scale) / TOKENS).astype(BF)
    scalars[...] = row_of([ss, sw, scale], 8, 128)


def back_kernel(pos, *refs):
    recv, full, send_a, send_b = refs[7:]
    for col, block in blocks(pos, refs[:7], 128):
        full[:, pl.ds(col, 128)] = block
    send = nt(full[...], recv[...]).astype(BF)
    send_a[...] = send[:256]
    send_b[...] = send[256:]


def own_back_kernel(full, keep, out):
    out[...] = nt(full[...], keep[...])


def delta_first_kernel(own, got_a, got_b, slope, tangent, squares, out):
    out[:256, :] = ((own[:256] + got_a[...].astype(F32)) * slope[:256]).astype(BF)
    out[256:512, :] = ((own[256:] + got_b[...].astype(F32)) * slope[256:]).astype(BF)
    delta = out[:512, :].astype(F32)
    sums = [total(squares[...]), total(tangent[...] * delta), total(delta * (delta * 1.0))]
    out[512:, :] = digits([jnp.broadcast_to(v, (1, 512)) for v in sums], 512)


def delta_second_kernel(own, got_a, got_b, slope, tan_start, tan_image, delta_one, out, sums):
    out[:256, :] = ((own[:256] + got_a[...].astype(F32)) * slope[:256]).astype(BF)
    out[256:, :] = ((own[256:] + got_b[...].astype(F32)) * slope[256:]).astype(BF)
    delta = out[...].astype(F32)
    ww = total(tan_image[...] * delta_one[:512].astype(F32))
    sums[...] = row_of([ww, total(tan_start[...] * delta), total(tan_image[...] * delta)], 8, 128)


def own_gram_kernel(feats, out):
    out[...] = nt(feats[...], feats[...])


def core_gram_kernel(feats, one, out):
    out[...] = nt(feats[...], one[...])


def far_gram_kernel(feats, one, two, out):
    out[:, :128] = nt(feats[...], one[...])
    out[:, 128:] = nt(feats[...], two[...])


def rows_kernel(pos, feats, out):
    out[...] = feats[:, pl.ds(pl.multiple_of(pos[3] * 1024, 1024), 1024)].T


def far_rows_kernel(pos, feats, out, other):
    c = pos[8]
    out[...] = feats[:, pl.ds(pl.multiple_of(c * 1024, 1024), 1024)].T
    other[...] = feats[:, pl.ds(pl.multiple_of((1 - c) * 1024, 1024), 1024)].T


def gram_split_kernel(pos, own, core, p0, p1, p2, p3, high, low):
    def put(cols, v):
        top = v.astype(BF)
        high[:, cols] = top
        low[:, cols] = (v - top.astype(F32)).astype(BF)

    put(slice(0, 512), own[...])
    put(slice(512, 1024), core[...])
    for i, p in enumerate((p0, p1, p2, p3)):
        q = lax.rem(pos[9] + i, 4) * 128
        put(pl.ds(pl.multiple_of(1024 + q, 128), 128), p[:, :128])
        put(pl.ds(pl.multiple_of(1536 + q, 128), 128), p[:, 128:])


def near_tangent_kernel(high, low, d0, d1, out):
    acc = nn(high[:, :512], d0[:512]) + nn(low[:, :512], d0[:512])
    out[...] = acc + nn(high[:, 512:1024], d1[:512]) + nn(low[:, 512:1024], d1[:512])


def far_tangent_kernel(near, high, low, d0, d1, d2, d3, slope, tangent, pushed_a, pushed_b):
    acc = near[...] + nn(high[:, 1024:1536], d2[:512]) + nn(low[:, 1024:1536], d2[:512])
    acc = acc + nn(high[:, 1536:], d3[:512]) + nn(low[:, 1536:], d3[:512])
    tangent[...] = acc
    pushed_a[...] = (slope[:256] * acc[:256]).astype(BF)
    pushed_b[:256, :] = (slope[256:] * acc[256:]).astype(BF)
    rows = d0[512:].astype(F32) + d1[512:].astype(F32) + d2[512:].astype(F32) + d3[512:].astype(F32)
    pushed_b[256:, :] = digits(undigit(rows), 512)


def near_image_kernel(r0, r1, d0, d1, out):
    out[...] = nn(r0[...], d0[:512]) + nn(r1[...], d1[:512])


def far_image_kernel(near, r2, r3, d2, d3, out):
    out[...] = near[...] + nn(r2[...], d2[:512]) + nn(r3[...], d3[:512])


def last_image_kernel(near, r2, r3, d2, d3, sums, out, block):
    acc = near[...] + nn(r2[...], d2[...]) + nn(r3[...], d3[...])
    out[...] = acc
    index = lax.broadcasted_iota(jnp.int32, (8, 128), 0)
    block[...] = jnp.where(index == 3, jnp.broadcast_to(total(acc * acc), (8, 128)), sums[...])


def final_kernel(got, scalars, start, image_one, image_two, out, coefficients):
    acc = got[0]
    for i in range(1, 128):
        acc = acc + got[i]
    ss, sw, scale = scalars[0:1], scalars[1:2], scalars[2:3]
    ww, uz, wz, zz = acc[0:1], acc[1:2], acc[2:3], acc[3:4]
    norm_sq = ss + EPS
    norm = jnp.sqrt(norm_sq)
    alpha_one = sw / norm_sq
    one_one = ss / norm_sq
    resid_sq = jnp.maximum(ww / norm_sq - alpha_one * alpha_one * (2.0 - one_one), 0.0)
    beta_one = jnp.sqrt(resid_sq + EPS)
    second = 1.0 / (norm * beta_one)
    image = second / scale
    alpha_two = image * second * (wz - alpha_one * uz)
    cross = image * uz / norm
    two_two = resid_sq / (resid_sq + EPS)
    one_two = alpha_one * (1.0 - one_one) / beta_one
    last_sq = (
        image * image * zz
        - alpha_two * alpha_two * (2.0 - two_two)
        - cross * cross * (2.0 - one_one)
        + 2.0 * alpha_two * cross * one_two
    )
    beta_two = jnp.sqrt(jnp.maximum(last_sq, 0.0) + EPS)
    index = lax.broadcasted_iota(jnp.int32, (1, 128), 1)
    row = jnp.zeros((1, 128), F32)
    for i, v in enumerate((alpha_one, beta_one, alpha_two, beta_two)):
        row = jnp.where(index == i, v, row)
    coefficients[...] = row
    f_two = image / beta_two
    f_one = -alpha_two * second / beta_two
    f_start = (alpha_two * alpha_one / beta_one - cross) / (norm * beta_two)
    for k in range(4):
        cols = slice(k * 128, (k + 1) * 128)
        out[:, cols] = f_two * image_two[:, cols] + f_one * image_one[:, cols] + f_start * start[:, cols]


def shards(tokens, gate_weight, up_weight, down_weight, curvature, start):
    yh, c, x, z, yl = [lax.axis_index(n).astype(jnp.int32) for n in NAMES]
    dp = yh * 2 + c
    quarter_of = lax.rem(x + 2 * z, 4)
    pos = jnp.stack(
        [x, z, yl, dp, dp, yh * 2 + 1 - c, (1 - yh) * 2 + c, (1 - yh) * 2 + 1 - c, c, quarter_of]
    )

    other = shift(tokens, "yl", 1)
    start_b, squares = call(cast_kernel, "cast_start", [((1024, 512), BF), ((8, 512), F32)], start)
    other, start_b = lax.optimization_barrier((other, start_b))
    far_start = shift(start_b, "yh", 1)
    starts = [start_b, shift(start_b, "c", 1), far_start, shift(far_start, "c", 1)]
    pair = jnp.where(
        yl == 0, jnp.concatenate([tokens, other], axis=1), jnp.concatenate([other, tokens], axis=1)
    )
    keep, send = call(
        split_kernel,
        "split_down",
        [((512, 2048), BF), ((256, 2048), BF)],
        pos, after(down_weight, pair),
    )
    pieces, send = gather(pair, send)
    recv = from_y(send)
    recv, pieces = lax.optimization_barrier((recv, pieces))
    feats, slope, tan_start, *pushed = call(
        front_kernel,
        "front",
        [((512, D), BF), ((512, 512), F32), ((512, 512), F32), ((256, 512), BF), ((256, 512), BF)],
        pos, *pieces, gate_weight, up_weight, *starts,
        mib=24,
    )
    recv = call(join_kernel, "join", [((512, 2048), BF)], pos, recv, shift(recv, "c", 1))
    row, block = (4, 512, 128), (512, 128)

    other = [shift(v, "yl", 1) for v in pushed]
    feats_c = shift(after(feats, recv), "c", 1)
    own_gram = call(own_gram_kernel, "own_gram", [((512, 512), F32)], after(feats, pushed))
    other, own_gram, feats_c = lax.optimization_barrier((other, own_gram, feats_c))
    parts = call(
        push_kernel,
        "push",
        [(row, BF)] * 3 + [(block, BF)] * 4,
        pos, *pushed, *other, keep, recv,
        scratch=[((512, 512), BF)],
    )
    quarter = lax.dynamic_slice_in_dim(feats, quarter_of * 128, 128, axis=0)
    quarter = shift(after(quarter, parts[0]), "yh", 1)
    parts = scatter(parts)
    moved, weighted = call(
        weigh_first_kernel, "weigh", [((512, 128), F32), ((512, 128), BF)], *parts, curvature
    )
    quarter, weighted = lax.optimization_barrier((quarter, weighted))
    pieces, quarter_c = gather(weighted, shift(quarter, "c", 1))
    far_gram = call(far_gram_kernel, "far_gram", [((512, 256), F32)], feats, quarter, quarter_c)
    recv_one, far_gram = lax.optimization_barrier((recv, far_gram))
    full, *send = call(
        back_kernel, "back_other", [((512, 2048), BF), ((256, 512), BF), ((256, 512), BF)], pos, *pieces, recv_one
    )
    got = [shift(v, "yl", 1) for v in send]
    far_gram = after(far_gram, *send)
    far_grams = [far_gram, shift(far_gram, "x", 1), shift(far_gram, "z", 1), shift(far_gram, "x", 3)]
    own = call(own_back_kernel, "back_own", [((512, 512), F32)], full, keep)
    got, far_grams = lax.optimization_barrier((got, far_grams))
    delta = call(delta_first_kernel, "delta", [((528, 512), BF)], own, *got, slope, tan_start, squares)
    deltas = [delta, shift(delta, "c", 1)]
    far_delta = shift(delta, "yh", 1)
    core_gram = call(core_gram_kernel, "core_gram", [((512, 512), F32)], after(feats, delta), feats_c)
    high, low = call(
        gram_split_kernel,
        "gram_split",
        [((512, 2048), BF)] * 2,
        pos, after(own_gram, delta), core_gram, *far_grams,
    )
    near = call(near_tangent_kernel, "near_tangent", [((512, 512), F32)], high, low, *deltas)
    far_delta, near = lax.optimization_barrier((far_delta, near))
    deltas += [far_delta, shift(far_delta, "c", 1)]
    tan_image, *pushed = call(
        far_tangent_kernel,
        "far_tangent",
        [((512, 512), F32), ((256, 512), BF), ((272, 512), BF)],
        near, high, low, *deltas, slope,
    )

    row, block = (4, 528, 128), (528, 128)
    other = [shift(v, "yl", 1) for v in pushed]
    first_deltas = deltas
    rows = [call(rows_kernel, "rows", [((1024, 512), BF)], pos, after(f, *pushed)) for f in (feats, feats_c)]
    near_one = call(near_image_kernel, "near_image", [((1024, 512), F32)], *rows, *first_deltas[:2])
    other, near_one = lax.optimization_barrier((other, near_one))
    parts = call(
        push_kernel,
        "push",
        [(row, BF)] * 3 + [(block, BF)] * 4,
        pos, *pushed, *other, keep, recv,
        scratch=[((512, 512), BF)],
    )
    theirs = lax.dynamic_slice_in_dim(feats, (1 - yh) * 2048, 2048, axis=1)
    far_rows = shift(after(theirs, parts[0]), "yh", 1)
    parts = scatter(parts)
    weighted, scalars = call(
        weigh_second_kernel, "weigh", [((512, 128), BF), ((8, 128), F32)], *parts, curvature, moved
    )
    pieces, _ = gather(weighted)
    full, *send = call(
        back_kernel, "back_other", [((512, 2048), BF), ((256, 512), BF), ((256, 512), BF)], pos, *pieces, recv
    )
    got = [shift(v, "yl", 1) for v in send]
    own = call(own_back_kernel, "back_own", [((512, 512), F32)], full, keep)
    mine, theirs = call(far_rows_kernel, "far_rows", [((1024, 512), BF)] * 2, pos, after(far_rows, *send))
    got, mine, theirs = lax.optimization_barrier((got, mine, theirs))
    rows += [mine, shift(theirs, "c", 1)]
    delta, sums = call(
        delta_second_kernel,
        "delta",
        [((512, 512), BF), ((8, 128), F32)],
        own, *got, slope, tan_start, tan_image, delta,
    )
    deltas = [delta, shift(delta, "c", 1)]
    far_delta = shift(delta, "yh", 1)
    image_one = call(
        far_image_kernel, "far_image", [((1024, 512), F32)], after(near_one, delta), *rows[2:], *first_deltas[2:]
    )
    near = call(near_image_kernel, "near_image", [((1024, 512), F32)], *rows[:2], *deltas)
    far_delta, near, image_one = lax.optimization_barrier((far_delta, near, image_one))
    deltas += [far_delta, shift(far_delta, "c", 1)]
    image_two, block = call(
        last_image_kernel, "last_image", [((1024, 512), F32), ((8, 128), F32)], near, *rows[2:], *deltas[2:], sums
    )
    got = lax.all_to_all(jnp.broadcast_to(block[None], (128, 8, 128)), NAMES, 0, 0, tiled=True)
    whole = lambda *s: pl.BlockSpec(s, lambda i: (0,) * len(s))
    band = pl.BlockSpec((256, 512), lambda i: (i, 0))
    next_vector, coefficients = pl.pallas_call(
        final_kernel,
        grid=(4,),
        out_shape=[jax.ShapeDtypeStruct((1024, 512), F32), jax.ShapeDtypeStruct((1, 128), F32)],
        in_specs=[whole(128, 8, 128), whole(8, 128), band, band, band],
        out_specs=[band, whole(1, 128)],
        compiler_params=pltpu.CompilerParams(vmem_limit_bytes=16 * MIB),
        name="final",
    )(got, scalars, start, image_one, image_two)
    return (coefficients[0, :4], next_vector)


def solution(mesh):
    inner = Mesh(mesh.devices.reshape([n for _, n in AXES]), NAMES)
    dp, fsdp = ("yh", "c"), ("x", "z", "yl")
    in_specs = (P(dp, fsdp), P(None, fsdp), P(None, fsdp), P(fsdp, None), P(dp, fsdp), P(dp, fsdp))
    out_specs = (P(), P(dp, fsdp))
    return jax.shard_map(shards, mesh=inner, in_specs=in_specs, out_specs=out_specs, check_vma=False)
```

```python
import jax
import jax.numpy as jnp
from jax import lax
from jax.experimental import pallas as pl
from jax.experimental.pallas import tpu as pltpu
from jax.sharding import Mesh
from jax.sharding import PartitionSpec as P

D = 4096
FF = 16384
EPS = 1e-06
TOKENS = 2048
SCALE_INV = 1.0 / (D * FF)
AXES = (("yh", 2), ("c", 2), ("x", 4), ("z", 4), ("yl", 2))
NAMES = tuple(name for name, _ in AXES)
SIZES = dict(AXES)
BF = jnp.bfloat16
F32 = jnp.float32
MIB = 1024 * 1024
VM = pl.BlockSpec(memory_space=pltpu.VMEM)
SM = pl.BlockSpec(memory_space=pltpu.SMEM)


def shift(value, axis, by):
    n = SIZES[axis]
    return lax.ppermute(value, axis, [((i + by) % n, i) for i in range(n)])


def from_y(v):
    pairs = []
    for y in range(4):
        for c in range(2):
            src = (y + (1 if c == 0 else 3)) % 4
            pairs.append(((src // 2 * 2 + c) * 2 + src % 2, (y // 2 * 2 + c) * 2 + y % 2))
    return lax.ppermute(v, ("yh", "c", "yl"), pairs)


def line(v, a):
    return [v, shift(v, a, 1), shift(v, a, 2), shift(v, a, 3)]


def after(value, *others):
    return lax.optimization_barrier((value, *others))[0]


def call(kernel, name, out, *operands, mib=16, scratch=()):
    specs = [SM if v.dtype == jnp.int32 else VM for v in operands]
    shapes = [jax.ShapeDtypeStruct(s, t) for s, t in out]
    got = pl.pallas_call(
        kernel,
        out_shape=shapes,
        in_specs=specs,
        out_specs=[VM] * len(shapes),
        scratch_shapes=[pltpu.VMEM(s, t) for s, t in scratch],
        compiler_params=pltpu.CompilerParams(vmem_limit_bytes=mib * MIB),
        name=name,
    )(*operands)
    return got if len(got) > 1 else got[0]


def gather(v, later=()):
    here, far, later = lax.optimization_barrier((line(v, "x"), shift(v, "z", 2), later))
    here = jnp.stack(here)
    return [here, shift(here, "z", 1), *line(far, "x"), shift(here, "z", 3)], later


def scatter(parts):
    row0, row1, row3, f0, f1, f2, f3 = parts
    up, down = shift(row1, "z", 3), shift(row3, "z", 1)
    far = [f0, shift(f1, "x", 3), shift(f2, "x", 2), shift(f3, "x", 1)]
    block = (f0.shape, BF)
    r0, r1, r2, r3, far = call(add_kernel, "add", [block] * 5, row0, up, down, *far)
    return [r0, shift(r1, "x", 3), shift(r2, "x", 2), shift(r3, "x", 1), shift(far, "z", 2)]


def add_up(*blocks):
    acc = blocks[0].astype(F32)
    for b in blocks[1:]:
        acc = acc + b.astype(F32)
    return acc[:512], undigit(acc[512:]) if acc.shape[0] > 512 else None


def add_kernel(row0, up, down, f0, f1, f2, f3, r0, r1, r2, r3, far):
    def put(out, *blocks):
        acc, sums = add_up(*blocks)
        out[:512, :] = acc.astype(BF)
        if sums is not None:
            out[512:, :] = digits(sums, 128)

    put(far, f0[...], f1[...], f2[...], f3[...])
    for i, r in enumerate((r0, r1, r2, r3)):
        put(r, row0[i], up[i], down[i])


def blocks(pos, refs, width):
    here, nxt, f0, f1, f2, f3, prev = refs
    for i, f in enumerate((f0, f1, f2, f3)):
        yield place(pos, i, 0, width), here[i]
        yield place(pos, i, 1, width), nxt[i]
        yield place(pos, i, 2, width), f[...]
        yield place(pos, i, 3, width), prev[i]


def nt(a, b):
    return lax.dot_general(a, b, (((1,), (1,)), ((), ())), preferred_element_type=F32)


def nn(a, b):
    return jnp.dot(a, b, preferred_element_type=F32)


def place(pos, i, j, width):
    return pl.multiple_of((lax.rem(pos[0] + i, 4) * 4 + lax.rem(pos[1] + j, 4)) * width, width)


def total(v):
    return jnp.sum(v, axis=(0, 1), keepdims=True) * SCALE_INV


def row_of(values, rows, width):
    index = lax.broadcasted_iota(jnp.int32, (rows, width), 0)
    out = jnp.zeros((rows, width), F32)
    for i, v in enumerate(values):
        out = jnp.where(index == i, jnp.broadcast_to(v, (rows, width)), out)
    return out


def digits(values, width):
    rows = []
    for v in values:
        for _ in range(3):
            d = v.astype(BF).astype(F32)
            rows.append(d)
            v = v - d
    return row_of(rows, 16, width).astype(BF)


def undigit(rows):
    return [rows[3 * i:3 * i + 1] + rows[3 * i + 1:3 * i + 2] + rows[3 * i + 2:3 * i + 3] for i in range(3)]


def cast_kernel(start, out, squares):
    acc = jnp.zeros((8, 512), F32)
    for i in range(0, 1024, 8):
        v = start[i:i + 8, :]
        acc = acc + v * v
    out[...] = start[...].astype(BF)
    squares[...] = acc


def split_kernel(pos, down, keep, send):
    yl = pos[2]
    mine = pl.ds(pl.multiple_of(pos[8] * 256, 256), 256)
    for b in range(16):
        keep[:, b * 128:(b + 1) * 128] = down[:, pl.ds(pl.multiple_of((2 * b + yl) * 128, 128), 128)]
        send[:, b * 128:(b + 1) * 128] = down[mine, pl.ds(pl.multiple_of((2 * b + 1 - yl) * 128, 128), 128)]


def join_kernel(pos, mine, theirs, out):
    out[pl.ds(pl.multiple_of(pos[8] * 256, 256), 256), :] = mine[...]
    out[pl.ds(pl.multiple_of((1 - pos[8]) * 256, 256), 256), :] = theirs[...]


def front_kernel(pos, *refs):
    gate_w, up_w = refs[7:9]
    rows = refs[9:13]
    feats, slope, tangent, pushed_a, pushed_b = refs[13:]
    for col, block in blocks(pos, refs[:7], 256):
        feats[:, pl.ds(col, 256)] = block
    gate = nn(feats[...], gate_w[...])
    sigma = 1.0 / (1.0 + jnp.exp(-gate))
    slope[...] = sigma * (1.0 + gate * (1.0 - sigma)) * nn(feats[...], up_w[...])
    acc = jnp.zeros(tangent.shape, F32)
    for k in range(4):
        cols = pl.multiple_of(pos[4 + k] * 1024, 1024)
        acc = acc + nn(feats[:, pl.ds(cols, 1024)], rows[k][...])
    tangent[...] = acc
    pushed_a[...] = (slope[:256] * acc[:256]).astype(BF)
    pushed_b[...] = (slope[256:] * acc[256:]).astype(BF)


def push_kernel(pos, own_a, own_b, other_a, other_b, keep, recv, row0, row1, row3, f0, f1, f2, f3, strip):
    x, z = pos[0], pos[1]
    extra = None
    if own_b.shape[0] > 256:
        extra = digits(undigit(own_b[256:].astype(F32) + other_b[256:].astype(F32)), 512)[:, :128]

    def put(out, block):
        out[:512] = block
        if extra is not None:
            out[512:] = extra

    for i, f in enumerate((f0, f1, f2, f3)):
        cols = pl.ds(pl.multiple_of(lax.rem(x + i, 4) * 512, 512), 512)
        strip[:256] = (nn(own_a[...], keep[:, cols]) + nn(other_a[...], recv[:, cols])).astype(BF)
        strip[256:] = (nn(own_b[:256], keep[:, cols]) + nn(other_b[:256], recv[:, cols])).astype(BF)
        for j, out in enumerate((row0.at[i], row1.at[i], f, row3.at[i])):
            put(out, strip[:, pl.ds(pl.multiple_of(lax.rem(z + j, 4) * 128, 128), 128)])


def weigh_first_kernel(b0, b1, b2, b3, b4, curvature, moved, weighted):
    acc, _ = add_up(b0[...], b1[...], b2[...], b3[...], b4[...])
    moved[...] = acc
    weighted[...] = (curvature[...] * acc / TOKENS).astype(BF)


def weigh_second_kernel(b0, b1, b2, b3, b4, curvature, moved, weighted, scalars):
    acc, (ss, sw, dd) = add_up(b0[...], b1[...], b2[...], b3[...], b4[...])
    alpha = sw / (ss + EPS)
    scale = lax.rsqrt(dd + 1e-30) * (1.0 / 1024.0)
    weighted[...] = (curvature[...] * ((acc - alpha * moved[...]) * scale) / TOKENS).astype(BF)
    scalars[...] = row_of([ss, sw, scale], 8, 128)


def back_kernel(pos, *refs):
    recv, full, send_a, send_b = refs[7:]
    for col, block in blocks(pos, refs[:7], 128):
        full[:, pl.ds(col, 128)] = block
    send = nt(full[...], recv[...]).astype(BF)
    send_a[...] = send[:256]
    send_b[...] = send[256:]


def own_back_kernel(full, keep, out):
    out[...] = nt(full[...], keep[...])


def delta_first_kernel(own, got_a, got_b, slope, tangent, squares, out):
    out[:256, :] = ((own[:256] + got_a[...].astype(F32)) * slope[:256]).astype(BF)
    out[256:512, :] = ((own[256:] + got_b[...].astype(F32)) * slope[256:]).astype(BF)
    delta = out[:512, :].astype(F32)
    sums = [total(squares[...]), total(tangent[...] * delta), total(delta * (delta * 1.0))]
    out[512:, :] = digits([jnp.broadcast_to(v, (1, 512)) for v in sums], 512)


def delta_second_kernel(own, got_a, got_b, slope, tan_start, tan_image, delta_one, out, sums):
    out[:256, :] = ((own[:256] + got_a[...].astype(F32)) * slope[:256]).astype(BF)
    out[256:, :] = ((own[256:] + got_b[...].astype(F32)) * slope[256:]).astype(BF)
    delta = out[...].astype(F32)
    ww = total(tan_image[...] * delta_one[:512].astype(F32))
    sums[...] = row_of([ww, total(tan_start[...] * delta), total(tan_image[...] * delta)], 8, 128)


def own_gram_kernel(feats, out):
    out[...] = nt(feats[...], feats[...])


def core_gram_kernel(feats, one, out):
    out[...] = nt(feats[...], one[...])


def far_gram_kernel(pos, feats, quarters, out):
    out[:, :128] = nt(feats[...], quarters[pos[6]])
    out[:, 128:] = nt(feats[...], quarters[pos[7]])


def rows_kernel(pos, feats, out):
    out[...] = feats[:, pl.ds(pl.multiple_of(pos[3] * 1024, 1024), 1024)].T


def far_rows_kernel(pos, feats, out, other):
    c, yh = pos[8], pos[10]
    out[...] = feats[1 - yh, :, pl.ds(pl.multiple_of(c * 1024, 1024), 1024)].T
    other[...] = feats[1 - yh, :, pl.ds(pl.multiple_of((1 - c) * 1024, 1024), 1024)].T


def gram_split_kernel(pos, own, core, p0, p1, p2, p3, high, low):
    def put(cols, v):
        top = v.astype(BF)
        high[:, cols] = top
        low[:, cols] = (v - top.astype(F32)).astype(BF)

    put(slice(0, 512), own[...])
    put(slice(512, 1024), core[...])
    for i, p in enumerate((p0, p1, p2, p3)):
        q = lax.rem(pos[9] + i, 4) * 128
        put(pl.ds(pl.multiple_of(1024 + q, 128), 128), p[:, :128])
        put(pl.ds(pl.multiple_of(1536 + q, 128), 128), p[:, 128:])


def near_tangent_kernel(high, low, d0, d1, out):
    acc = nn(high[:, :512], d0[:512]) + nn(low[:, :512], d0[:512])
    out[...] = acc + nn(high[:, 512:1024], d1[:512]) + nn(low[:, 512:1024], d1[:512])


def far_tangent_kernel(near, high, low, d0, d1, d2, d3, slope, tangent, pushed_a, pushed_b):
    acc = near[...] + nn(high[:, 1024:1536], d2[:512]) + nn(low[:, 1024:1536], d2[:512])
    acc = acc + nn(high[:, 1536:], d3[:512]) + nn(low[:, 1536:], d3[:512])
    tangent[...] = acc
    pushed_a[...] = (slope[:256] * acc[:256]).astype(BF)
    pushed_b[:256, :] = (slope[256:] * acc[256:]).astype(BF)
    rows = d0[512:].astype(F32) + d1[512:].astype(F32) + d2[512:].astype(F32) + d3[512:].astype(F32)
    pushed_b[256:, :] = digits(undigit(rows), 512)


def near_image_kernel(r0, r1, d0, d1, out):
    out[...] = nn(r0[...], d0[:512]) + nn(r1[...], d1[:512])


def far_image_kernel(near, r2, r3, d2, d3, out):
    out[...] = near[...] + nn(r2[...], d2[:512]) + nn(r3[...], d3[:512])


def last_image_kernel(near, r2, r3, d2, d3, sums, out, block):
    acc = near[...] + nn(r2[...], d2[...]) + nn(r3[...], d3[...])
    out[...] = acc
    index = lax.broadcasted_iota(jnp.int32, (8, 128), 0)
    block[...] = jnp.where(index == 3, jnp.broadcast_to(total(acc * acc), (8, 128)), sums[...])


def final_kernel(got, scalars, start, image_one, image_two, out, coefficients):
    acc = got[0]
    for i in range(1, 128):
        acc = acc + got[i]
    ss, sw, scale = scalars[0:1], scalars[1:2], scalars[2:3]
    ww, uz, wz, zz = acc[0:1], acc[1:2], acc[2:3], acc[3:4]
    norm_sq = ss + EPS
    norm = jnp.sqrt(norm_sq)
    alpha_one = sw / norm_sq
    one_one = ss / norm_sq
    resid_sq = jnp.maximum(ww / norm_sq - alpha_one * alpha_one * (2.0 - one_one), 0.0)
    beta_one = jnp.sqrt(resid_sq + EPS)
    second = 1.0 / (norm * beta_one)
    image = second / scale
    alpha_two = image * second * (wz - alpha_one * uz)
    cross = image * uz / norm
    two_two = resid_sq / (resid_sq + EPS)
    one_two = alpha_one * (1.0 - one_one) / beta_one
    last_sq = (
        image * image * zz
        - alpha_two * alpha_two * (2.0 - two_two)
        - cross * cross * (2.0 - one_one)
        + 2.0 * alpha_two * cross * one_two
    )
    beta_two = jnp.sqrt(jnp.maximum(last_sq, 0.0) + EPS)
    index = lax.broadcasted_iota(jnp.int32, (1, 128), 1)
    row = jnp.zeros((1, 128), F32)
    for i, v in enumerate((alpha_one, beta_one, alpha_two, beta_two)):
        row = jnp.where(index == i, v, row)
    coefficients[...] = row
    f_two = image / beta_two
    f_one = -alpha_two * second / beta_two
    f_start = (alpha_two * alpha_one / beta_one - cross) / (norm * beta_two)
    for k in range(4):
        cols = slice(k * 128, (k + 1) * 128)
        out[:, cols] = f_two * image_two[:, cols] + f_one * image_one[:, cols] + f_start * start[:, cols]


def shards(tokens, gate_weight, up_weight, down_weight, curvature, start):
    yh, c, x, z, yl = [lax.axis_index(n).astype(jnp.int32) for n in NAMES]
    dp = yh * 2 + c
    quarter_of = lax.rem(x + 2 * z, 4)
    pos = jnp.stack(
        [x, z, yl, dp, dp, yh * 2 + 1 - c, (1 - yh) * 2 + c, (1 - yh) * 2 + 1 - c, c, quarter_of, yh]
    )

    other = shift(tokens, "yl", 1)
    start_b, squares = call(cast_kernel, "cast_start", [((1024, 512), BF), ((8, 512), F32)], start)
    other, start_b = lax.optimization_barrier((other, start_b))
    far_start = shift(start_b, "yh", 1)
    starts = [start_b, shift(start_b, "c", 1), far_start, shift(far_start, "c", 1)]
    pair = jnp.where(
        yl == 0, jnp.concatenate([tokens, other], axis=1), jnp.concatenate([other, tokens], axis=1)
    )
    keep, send = call(
        split_kernel,
        "split_down",
        [((512, 2048), BF), ((256, 2048), BF)],
        pos, after(down_weight, pair),
    )
    pieces, send = gather(pair, send)
    recv = from_y(send)
    recv, pieces = lax.optimization_barrier((recv, pieces))
    feats, slope, tan_start, *pushed = call(
        front_kernel,
        "front",
        [((512, D), BF), ((512, 512), F32), ((512, 512), F32), ((256, 512), BF), ((256, 512), BF)],
        pos, *pieces, gate_weight, up_weight, *starts,
        mib=24,
    )
    recv = call(join_kernel, "join", [((512, 2048), BF)], pos, recv, shift(recv, "c", 1))
    row, block = (4, 512, 128), (512, 128)

    other = [shift(v, "yl", 1) for v in pushed]
    feats_c = shift(after(feats, recv), "c", 1)
    own_gram = call(own_gram_kernel, "own_gram", [((512, 512), F32)], after(feats, pushed))
    other, own_gram, feats_c = lax.optimization_barrier((other, own_gram, feats_c))
    parts = call(
        push_kernel,
        "push",
        [(row, BF)] * 3 + [(block, BF)] * 4,
        pos, *pushed, *other, keep, recv,
        scratch=[((512, 512), BF)],
    )
    quarter = lax.dynamic_slice_in_dim(feats, quarter_of * 128, 128, axis=0)
    quarters = lax.all_gather(after(quarter, parts[0]), ("yh", "c"))
    parts = scatter(parts)
    moved, weighted = call(
        weigh_first_kernel, "weigh", [((512, 128), F32), ((512, 128), BF)], *parts, curvature
    )
    pieces, _ = gather(weighted)
    far_gram = call(
        far_gram_kernel, "far_gram", [((512, 256), F32)], pos, after(feats, pieces[0]), quarters
    )
    recv_one, far_gram = lax.optimization_barrier((recv, far_gram))
    full, *send = call(
        back_kernel, "back_other", [((512, 2048), BF), ((256, 512), BF), ((256, 512), BF)], pos, *pieces, recv_one
    )
    got = [shift(v, "yl", 1) for v in send]
    far_gram = after(far_gram, *send)
    far_grams = [far_gram, shift(far_gram, "x", 1), shift(far_gram, "z", 1), shift(far_gram, "x", 3)]
    own = call(own_back_kernel, "back_own", [((512, 512), F32)], full, keep)
    got, far_grams = lax.optimization_barrier((got, far_grams))
    delta = call(delta_first_kernel, "delta", [((528, 512), BF)], own, *got, slope, tan_start, squares)
    deltas = [delta, shift(delta, "c", 1)]
    far_delta = shift(delta, "yh", 1)
    core_gram = call(core_gram_kernel, "core_gram", [((512, 512), F32)], after(feats, delta), feats_c)
    high, low = call(
        gram_split_kernel,
        "gram_split",
        [((512, 2048), BF)] * 2,
        pos, after(own_gram, delta), core_gram, *far_grams,
    )
    near = call(near_tangent_kernel, "near_tangent", [((512, 512), F32)], high, low, *deltas)
    far_delta, near = lax.optimization_barrier((far_delta, near))
    deltas += [far_delta, shift(far_delta, "c", 1)]
    tan_image, *pushed = call(
        far_tangent_kernel,
        "far_tangent",
        [((512, 512), F32), ((256, 512), BF), ((272, 512), BF)],
        near, high, low, *deltas, slope,
    )

    row, block = (4, 528, 128), (528, 128)
    other = [shift(v, "yl", 1) for v in pushed]
    first_deltas = deltas
    rows = [call(rows_kernel, "rows", [((1024, 512), BF)], pos, after(f, *pushed)) for f in (feats, feats_c)]
    near_one = call(near_image_kernel, "near_image", [((1024, 512), F32)], *rows, *first_deltas[:2])
    other, near_one = lax.optimization_barrier((other, near_one))
    parts = call(
        push_kernel,
        "push",
        [(row, BF)] * 3 + [(block, BF)] * 4,
        pos, *pushed, *other, keep, recv,
        scratch=[((512, 512), BF)],
    )
    theirs = lax.dynamic_slice_in_dim(feats, (1 - yh) * 2048, 2048, axis=1)
    far_rows = lax.all_gather(after(theirs, parts[0]), "yh")
    parts = scatter(parts)
    weighted, scalars = call(
        weigh_second_kernel, "weigh", [((512, 128), BF), ((8, 128), F32)], *parts, curvature, moved
    )
    pieces, _ = gather(weighted)
    full, *send = call(
        back_kernel, "back_other", [((512, 2048), BF), ((256, 512), BF), ((256, 512), BF)], pos, *pieces, recv
    )
    got = [shift(v, "yl", 1) for v in send]
    own = call(own_back_kernel, "back_own", [((512, 512), F32)], full, keep)
    mine, theirs = call(far_rows_kernel, "far_rows", [((1024, 512), BF)] * 2, pos, after(far_rows, *send))
    got, mine, theirs = lax.optimization_barrier((got, mine, theirs))
    rows += [mine, shift(theirs, "c", 1)]
    delta, sums = call(
        delta_second_kernel,
        "delta",
        [((512, 512), BF), ((8, 128), F32)],
        own, *got, slope, tan_start, tan_image, delta,
    )
    deltas = [delta, shift(delta, "c", 1)]
    far_delta = shift(delta, "yh", 1)
    image_one = call(
        far_image_kernel, "far_image", [((1024, 512), F32)], after(near_one, delta), *rows[2:], *first_deltas[2:]
    )
    near = call(near_image_kernel, "near_image", [((1024, 512), F32)], *rows[:2], *deltas)
    far_delta, near, image_one = lax.optimization_barrier((far_delta, near, image_one))
    deltas += [far_delta, shift(far_delta, "c", 1)]
    image_two, block = call(
        last_image_kernel, "last_image", [((1024, 512), F32), ((8, 128), F32)], near, *rows[2:], *deltas[2:], sums
    )
    got = lax.all_to_all(jnp.broadcast_to(block[None], (128, 8, 128)), NAMES, 0, 0, tiled=True)
    whole = lambda *s: pl.BlockSpec(s, lambda i: (0,) * len(s))
    band = pl.BlockSpec((256, 512), lambda i: (i, 0))
    next_vector, coefficients = pl.pallas_call(
        final_kernel,
        grid=(4,),
        out_shape=[jax.ShapeDtypeStruct((1024, 512), F32), jax.ShapeDtypeStruct((1, 128), F32)],
        in_specs=[whole(128, 8, 128), whole(8, 128), band, band, band],
        out_specs=[band, whole(1, 128)],
        compiler_params=pltpu.CompilerParams(vmem_limit_bytes=16 * MIB),
        name="final",
    )(got, scalars, start, image_one, image_two)
    return (coefficients[0, :4], next_vector)


def solution(mesh):
    inner = Mesh(mesh.devices.reshape([n for _, n in AXES]), NAMES)
    dp, fsdp = ("yh", "c"), ("x", "z", "yl")
    in_specs = (P(dp, fsdp), P(None, fsdp), P(None, fsdp), P(fsdp, None), P(dp, fsdp), P(dp, fsdp))
    out_specs = (P(), P(dp, fsdp))
    return jax.shard_map(shards, mesh=inner, in_specs=in_specs, out_specs=out_specs, check_vma=False)
```

```python
import jax
import jax.numpy as jnp
from jax import lax
from jax.experimental import pallas as pl
from jax.experimental.pallas import tpu as pltpu
from jax.sharding import Mesh
from jax.sharding import PartitionSpec as P

D = 4096
FF = 16384
EPS = 1e-06
TOKENS = 2048
SCALE_INV = 1.0 / (D * FF)
AXES = (("yh", 2), ("c", 2), ("x", 4), ("z", 4), ("yl", 2))
NAMES = tuple(name for name, _ in AXES)
SIZES = dict(AXES)
BF = jnp.bfloat16
F32 = jnp.float32
MIB = 1024 * 1024
VM = pl.BlockSpec(memory_space=pltpu.VMEM)
SM = pl.BlockSpec(memory_space=pltpu.SMEM)


def shift(value, axis, by):
    n = SIZES[axis]
    return lax.ppermute(value, axis, [((i + by) % n, i) for i in range(n)])


def from_y(v):
    pairs = []
    for y in range(4):
        for c in range(2):
            src = (y + (1 if c == 0 else 3)) % 4
            pairs.append(((src // 2 * 2 + c) * 2 + src % 2, (y // 2 * 2 + c) * 2 + y % 2))
    return lax.ppermute(v, ("yh", "c", "yl"), pairs)


def line(v, a):
    return [v, shift(v, a, 1), shift(v, a, 2), shift(v, a, 3)]


def after(value, *others):
    return lax.optimization_barrier((value, *others))[0]


def call(kernel, name, out, *operands, mib=16, scratch=()):
    specs = [SM if v.dtype == jnp.int32 else VM for v in operands]
    shapes = [jax.ShapeDtypeStruct(s, t) for s, t in out]
    got = pl.pallas_call(
        kernel,
        out_shape=shapes,
        in_specs=specs,
        out_specs=[VM] * len(shapes),
        scratch_shapes=[pltpu.VMEM(s, t) for s, t in scratch],
        compiler_params=pltpu.CompilerParams(vmem_limit_bytes=mib * MIB),
        name=name,
    )(*operands)
    return got if len(got) > 1 else got[0]


def gather(v, later=()):
    here, far, later = lax.optimization_barrier((line(v, "x"), shift(v, "z", 2), later))
    here = jnp.stack(here)
    return [here, shift(here, "z", 1), *line(far, "x"), shift(here, "z", 3)], later


def scatter(parts):
    row0, row1, row3, f0, f1, f2, f3 = parts
    up, down = shift(row1, "z", 3), shift(row3, "z", 1)
    far = [f0, shift(f1, "x", 3), shift(f2, "x", 2), shift(f3, "x", 1)]
    block = (f0.shape, BF)
    r0, r1, r2, r3, far = call(add_kernel, "add", [block] * 5, row0, up, down, *far)
    return [r0, shift(r1, "x", 3), shift(r2, "x", 2), shift(r3, "x", 1), shift(far, "z", 2)]


def add_up(*blocks):
    acc = blocks[0].astype(F32)
    for b in blocks[1:]:
        acc = acc + b.astype(F32)
    return acc[:512], undigit(acc[512:]) if acc.shape[0] > 512 else None


def add_kernel(row0, up, down, f0, f1, f2, f3, r0, r1, r2, r3, far):
    def put(out, *blocks):
        acc, sums = add_up(*blocks)
        out[:512, :] = acc.astype(BF)
        if sums is not None:
            out[512:, :] = digits(sums, 128)

    put(far, f0[...], f1[...], f2[...], f3[...])
    for i, r in enumerate((r0, r1, r2, r3)):
        put(r, row0[i], up[i], down[i])


def blocks(pos, refs, width):
    here, nxt, f0, f1, f2, f3, prev = refs
    for i, f in enumerate((f0, f1, f2, f3)):
        yield place(pos, i, 0, width), here[i]
        yield place(pos, i, 1, width), nxt[i]
        yield place(pos, i, 2, width), f[...]
        yield place(pos, i, 3, width), prev[i]


def nt(a, b):
    return lax.dot_general(a, b, (((1,), (1,)), ((), ())), preferred_element_type=F32)


def nn(a, b):
    return jnp.dot(a, b, preferred_element_type=F32)


def place(pos, i, j, width):
    return pl.multiple_of((lax.rem(pos[0] + i, 4) * 4 + lax.rem(pos[1] + j, 4)) * width, width)


def total(v):
    return jnp.sum(v, axis=(0, 1), keepdims=True) * SCALE_INV


def row_of(values, rows, width):
    index = lax.broadcasted_iota(jnp.int32, (rows, width), 0)
    out = jnp.zeros((rows, width), F32)
    for i, v in enumerate(values):
        out = jnp.where(index == i, jnp.broadcast_to(v, (rows, width)), out)
    return out


def digits(values, width):
    rows = []
    for v in values:
        for _ in range(3):
            d = v.astype(BF).astype(F32)
            rows.append(d)
            v = v - d
    return row_of(rows, 16, width).astype(BF)


def undigit(rows):
    return [rows[3 * i:3 * i + 1] + rows[3 * i + 1:3 * i + 2] + rows[3 * i + 2:3 * i + 3] for i in range(3)]


def cast_kernel(start, out, squares):
    acc = jnp.zeros((8, 512), F32)
    for i in range(0, 1024, 8):
        v = start[i:i + 8, :]
        acc = acc + v * v
    out[...] = start[...].astype(BF)
    squares[...] = acc


def split_kernel(pos, down, keep, send):
    yl = pos[2]
    mine = pl.ds(pl.multiple_of(pos[8] * 256, 256), 256)
    for b in range(16):
        keep[:, b * 128:(b + 1) * 128] = down[:, pl.ds(pl.multiple_of((2 * b + yl) * 128, 128), 128)]
        send[:, b * 128:(b + 1) * 128] = down[mine, pl.ds(pl.multiple_of((2 * b + 1 - yl) * 128, 128), 128)]


def join_kernel(pos, mine, theirs, out):
    out[pl.ds(pl.multiple_of(pos[8] * 256, 256), 256), :] = mine[...]
    out[pl.ds(pl.multiple_of((1 - pos[8]) * 256, 256), 256), :] = theirs[...]


def front_kernel(pos, *refs):
    gate_w, up_w = refs[7:9]
    rows = refs[9:13]
    feats, slope, tangent, pushed_a, pushed_b = refs[13:]
    for col, block in blocks(pos, refs[:7], 256):
        feats[:, pl.ds(col, 256)] = block
    gate = nn(feats[...], gate_w[...])
    sigma = 1.0 / (1.0 + jnp.exp(-gate))
    slope[...] = sigma * (1.0 + gate * (1.0 - sigma)) * nn(feats[...], up_w[...])
    acc = jnp.zeros(tangent.shape, F32)
    for k in range(4):
        cols = pl.multiple_of(pos[4 + k] * 1024, 1024)
        acc = acc + nn(feats[:, pl.ds(cols, 1024)], rows[k][...])
    tangent[...] = acc
    pushed_a[...] = (slope[:256] * acc[:256]).astype(BF)
    pushed_b[...] = (slope[256:] * acc[256:]).astype(BF)


def push_kernel(pos, own_a, own_b, other_a, other_b, keep, recv, row0, row1, row3, f0, f1, f2, f3, strip, own, other):
    x, z = pos[0], pos[1]
    extra = None
    if own_b.shape[0] > 256:
        extra = digits(undigit(own_b[256:].astype(F32) + other_b[256:].astype(F32)), 512)[:, :128]

    def put(out, block):
        out[:512] = block
        if extra is not None:
            out[512:] = extra

    for whole, a, b in ((own, own_a, own_b), (other, other_a, other_b)):
        whole[:256] = a[...]
        whole[256:] = b[:256]
    for i, f in enumerate((f0, f1, f2, f3)):
        cols = pl.ds(pl.multiple_of(lax.rem(x + i, 4) * 512, 512), 512)
        strip[...] = (nn(own[...], keep[:, cols]) + nn(other[...], recv[:, cols])).astype(BF)
        for j, out in enumerate((row0.at[i], row1.at[i], f, row3.at[i])):
            put(out, strip[:, pl.ds(pl.multiple_of(lax.rem(z + j, 4) * 128, 128), 128)])


def weigh_first_kernel(b0, b1, b2, b3, b4, curvature, moved, weighted):
    acc, _ = add_up(b0[...], b1[...], b2[...], b3[...], b4[...])
    moved[...] = acc
    weighted[...] = (curvature[...] * acc / TOKENS).astype(BF)


def weigh_second_kernel(b0, b1, b2, b3, b4, curvature, moved, weighted, scalars):
    acc, (ss, sw, dd) = add_up(b0[...], b1[...], b2[...], b3[...], b4[...])
    alpha = sw / (ss + EPS)
    scale = lax.rsqrt(dd + 1e-30) * (1.0 / 1024.0)
    weighted[...] = (curvature[...] * ((acc - alpha * moved[...]) * scale) / TOKENS).astype(BF)
    scalars[...] = row_of([ss, sw, scale], 8, 128)


def back_kernel(pos, *refs):
    recv, full, send_a, send_b = refs[7:]
    for col, block in blocks(pos, refs[:7], 128):
        full[:, pl.ds(col, 128)] = block
    send = nt(full[...], recv[...]).astype(BF)
    send_a[...] = send[:256]
    send_b[...] = send[256:]


def own_back_kernel(full, keep, out):
    out[...] = nt(full[...], keep[...])


def delta_first_kernel(own, got_a, got_b, slope, tangent, squares, out):
    out[:256, :] = ((own[:256] + got_a[...].astype(F32)) * slope[:256]).astype(BF)
    out[256:512, :] = ((own[256:] + got_b[...].astype(F32)) * slope[256:]).astype(BF)
    delta = out[:512, :].astype(F32)
    sums = [total(squares[...]), total(tangent[...] * delta), total(delta * (delta * 1.0))]
    out[512:, :] = digits([jnp.broadcast_to(v, (1, 512)) for v in sums], 512)


def delta_second_kernel(own, got_a, got_b, slope, tan_start, tan_image, delta_one, out, sums):
    out[:256, :] = ((own[:256] + got_a[...].astype(F32)) * slope[:256]).astype(BF)
    out[256:, :] = ((own[256:] + got_b[...].astype(F32)) * slope[256:]).astype(BF)
    delta = out[...].astype(F32)
    ww = total(tan_image[...] * delta_one[:512].astype(F32))
    sums[...] = row_of([ww, total(tan_start[...] * delta), total(tan_image[...] * delta)], 8, 128)


def own_gram_kernel(feats, out):
    out[...] = nt(feats[...], feats[...])


def core_gram_kernel(feats, one, out):
    out[...] = nt(feats[...], one[...])


def far_gram_kernel(feats, one, two, out):
    out[:, :128] = nt(feats[...], one[...])
    out[:, 128:] = nt(feats[...], two[...])


def rows_kernel(pos, feats, out):
    out[...] = feats[:, pl.ds(pl.multiple_of(pos[3] * 1024, 1024), 1024)].T


def far_rows_kernel(pos, feats, out, other):
    c = pos[8]
    out[...] = feats[:, pl.ds(pl.multiple_of(c * 1024, 1024), 1024)].T
    other[...] = feats[:, pl.ds(pl.multiple_of((1 - c) * 1024, 1024), 1024)].T


def gram_split_kernel(pos, own, core, p0, p1, p2, p3, high, low):
    def put(cols, v):
        top = v.astype(BF)
        high[:, cols] = top
        low[:, cols] = (v - top.astype(F32)).astype(BF)

    put(slice(0, 512), own[...])
    put(slice(512, 1024), core[...])
    for i, p in enumerate((p0, p1, p2, p3)):
        q = lax.rem(pos[9] + i, 4) * 128
        put(pl.ds(pl.multiple_of(1024 + q, 128), 128), p[:, :128])
        put(pl.ds(pl.multiple_of(1536 + q, 128), 128), p[:, 128:])


def near_tangent_kernel(high, low, d0, d1, out):
    acc = nn(high[:, :512], d0[:512]) + nn(low[:, :512], d0[:512])
    out[...] = acc + nn(high[:, 512:1024], d1[:512]) + nn(low[:, 512:1024], d1[:512])


def far_tangent_kernel(near, high, low, d0, d1, d2, d3, slope, tangent, pushed_a, pushed_b):
    acc = near[...] + nn(high[:, 1024:1536], d2[:512]) + nn(low[:, 1024:1536], d2[:512])
    acc = acc + nn(high[:, 1536:], d3[:512]) + nn(low[:, 1536:], d3[:512])
    tangent[...] = acc
    pushed_a[...] = (slope[:256] * acc[:256]).astype(BF)
    pushed_b[:256, :] = (slope[256:] * acc[256:]).astype(BF)
    rows = d0[512:].astype(F32) + d1[512:].astype(F32) + d2[512:].astype(F32) + d3[512:].astype(F32)
    pushed_b[256:, :] = digits(undigit(rows), 512)


def near_image_kernel(r0, r1, d0, d1, out):
    out[...] = nn(r0[...], d0[:512]) + nn(r1[...], d1[:512])


def far_image_kernel(near, r2, r3, d2, d3, out):
    out[...] = near[...] + nn(r2[...], d2[:512]) + nn(r3[...], d3[:512])


def last_image_kernel(near, r2, r3, d2, d3, sums, out, block):
    acc = near[...] + nn(r2[...], d2[...]) + nn(r3[...], d3[...])
    out[...] = acc
    index = lax.broadcasted_iota(jnp.int32, (8, 128), 0)
    block[...] = jnp.where(index == 3, jnp.broadcast_to(total(acc * acc), (8, 128)), sums[...])


def final_kernel(got, scalars, start, image_one, image_two, out, coefficients):
    acc = got[0]
    for i in range(1, 128):
        acc = acc + got[i]
    ss, sw, scale = scalars[0:1], scalars[1:2], scalars[2:3]
    ww, uz, wz, zz = acc[0:1], acc[1:2], acc[2:3], acc[3:4]
    norm_sq = ss + EPS
    norm = jnp.sqrt(norm_sq)
    alpha_one = sw / norm_sq
    one_one = ss / norm_sq
    resid_sq = jnp.maximum(ww / norm_sq - alpha_one * alpha_one * (2.0 - one_one), 0.0)
    beta_one = jnp.sqrt(resid_sq + EPS)
    second = 1.0 / (norm * beta_one)
    image = second / scale
    alpha_two = image * second * (wz - alpha_one * uz)
    cross = image * uz / norm
    two_two = resid_sq / (resid_sq + EPS)
    one_two = alpha_one * (1.0 - one_one) / beta_one
    last_sq = (
        image * image * zz
        - alpha_two * alpha_two * (2.0 - two_two)
        - cross * cross * (2.0 - one_one)
        + 2.0 * alpha_two * cross * one_two
    )
    beta_two = jnp.sqrt(jnp.maximum(last_sq, 0.0) + EPS)
    index = lax.broadcasted_iota(jnp.int32, (1, 128), 1)
    row = jnp.zeros((1, 128), F32)
    for i, v in enumerate((alpha_one, beta_one, alpha_two, beta_two)):
        row = jnp.where(index == i, v, row)
    coefficients[...] = row
    f_two = image / beta_two
    f_one = -alpha_two * second / beta_two
    f_start = (alpha_two * alpha_one / beta_one - cross) / (norm * beta_two)
    for k in range(4):
        cols = slice(k * 128, (k + 1) * 128)
        out[:, cols] = f_two * image_two[:, cols] + f_one * image_one[:, cols] + f_start * start[:, cols]


def shards(tokens, gate_weight, up_weight, down_weight, curvature, start):
    yh, c, x, z, yl = [lax.axis_index(n).astype(jnp.int32) for n in NAMES]
    dp = yh * 2 + c
    quarter_of = lax.rem(x + 2 * z, 4)
    pos = jnp.stack(
        [x, z, yl, dp, dp, yh * 2 + 1 - c, (1 - yh) * 2 + c, (1 - yh) * 2 + 1 - c, c, quarter_of]
    )

    other = shift(tokens, "yl", 1)
    start_b, squares = call(cast_kernel, "cast_start", [((1024, 512), BF), ((8, 512), F32)], start)
    keep, send = call(
        split_kernel,
        "split_down",
        [((512, 2048), BF), ((256, 2048), BF)],
        pos, down_weight,
    )
    pair = jnp.where(
        yl == 0, jnp.concatenate([tokens, other], axis=1), jnp.concatenate([other, tokens], axis=1)
    )
    pieces, (recv, start_b) = gather(pair, (from_y(after(send, other)), start_b))
    far_start = shift(start_b, "yh", 1)
    pieces, start_b, far_start, recv = lax.optimization_barrier((pieces, start_b, far_start, recv))
    starts = [start_b, shift(start_b, "c", 1), far_start, shift(far_start, "c", 1)]
    recv = call(join_kernel, "join", [((512, 2048), BF)], pos, recv, shift(recv, "c", 1))
    recv, pieces = lax.optimization_barrier((recv, pieces))
    feats, slope, tan_start, *pushed = call(
        front_kernel,
        "front",
        [((512, D), BF), ((512, 512), F32), ((512, 512), F32), ((256, 512), BF), ((256, 512), BF)],
        pos, *pieces, gate_weight, up_weight, *starts,
        mib=24,
    )
    row, block = (4, 512, 128), (512, 128)

    other = [shift(v, "yl", 1) for v in pushed]
    feats_c = shift(after(feats, recv), "c", 1)
    own_gram = call(own_gram_kernel, "own_gram", [((512, 512), F32)], after(feats, pushed))
    other, own_gram, feats_c = lax.optimization_barrier((other, own_gram, feats_c))
    parts = call(
        push_kernel,
        "push",
        [(row, BF)] * 3 + [(block, BF)] * 4,
        pos, *pushed, *other, keep, recv,
        scratch=[((512, 512), BF)] * 3,
    )
    quarter = lax.dynamic_slice_in_dim(feats, quarter_of * 128, 128, axis=0)
    quarter = shift(after(quarter, parts[0]), "yh", 1)
    parts = scatter(parts)
    moved, weighted = call(
        weigh_first_kernel, "weigh", [((512, 128), F32), ((512, 128), BF)], *parts, curvature
    )
    quarter, weighted = lax.optimization_barrier((quarter, weighted))
    pieces, quarter_c = gather(weighted, shift(quarter, "c", 1))
    far_gram = call(far_gram_kernel, "far_gram", [((512, 256), F32)], feats, quarter, quarter_c)
    recv_one, far_gram = lax.optimization_barrier((recv, far_gram))
    full, *send = call(
        back_kernel, "back_other", [((512, 2048), BF), ((256, 512), BF), ((256, 512), BF)], pos, *pieces, recv_one
    )
    got = [shift(v, "yl", 1) for v in send]
    own = call(own_back_kernel, "back_own", [((512, 512), F32)], full, keep)
    far_gram = after(far_gram, own)
    far_grams = [far_gram, shift(far_gram, "x", 1), shift(far_gram, "z", 1), shift(far_gram, "x", 3)]
    delta = call(delta_first_kernel, "delta", [((528, 512), BF)], own, *got, slope, tan_start, squares)
    deltas = [delta, shift(delta, "c", 1)]
    far_delta = shift(delta, "yh", 1)
    core_gram = call(core_gram_kernel, "core_gram", [((512, 512), F32)], after(feats, delta), feats_c)
    high, low = call(
        gram_split_kernel,
        "gram_split",
        [((512, 2048), BF)] * 2,
        pos, after(own_gram, delta), core_gram, *far_grams,
    )
    near = call(near_tangent_kernel, "near_tangent", [((512, 512), F32)], high, low, *deltas)
    far_delta, near = lax.optimization_barrier((far_delta, near))
    deltas += [far_delta, shift(far_delta, "c", 1)]
    tan_image, *pushed = call(
        far_tangent_kernel,
        "far_tangent",
        [((512, 512), F32), ((256, 512), BF), ((272, 512), BF)],
        near, high, low, *deltas, slope,
    )

    row, block = (4, 528, 128), (528, 128)
    other = [shift(v, "yl", 1) for v in pushed]
    first_deltas = deltas
    rows = [call(rows_kernel, "rows", [((1024, 512), BF)], pos, after(f, *pushed)) for f in (feats, feats_c)]
    near_one = call(near_image_kernel, "near_image", [((1024, 512), F32)], *rows, *first_deltas[:2])
    other, near_one = lax.optimization_barrier((other, near_one))
    parts = call(
        push_kernel,
        "push",
        [(row, BF)] * 3 + [(block, BF)] * 4,
        pos, *pushed, *other, keep, recv,
        scratch=[((512, 512), BF)] * 3,
    )
    theirs = lax.dynamic_slice_in_dim(feats, (1 - yh) * 2048, 2048, axis=1)
    far_rows = shift(after(theirs, parts[0]), "yh", 1)
    parts = scatter(parts)
    weighted, scalars = call(
        weigh_second_kernel, "weigh", [((512, 128), BF), ((8, 128), F32)], *parts, curvature, moved
    )
    pieces, _ = gather(weighted)
    full, *send = call(
        back_kernel, "back_other", [((512, 2048), BF), ((256, 512), BF), ((256, 512), BF)], pos, *pieces, recv
    )
    got = [shift(v, "yl", 1) for v in send]
    own = call(own_back_kernel, "back_own", [((512, 512), F32)], full, keep)
    mine, theirs = call(far_rows_kernel, "far_rows", [((1024, 512), BF)] * 2, pos, after(far_rows, *send))
    got, mine, theirs = lax.optimization_barrier((got, mine, theirs))
    rows += [mine, shift(theirs, "c", 1)]
    delta, sums = call(
        delta_second_kernel,
        "delta",
        [((512, 512), BF), ((8, 128), F32)],
        own, *got, slope, tan_start, tan_image, delta,
    )
    deltas = [delta, shift(delta, "c", 1)]
    far_delta = shift(delta, "yh", 1)
    image_one = call(
        far_image_kernel, "far_image", [((1024, 512), F32)], after(near_one, delta), *rows[2:], *first_deltas[2:]
    )
    near = call(near_image_kernel, "near_image", [((1024, 512), F32)], *rows[:2], *deltas)
    far_delta, near, image_one = lax.optimization_barrier((far_delta, near, image_one))
    deltas += [far_delta, shift(far_delta, "c", 1)]
    image_two, block = call(
        last_image_kernel, "last_image", [((1024, 512), F32), ((8, 128), F32)], near, *rows[2:], *deltas[2:], sums
    )
    got = lax.all_to_all(jnp.broadcast_to(block[None], (128, 8, 128)), NAMES, 0, 0, tiled=True)
    whole = lambda *s: pl.BlockSpec(s, lambda i: (0,) * len(s))
    band = pl.BlockSpec((256, 512), lambda i: (i, 0))
    next_vector, coefficients = pl.pallas_call(
        final_kernel,
        grid=(4,),
        out_shape=[jax.ShapeDtypeStruct((1024, 512), F32), jax.ShapeDtypeStruct((1, 128), F32)],
        in_specs=[whole(128, 8, 128), whole(8, 128), band, band, band],
        out_specs=[band, whole(1, 128)],
        compiler_params=pltpu.CompilerParams(vmem_limit_bytes=16 * MIB),
        name="final",
    )(got, scalars, start, image_one, image_two)
    return (coefficients[0, :4], next_vector)


def solution(mesh):
    inner = Mesh(mesh.devices.reshape([n for _, n in AXES]), NAMES)
    dp, fsdp = ("yh", "c"), ("x", "z", "yl")
    in_specs = (P(dp, fsdp), P(None, fsdp), P(None, fsdp), P(fsdp, None), P(dp, fsdp), P(dp, fsdp))
    out_specs = (P(), P(dp, fsdp))
    return jax.shard_map(shards, mesh=inner, in_specs=in_specs, out_specs=out_specs, check_vma=False)
```

```python
import jax
import jax.numpy as jnp
from jax import lax
from jax.experimental import pallas as pl
from jax.experimental.pallas import tpu as pltpu
from jax.sharding import Mesh
from jax.sharding import PartitionSpec as P

D = 4096
FF = 16384
EPS = 1e-06
TOKENS = 2048
SCALE_INV = 1.0 / (D * FF)
AXES = (("yh", 2), ("c", 2), ("x", 4), ("z", 4), ("yl", 2))
NAMES = tuple(name for name, _ in AXES)
SIZES = dict(AXES)
BF = jnp.bfloat16
F32 = jnp.float32
MIB = 1024 * 1024
VM = pl.BlockSpec(memory_space=pltpu.VMEM)
SM = pl.BlockSpec(memory_space=pltpu.SMEM)


def shift(value, axis, by):
    n = SIZES[axis]
    return lax.ppermute(value, axis, [((i + by) % n, i) for i in range(n)])


def from_y(v):
    pairs = []
    for y in range(4):
        for c in range(2):
            src = (y + (1 if c == 0 else 3)) % 4
            pairs.append(((src // 2 * 2 + c) * 2 + src % 2, (y // 2 * 2 + c) * 2 + y % 2))
    return lax.ppermute(v, ("yh", "c", "yl"), pairs)


def line(v, a):
    return [v, shift(v, a, 1), shift(v, a, 2), shift(v, a, 3)]


def after(value, *others):
    return lax.optimization_barrier((value, *others))[0]


def call(kernel, name, out, *operands, mib=12, scratch=()):
    specs = [SM if v.dtype == jnp.int32 else VM for v in operands]
    shapes = [jax.ShapeDtypeStruct(s, t) for s, t in out]
    got = pl.pallas_call(
        kernel,
        out_shape=shapes,
        in_specs=specs,
        out_specs=[VM] * len(shapes),
        scratch_shapes=[pltpu.VMEM(s, t) for s, t in scratch],
        compiler_params=pltpu.CompilerParams(vmem_limit_bytes=mib * MIB),
        name=name,
    )(*operands)
    return got if len(got) > 1 else got[0]


def gather(v, later=()):
    here, far, later = lax.optimization_barrier((line(v, "x"), shift(v, "z", 2), later))
    here = jnp.stack(here)
    return [here, shift(here, "z", 1), *line(far, "x"), shift(here, "z", 3)], later


def scatter(parts):
    row0, row1, row3, f0, f1, f2, f3 = parts
    up, down = shift(row1, "z", 3), shift(row3, "z", 1)
    far = [f0, shift(f1, "x", 3), shift(f2, "x", 2), shift(f3, "x", 1)]
    block = (f0.shape, BF)
    r0, r1, r2, r3, far = call(add_kernel, "add", [block] * 5, row0, up, down, *far)
    return [r0, shift(r1, "x", 3), shift(r2, "x", 2), shift(r3, "x", 1), shift(far, "z", 2)]


def add_up(*blocks):
    acc = blocks[0].astype(F32)
    for b in blocks[1:]:
        acc = acc + b.astype(F32)
    return acc[:512], undigit(acc[512:]) if acc.shape[0] > 512 else None


def add_kernel(row0, up, down, f0, f1, f2, f3, r0, r1, r2, r3, far):
    def put(out, *blocks):
        acc, sums = add_up(*blocks)
        out[:512, :] = acc.astype(BF)
        if sums is not None:
            out[512:, :] = digits(sums, 128)

    put(far, f0[...], f1[...], f2[...], f3[...])
    for i, r in enumerate((r0, r1, r2, r3)):
        put(r, row0[i], up[i], down[i])


def blocks(pos, refs, width):
    here, nxt, f0, f1, f2, f3, prev = refs
    for i, f in enumerate((f0, f1, f2, f3)):
        yield place(pos, i, 0, width), here[i]
        yield place(pos, i, 1, width), nxt[i]
        yield place(pos, i, 2, width), f[...]
        yield place(pos, i, 3, width), prev[i]


def nt(a, b):
    return lax.dot_general(a, b, (((1,), (1,)), ((), ())), preferred_element_type=F32)


def nn(a, b):
    return jnp.dot(a, b, preferred_element_type=F32)


def place(pos, i, j, width):
    return pl.multiple_of((lax.rem(pos[0] + i, 4) * 4 + lax.rem(pos[1] + j, 4)) * width, width)


def total(v):
    return jnp.sum(v, axis=(0, 1), keepdims=True) * SCALE_INV


def row_of(values, rows, width):
    index = lax.broadcasted_iota(jnp.int32, (rows, width), 0)
    out = jnp.zeros((rows, width), F32)
    for i, v in enumerate(values):
        out = jnp.where(index == i, jnp.broadcast_to(v, (rows, width)), out)
    return out


def digits(values, width):
    rows = []
    for v in values:
        for _ in range(3):
            d = v.astype(BF).astype(F32)
            rows.append(d)
            v = v - d
    return row_of(rows, 16, width).astype(BF)


def undigit(rows):
    return [rows[3 * i:3 * i + 1] + rows[3 * i + 1:3 * i + 2] + rows[3 * i + 2:3 * i + 3] for i in range(3)]


def cast_kernel(start, out, squares):
    acc = jnp.zeros((8, 512), F32)
    for i in range(0, 1024, 8):
        v = start[i:i + 8, :]
        acc = acc + v * v
    out[...] = start[...].astype(BF)
    squares[...] = acc


def split_kernel(pos, down, keep, send):
    yl = pos[2]
    mine = pl.ds(pl.multiple_of(pos[8] * 256, 256), 256)
    for b in range(16):
        keep[:, b * 128:(b + 1) * 128] = down[:, pl.ds(pl.multiple_of((2 * b + yl) * 128, 128), 128)]
        send[:, b * 128:(b + 1) * 128] = down[mine, pl.ds(pl.multiple_of((2 * b + 1 - yl) * 128, 128), 128)]


def join_kernel(pos, mine, theirs, out):
    out[pl.ds(pl.multiple_of(pos[8] * 256, 256), 256), :] = mine[...]
    out[pl.ds(pl.multiple_of((1 - pos[8]) * 256, 256), 256), :] = theirs[...]


def front_kernel(pos, *refs):
    gate_w, up_w = refs[7:9]
    rows = refs[9:13]
    feats, slope, tangent, pushed_a, pushed_b = refs[13:]
    for col, block in blocks(pos, refs[:7], 256):
        feats[:, pl.ds(col, 256)] = block
    gate = nn(feats[...], gate_w[...])
    sigma = 1.0 / (1.0 + jnp.exp(-gate))
    slope[...] = sigma * (1.0 + gate * (1.0 - sigma)) * nn(feats[...], up_w[...])
    acc = jnp.zeros(tangent.shape, F32)
    for k in range(4):
        cols = pl.multiple_of(pos[4 + k] * 1024, 1024)
        acc = acc + nn(feats[:, pl.ds(cols, 1024)], rows[k][...])
    tangent[...] = acc
    pushed_a[...] = (slope[:256] * acc[:256]).astype(BF)
    pushed_b[...] = (slope[256:] * acc[256:]).astype(BF)


def push_kernel(pos, own_a, own_b, other_a, other_b, keep, recv, row0, row1, row3, f0, f1, f2, f3, strip):
    x, z = pos[0], pos[1]
    extra = None
    if own_b.shape[0] > 256:
        extra = digits(undigit(own_b[256:].astype(F32) + other_b[256:].astype(F32)), 512)[:, :128]

    def put(out, block):
        out[:512] = block
        if extra is not None:
            out[512:] = extra

    for i, f in enumerate((f0, f1, f2, f3)):
        cols = pl.ds(pl.multiple_of(lax.rem(x + i, 4) * 512, 512), 512)
        strip[:256] = (nn(own_a[...], keep[:, cols]) + nn(other_a[...], recv[:, cols])).astype(BF)
        strip[256:] = (nn(own_b[:256], keep[:, cols]) + nn(other_b[:256], recv[:, cols])).astype(BF)
        for j, out in enumerate((row0.at[i], row1.at[i], f, row3.at[i])):
            put(out, strip[:, pl.ds(pl.multiple_of(lax.rem(z + j, 4) * 128, 128), 128)])


def weigh_first_kernel(b0, b1, b2, b3, b4, curvature, moved, weighted):
    acc, _ = add_up(b0[...], b1[...], b2[...], b3[...], b4[...])
    moved[...] = acc
    weighted[...] = (curvature[...] * acc / TOKENS).astype(BF)


def weigh_second_kernel(b0, b1, b2, b3, b4, curvature, moved, weighted, scalars):
    acc, (ss, sw, dd) = add_up(b0[...], b1[...], b2[...], b3[...], b4[...])
    alpha = sw / (ss + EPS)
    scale = lax.rsqrt(dd + 1e-30) * (1.0 / 1024.0)
    weighted[...] = (curvature[...] * ((acc - alpha * moved[...]) * scale) / TOKENS).astype(BF)
    scalars[...] = row_of([ss, sw, scale], 8, 128)


def back_kernel(pos, *refs):
    recv, full, send_a, send_b = refs[7:]
    for col, block in blocks(pos, refs[:7], 128):
        full[:, pl.ds(col, 128)] = block
    send = nt(full[...], recv[...]).astype(BF)
    send_a[...] = send[:256]
    send_b[...] = send[256:]


def own_back_kernel(full, keep, out):
    out[...] = nt(full[...], keep[...])


def delta_first_kernel(own, got_a, got_b, slope, tangent, squares, out):
    out[:256, :] = ((own[:256] + got_a[...].astype(F32)) * slope[:256]).astype(BF)
    out[256:512, :] = ((own[256:] + got_b[...].astype(F32)) * slope[256:]).astype(BF)
    delta = out[:512, :].astype(F32)
    sums = [total(squares[...]), total(tangent[...] * delta), total(delta * (delta * 1.0))]
    out[512:, :] = digits([jnp.broadcast_to(v, (1, 512)) for v in sums], 512)


def delta_second_kernel(own, got_a, got_b, slope, tan_start, tan_image, delta_one, out, sums):
    out[:256, :] = ((own[:256] + got_a[...].astype(F32)) * slope[:256]).astype(BF)
    out[256:, :] = ((own[256:] + got_b[...].astype(F32)) * slope[256:]).astype(BF)
    delta = out[...].astype(F32)
    ww = total(tan_image[...] * delta_one[:512].astype(F32))
    sums[...] = row_of([ww, total(tan_start[...] * delta), total(tan_image[...] * delta)], 8, 128)


def own_gram_kernel(feats, out):
    out[...] = nt(feats[...], feats[...])


def quarter_kernel(pos, feats, out):
    out[...] = feats[pl.ds(pl.multiple_of(pos[9] * 128, 128), 128), :]


def their_rows_kernel(pos, feats, out):
    out[...] = feats[:, pl.ds(pl.multiple_of((1 - pos[10]) * 2048, 2048), 2048)]


def core_gram_kernel(feats, one, out):
    out[...] = nt(feats[...], one[...])


def far_gram_kernel(feats, one, two, out):
    out[:, :128] = nt(feats[...], one[...])
    out[:, 128:] = nt(feats[...], two[...])


def rows_kernel(pos, feats, out):
    out[...] = feats[:, pl.ds(pl.multiple_of(pos[3] * 1024, 1024), 1024)].T


def far_rows_kernel(pos, feats, out, other):
    c = pos[8]
    out[...] = feats[:, pl.ds(pl.multiple_of(c * 1024, 1024), 1024)].T
    other[...] = feats[:, pl.ds(pl.multiple_of((1 - c) * 1024, 1024), 1024)].T


def gram_split_kernel(pos, own, core, p0, p1, p2, p3, high, low):
    def put(cols, v):
        top = v.astype(BF)
        high[:, cols] = top
        low[:, cols] = (v - top.astype(F32)).astype(BF)

    put(slice(0, 512), own[...])
    put(slice(512, 1024), core[...])
    for i, p in enumerate((p0, p1, p2, p3)):
        q = lax.rem(pos[9] + i, 4) * 128
        put(pl.ds(pl.multiple_of(1024 + q, 128), 128), p[:, :128])
        put(pl.ds(pl.multiple_of(1536 + q, 128), 128), p[:, 128:])


def near_tangent_kernel(high, low, d0, d1, out):
    acc = nn(high[:, :512], d0[:512]) + nn(low[:, :512], d0[:512])
    out[...] = acc + nn(high[:, 512:1024], d1[:512]) + nn(low[:, 512:1024], d1[:512])


def far_tangent_kernel(near, high, low, d0, d1, d2, d3, slope, tangent, pushed_a, pushed_b):
    acc = near[...] + nn(high[:, 1024:1536], d2[:512]) + nn(low[:, 1024:1536], d2[:512])
    acc = acc + nn(high[:, 1536:], d3[:512]) + nn(low[:, 1536:], d3[:512])
    tangent[...] = acc
    pushed_a[...] = (slope[:256] * acc[:256]).astype(BF)
    pushed_b[:256, :] = (slope[256:] * acc[256:]).astype(BF)
    rows = d0[512:].astype(F32) + d1[512:].astype(F32) + d2[512:].astype(F32) + d3[512:].astype(F32)
    pushed_b[256:, :] = digits(undigit(rows), 512)


def near_image_kernel(r0, r1, d0, d1, out):
    out[...] = nn(r0[...], d0[:512]) + nn(r1[...], d1[:512])


def far_image_kernel(near, r2, r3, d2, d3, out):
    out[...] = near[...] + nn(r2[...], d2[:512]) + nn(r3[...], d3[:512])


def last_image_kernel(near, r2, r3, d2, d3, sums, out, block):
    acc = near[...] + nn(r2[...], d2[...]) + nn(r3[...], d3[...])
    out[...] = acc
    index = lax.broadcasted_iota(jnp.int32, (8, 128), 0)
    block[...] = jnp.where(index == 3, jnp.broadcast_to(total(acc * acc), (8, 128)), sums[...])


def final_kernel(got, scalars, start, image_one, image_two, out, coefficients):
    acc = got[0]
    for i in range(1, 128):
        acc = acc + got[i]
    ss, sw, scale = scalars[0:1], scalars[1:2], scalars[2:3]
    ww, uz, wz, zz = acc[0:1], acc[1:2], acc[2:3], acc[3:4]
    norm_sq = ss + EPS
    norm = jnp.sqrt(norm_sq)
    alpha_one = sw / norm_sq
    one_one = ss / norm_sq
    resid_sq = jnp.maximum(ww / norm_sq - alpha_one * alpha_one * (2.0 - one_one), 0.0)
    beta_one = jnp.sqrt(resid_sq + EPS)
    second = 1.0 / (norm * beta_one)
    image = second / scale
    alpha_two = image * second * (wz - alpha_one * uz)
    cross = image * uz / norm
    two_two = resid_sq / (resid_sq + EPS)
    one_two = alpha_one * (1.0 - one_one) / beta_one
    last_sq = (
        image * image * zz
        - alpha_two * alpha_two * (2.0 - two_two)
        - cross * cross * (2.0 - one_one)
        + 2.0 * alpha_two * cross * one_two
    )
    beta_two = jnp.sqrt(jnp.maximum(last_sq, 0.0) + EPS)
    for i, v in enumerate((alpha_one, beta_one, alpha_two, beta_two)):
        coefficients[i] = v[0, 0]
    f_two = image / beta_two
    f_one = -alpha_two * second / beta_two
    f_start = (alpha_two * alpha_one / beta_one - cross) / (norm * beta_two)
    for k in range(4):
        cols = slice(k * 128, (k + 1) * 128)
        out[:, cols] = f_two * image_two[:, cols] + f_one * image_one[:, cols] + f_start * start[:, cols]


def shards(tokens, gate_weight, up_weight, down_weight, curvature, start):
    yh, c, x, z, yl = [lax.axis_index(n).astype(jnp.int32) for n in NAMES]
    dp = yh * 2 + c
    quarter_of = lax.rem(x + 2 * z, 4)
    pos = jnp.stack(
        [x, z, yl, dp, dp, yh * 2 + 1 - c, (1 - yh) * 2 + c, (1 - yh) * 2 + 1 - c, c, quarter_of, yh]
    )

    other = shift(tokens, "yl", 1)
    start_b, squares = call(cast_kernel, "cast_start", [((1024, 512), BF), ((8, 512), F32)], start)
    other, start_b = lax.optimization_barrier((other, start_b))
    far_start = shift(start_b, "yh", 1)
    starts = [start_b, shift(start_b, "c", 1), far_start, shift(far_start, "c", 1)]
    pair = jnp.where(
        yl == 0, jnp.concatenate([tokens, other], axis=1), jnp.concatenate([other, tokens], axis=1)
    )
    keep, send = call(
        split_kernel,
        "split_down",
        [((512, 2048), BF), ((256, 2048), BF)],
        pos, after(down_weight, pair),
    )
    pieces, send = gather(pair, send)
    recv = from_y(after(send, far_start))
    recv, pieces = lax.optimization_barrier((recv, pieces))
    feats, slope, tan_start, *pushed = call(
        front_kernel,
        "front",
        [((512, D), BF), ((512, 512), F32), ((512, 512), F32), ((256, 512), BF), ((256, 512), BF)],
        pos, *pieces, gate_weight, up_weight, *starts,
        mib=12,
    )
    recv = call(join_kernel, "join", [((512, 2048), BF)], pos, recv, shift(recv, "c", 1))
    row, block = (4, 512, 128), (512, 128)

    other = [shift(v, "yl", 1) for v in pushed]
    feats_c = shift(after(feats, recv), "c", 1)
    own_gram = call(own_gram_kernel, "own_gram", [((512, 512), F32)], after(feats, pushed))
    quarter = call(quarter_kernel, "quarter", [((128, D), BF)], pos, after(feats, *pushed))
    other, own_gram, feats_c, quarter = lax.optimization_barrier((other, own_gram, feats_c, quarter))
    parts = call(
        push_kernel,
        "push",
        [(row, BF)] * 3 + [(block, BF)] * 4,
        pos, *pushed, *other, keep, recv,
        scratch=[((512, 512), BF)],
    )
    quarter = shift(after(quarter, parts[0]), "yh", 1)
    parts = scatter(parts)
    moved, weighted = call(
        weigh_first_kernel, "weigh", [((512, 128), F32), ((512, 128), BF)], *parts, curvature
    )
    quarter, weighted = lax.optimization_barrier((quarter, weighted))
    pieces, quarter_c = gather(weighted, shift(quarter, "c", 1))
    far_gram = call(far_gram_kernel, "far_gram", [((512, 256), F32)], feats, quarter, quarter_c)
    recv_one, far_gram = lax.optimization_barrier((recv, far_gram))
    full, *send = call(
        back_kernel, "back_other", [((512, 2048), BF), ((256, 512), BF), ((256, 512), BF)], pos, *pieces, recv_one
    )
    got = [shift(v, "yl", 1) for v in send]
    far_gram = after(far_gram, *send)
    far_grams = [far_gram, shift(far_gram, "x", 1), shift(far_gram, "z", 1), shift(far_gram, "x", 3)]
    own = call(own_back_kernel, "back_own", [((512, 512), F32)], full, keep)
    got, far_grams = lax.optimization_barrier((got, far_grams))
    delta = call(delta_first_kernel, "delta", [((528, 512), BF)], own, *got, slope, tan_start, squares)
    deltas = [delta, shift(delta, "c", 1)]
    far_delta = shift(delta, "yh", 1)
    core_gram = call(core_gram_kernel, "core_gram", [((512, 512), F32)], after(feats, delta), feats_c)
    high, low = call(
        gram_split_kernel,
        "gram_split",
        [((512, 2048), BF)] * 2,
        pos, after(own_gram, delta), core_gram, *far_grams,
    )
    near = call(near_tangent_kernel, "near_tangent", [((512, 512), F32)], high, low, *deltas)
    far_delta, near = lax.optimization_barrier((far_delta, near))
    deltas += [far_delta, shift(far_delta, "c", 1)]
    tan_image, *pushed = call(
        far_tangent_kernel,
        "far_tangent",
        [((512, 512), F32), ((256, 512), BF), ((272, 512), BF)],
        near, high, low, *deltas, slope,
    )

    row, block = (4, 528, 128), (528, 128)
    other = [shift(v, "yl", 1) for v in pushed]
    first_deltas = deltas
    rows = [call(rows_kernel, "rows", [((1024, 512), BF)], pos, after(f, *pushed)) for f in (feats, feats_c)]
    near_one = call(near_image_kernel, "near_image", [((1024, 512), F32)], *rows, *first_deltas[:2])
    theirs = call(their_rows_kernel, "their_rows", [((512, 2048), BF)], pos, after(feats, *pushed))
    other, near_one, theirs = lax.optimization_barrier((other, near_one, theirs))
    parts = call(
        push_kernel,
        "push",
        [(row, BF)] * 3 + [(block, BF)] * 4,
        pos, *pushed, *other, keep, recv,
        scratch=[((512, 512), BF)],
    )
    far_rows = shift(after(theirs, parts[0]), "yh", 1)
    parts = scatter(parts)
    weighted, scalars = call(
        weigh_second_kernel, "weigh", [((512, 128), BF), ((8, 128), F32)], *parts, curvature, moved
    )
    pieces, _ = gather(weighted)
    full, *send = call(
        back_kernel, "back_other", [((512, 2048), BF), ((256, 512), BF), ((256, 512), BF)], pos, *pieces, recv
    )
    got = [shift(v, "yl", 1) for v in send]
    own = call(own_back_kernel, "back_own", [((512, 512), F32)], full, keep)
    mine, theirs = call(far_rows_kernel, "far_rows", [((1024, 512), BF)] * 2, pos, after(far_rows, *send))
    got, mine, theirs = lax.optimization_barrier((got, mine, theirs))
    rows += [mine, shift(theirs, "c", 1)]
    delta, sums = call(
        delta_second_kernel,
        "delta",
        [((512, 512), BF), ((8, 128), F32)],
        own, *got, slope, tan_start, tan_image, delta,
    )
    deltas = [delta, shift(delta, "c", 1)]
    far_delta = shift(delta, "yh", 1)
    image_one = call(
        far_image_kernel, "far_image", [((1024, 512), F32)], after(near_one, delta), *rows[2:], *first_deltas[2:]
    )
    near = call(near_image_kernel, "near_image", [((1024, 512), F32)], *rows[:2], *deltas)
    far_delta, near, image_one = lax.optimization_barrier((far_delta, near, image_one))
    deltas += [far_delta, shift(far_delta, "c", 1)]
    image_two, block = call(
        last_image_kernel, "last_image", [((1024, 512), F32), ((8, 128), F32)], near, *rows[2:], *deltas[2:], sums
    )
    got = lax.all_to_all(jnp.broadcast_to(block[None], (128, 8, 128)), NAMES, 0, 0, tiled=True)
    whole = lambda *s: pl.BlockSpec(s, lambda i: (0,) * len(s))
    band = pl.BlockSpec((256, 512), lambda i: (i, 0))
    next_vector, coefficients = pl.pallas_call(
        final_kernel,
        grid=(4,),
        out_shape=[jax.ShapeDtypeStruct((1024, 512), F32), jax.ShapeDtypeStruct((4,), F32)],
        in_specs=[whole(128, 8, 128), whole(8, 128), band, band, band],
        out_specs=[band, SM],
        compiler_params=pltpu.CompilerParams(vmem_limit_bytes=16 * MIB),
        name="final",
    )(got, scalars, start, image_one, image_two)
    return (coefficients, next_vector)


def solution(mesh):
    inner = Mesh(mesh.devices.reshape([n for _, n in AXES]), NAMES)
    dp, fsdp = ("yh", "c"), ("x", "z", "yl")
    in_specs = (P(dp, fsdp), P(None, fsdp), P(None, fsdp), P(fsdp, None), P(dp, fsdp), P(dp, fsdp))
    out_specs = (P(), P(dp, fsdp))
    return jax.shard_map(shards, mesh=inner, in_specs=in_specs, out_specs=out_specs, check_vma=False)
```

```python
import jax
import jax.numpy as jnp
from jax import lax
from jax.experimental import pallas as pl
from jax.experimental.pallas import tpu as pltpu
from jax.sharding import Mesh
from jax.sharding import PartitionSpec as P

D = 4096
FF = 16384
EPS = 1e-06
TOKENS = 2048
SCALE_INV = 1.0 / (D * FF)
AXES = (("yh", 2), ("c", 2), ("x", 4), ("z", 4), ("yl", 2))
NAMES = tuple(name for name, _ in AXES)
SIZES = dict(AXES)
BF = jnp.bfloat16
F32 = jnp.float32
MIB = 1024 * 1024
VM = pl.BlockSpec(memory_space=pltpu.VMEM)
SM = pl.BlockSpec(memory_space=pltpu.SMEM)


def shift(value, axis, by):
    n = SIZES[axis]
    return lax.ppermute(value, axis, [((i + by) % n, i) for i in range(n)])


def from_y(v):
    pairs = []
    for y in range(4):
        for c in range(2):
            src = (y + (1 if c == 0 else 3)) % 4
            pairs.append(((src // 2 * 2 + c) * 2 + src % 2, (y // 2 * 2 + c) * 2 + y % 2))
    return lax.ppermute(v, ("yh", "c", "yl"), pairs)


def line(v, a):
    return [v, shift(v, a, 1), shift(v, a, 2), shift(v, a, 3)]


def after(value, *others):
    return lax.optimization_barrier((value, *others))[0]


def call(kernel, name, out, *operands, mib=12, scratch=(), aliases={}):
    specs = [SM if v.dtype == jnp.int32 else VM for v in operands]
    shapes = [jax.ShapeDtypeStruct(s, t) for s, t in out]
    got = pl.pallas_call(
        kernel,
        out_shape=shapes,
        in_specs=specs,
        out_specs=[VM] * len(shapes),
        scratch_shapes=[pltpu.VMEM(s, t) for s, t in scratch],
        input_output_aliases=aliases,
        compiler_params=pltpu.CompilerParams(vmem_limit_bytes=mib * MIB),
        name=name,
    )(*operands)
    return got if len(got) > 1 else got[0]


def gather(v, later=()):
    here, far, later = lax.optimization_barrier((line(v, "x"), shift(v, "z", 2), later))
    here = jnp.stack(here)
    return [here, shift(here, "z", 1), *line(far, "x"), shift(here, "z", 3)], later


def scatter(parts):
    row0, row1, row3, f0, f1, f2, f3 = parts
    up, down = shift(row1, "z", 3), shift(row3, "z", 1)
    far = [f0, shift(f1, "x", 3), shift(f2, "x", 2), shift(f3, "x", 1)]
    block = (f0.shape, BF)
    r0, r1, r2, r3, far = call(add_kernel, "add", [block] * 5, row0, up, down, *far)
    return [r0, shift(r1, "x", 3), shift(r2, "x", 2), shift(r3, "x", 1), shift(far, "z", 2)]


def add_up(*blocks):
    acc = blocks[0].astype(F32)
    for b in blocks[1:]:
        acc = acc + b.astype(F32)
    return acc[:512], undigit(acc[512:]) if acc.shape[0] > 512 else None


def add_kernel(row0, up, down, f0, f1, f2, f3, r0, r1, r2, r3, far):
    def put(out, *blocks):
        acc, sums = add_up(*blocks)
        out[:512, :] = acc.astype(BF)
        if sums is not None:
            out[512:, :] = digits(sums, 128)

    put(far, f0[...], f1[...], f2[...], f3[...])
    for i, r in enumerate((r0, r1, r2, r3)):
        put(r, row0[i], up[i], down[i])


def blocks(pos, refs, width):
    here, nxt, f0, f1, f2, f3, prev = refs
    for i, f in enumerate((f0, f1, f2, f3)):
        yield place(pos, i, 0, width), here[i]
        yield place(pos, i, 1, width), nxt[i]
        yield place(pos, i, 2, width), f[...]
        yield place(pos, i, 3, width), prev[i]


def nt(a, b):
    return lax.dot_general(a, b, (((1,), (1,)), ((), ())), preferred_element_type=F32)


def nn(a, b):
    return jnp.dot(a, b, preferred_element_type=F32)


def place(pos, i, j, width):
    return pl.multiple_of((lax.rem(pos[0] + i, 4) * 4 + lax.rem(pos[1] + j, 4)) * width, width)


def total(v):
    return jnp.sum(v, axis=(0, 1), keepdims=True) * SCALE_INV


def row_of(values, rows, width):
    index = lax.broadcasted_iota(jnp.int32, (rows, width), 0)
    out = jnp.zeros((rows, width), F32)
    for i, v in enumerate(values):
        out = jnp.where(index == i, jnp.broadcast_to(v, (rows, width)), out)
    return out


def digits(values, width):
    rows = []
    for v in values:
        for _ in range(3):
            d = v.astype(BF).astype(F32)
            rows.append(d)
            v = v - d
    return row_of(rows, 16, width).astype(BF)


def undigit(rows):
    return [rows[3 * i:3 * i + 1] + rows[3 * i + 1:3 * i + 2] + rows[3 * i + 2:3 * i + 3] for i in range(3)]


def cast_kernel(start, out, squares):
    acc = jnp.zeros((8, 512), F32)
    for i in range(0, 1024, 8):
        v = start[i:i + 8, :]
        acc = acc + v * v
    out[...] = start[...].astype(BF)
    squares[...] = acc


def split_kernel(pos, down, near, keep, send):
    del near
    yl = pos[2]
    mine = pl.ds(pl.multiple_of(pos[8] * 256, 256), 256)
    for b in range(16):
        keep[:, b * 128:(b + 1) * 128] = down[:, pl.ds(pl.multiple_of((2 * b + yl) * 128, 128), 128)]
        send[:, b * 128:(b + 1) * 128] = down[mine, pl.ds(pl.multiple_of((2 * b + 1 - yl) * 128, 128), 128)]


def join_kernel(pos, mine, theirs, out):
    out[pl.ds(pl.multiple_of(pos[8] * 256, 256), 256), :] = mine[...]
    out[pl.ds(pl.multiple_of((1 - pos[8]) * 256, 256), 256), :] = theirs[...]


def front_half(pos, rows, feats, gate_w, up_w, starts, slope, tangent, pushed):
    acc = jnp.zeros((256, 512), F32)
    for k in range(4):
        cols = pl.multiple_of(pos[4 + k] * 1024, 1024)
        acc = acc + nn(feats[rows, pl.ds(cols, 1024)], starts[k][...])
    tangent[rows] = acc
    gate = nn(feats[rows], gate_w[...])
    sigma = 1.0 / (1.0 + jnp.exp(-gate))
    slope[rows] = sigma * (1.0 + gate * (1.0 - sigma)) * nn(feats[rows], up_w[...])
    pushed[...] = (slope[rows] * acc).astype(BF)


def front_first_kernel(pos, *refs):
    gate_w, up_w = refs[7:9]
    starts = refs[9:13]
    feats, slope, tangent, pushed = refs[13:]
    for col, block in blocks(pos, refs[:7], 256):
        feats[:, pl.ds(col, 256)] = block
    front_half(pos, slice(0, 256), feats, gate_w, up_w, starts, slope, tangent, pushed)


def front_second_kernel(pos, feats, gate_w, up_w, s0, s1, s2, s3, slope_in, tangent_in, slope, tangent, pushed):
    front_half(pos, slice(256, 512), feats, gate_w, up_w, (s0, s1, s2, s3), slope, tangent, pushed)


def push_half(pos, rows, own, other, keep, recv, row0, row1, row3, fars, strip):
    x, z = pos[0], pos[1]
    for i, f in enumerate(fars):
        cols = pl.ds(pl.multiple_of(lax.rem(x + i, 4) * 512, 512), 512)
        strip[...] = (nn(own[:256], keep[:, cols]) + nn(other[:256], recv[:, cols])).astype(BF)
        for j, out in enumerate((row0.at[i], row1.at[i], f, row3.at[i])):
            out[rows] = strip[:, pl.ds(pl.multiple_of(lax.rem(z + j, 4) * 128, 128), 128)]


def push_first_kernel(pos, own, other, keep, recv, row0, row1, row3, f0, f1, f2, f3, strip):
    push_half(pos, slice(0, 256), own, other, keep, recv, row0, row1, row3, (f0, f1, f2, f3), strip)
    if own.shape[0] > 256:
        extra = digits(undigit(own[256:].astype(F32) + other[256:].astype(F32)), 512)[:, :128]
        for i in range(4):
            for out in (row0, row1, row3):
                out[i, 512:] = extra
        for f in (f0, f1, f2, f3):
            f[512:] = extra


def push_second_kernel(pos, own, other, keep, recv, *refs):
    row0, row1, row3, f0, f1, f2, f3, strip = refs[7:]
    push_half(pos, slice(256, 512), own, other, keep, recv, row0, row1, row3, (f0, f1, f2, f3), strip)


def push_down(pos, pushed, other, keep, recv, row, block):
    out = [(row, BF)] * 3 + [(block, BF)] * 4
    scratch = [((256, 512), BF)]
    parts = call(push_first_kernel, "push_first", out, pos, pushed[0], other[0], keep, recv, scratch=scratch)
    return call(
        push_second_kernel,
        "push_second",
        out,
        pos, pushed[1], other[1], keep, recv, *parts,
        scratch=scratch,
        aliases={5 + i: i for i in range(7)},
    )


def weigh_first_kernel(b0, b1, b2, b3, b4, curvature, moved, weighted):
    acc, _ = add_up(b0[...], b1[...], b2[...], b3[...], b4[...])
    moved[...] = acc
    weighted[...] = (curvature[...] * acc / TOKENS).astype(BF)


def weigh_second_kernel(b0, b1, b2, b3, b4, curvature, moved, weighted, scalars):
    acc, (ss, sw, dd) = add_up(b0[...], b1[...], b2[...], b3[...], b4[...])
    alpha = sw / (ss + EPS)
    scale = lax.rsqrt(dd + 1e-30) * (1.0 / 1024.0)
    weighted[...] = (curvature[...] * ((acc - alpha * moved[...]) * scale) / TOKENS).astype(BF)
    scalars[...] = row_of([ss, sw, scale], 8, 128)


def back_kernel(pos, *refs):
    recv, full, send_a, send_b = refs[7:]
    for col, block in blocks(pos, refs[:7], 128):
        full[:, pl.ds(col, 128)] = block
    send = nt(full[...], recv[...]).astype(BF)
    send_a[...] = send[:256]
    send_b[...] = send[256:]


def own_back_kernel(full, keep, out):
    out[...] = nt(full[...], keep[...])


def delta_first_kernel(own, got_a, got_b, slope, tangent, squares, out):
    out[:256, :] = ((own[:256] + got_a[...].astype(F32)) * slope[:256]).astype(BF)
    out[256:512, :] = ((own[256:] + got_b[...].astype(F32)) * slope[256:]).astype(BF)
    delta = out[:512, :].astype(F32)
    sums = [total(squares[...]), total(tangent[...] * delta), total(delta * (delta * 1.0))]
    out[512:, :] = digits([jnp.broadcast_to(v, (1, 512)) for v in sums], 512)


def delta_second_kernel(own, got_a, got_b, slope, tan_start, tan_image, delta_one, out, sums):
    out[:256, :] = ((own[:256] + got_a[...].astype(F32)) * slope[:256]).astype(BF)
    out[256:, :] = ((own[256:] + got_b[...].astype(F32)) * slope[256:]).astype(BF)
    delta = out[...].astype(F32)
    ww = total(tan_image[...] * delta_one[:512].astype(F32))
    sums[...] = row_of([ww, total(tan_start[...] * delta), total(tan_image[...] * delta)], 8, 128)


def own_gram_kernel(feats, out):
    out[...] = nt(feats[...], feats[...])


def quarter_kernel(pos, feats, out):
    out[...] = feats[pl.ds(pl.multiple_of(pos[9] * 128, 128), 128), :]


def their_rows_kernel(pos, feats, out):
    out[...] = feats[:, pl.ds(pl.multiple_of((1 - pos[10]) * 2048, 2048), 2048)]


def core_gram_kernel(feats, one, out):
    out[...] = nt(feats[...], one[...])


def far_gram_kernel(feats, one, two, out):
    out[:, :128] = nt(feats[...], one[...])
    out[:, 128:] = nt(feats[...], two[...])


def rows_kernel(pos, feats, out):
    out[...] = feats[:, pl.ds(pl.multiple_of(pos[3] * 1024, 1024), 1024)].T


def far_rows_kernel(pos, feats, out, other):
    c = pos[8]
    out[...] = feats[:, pl.ds(pl.multiple_of(c * 1024, 1024), 1024)].T
    other[...] = feats[:, pl.ds(pl.multiple_of((1 - c) * 1024, 1024), 1024)].T


def gram_split_kernel(pos, own, core, p0, p1, p2, p3, high, low):
    def put(cols, v):
        top = v.astype(BF)
        high[:, cols] = top
        low[:, cols] = (v - top.astype(F32)).astype(BF)

    put(slice(0, 512), own[...])
    put(slice(512, 1024), core[...])
    for i, p in enumerate((p0, p1, p2, p3)):
        q = lax.rem(pos[9] + i, 4) * 128
        put(pl.ds(pl.multiple_of(1024 + q, 128), 128), p[:, :128])
        put(pl.ds(pl.multiple_of(1536 + q, 128), 128), p[:, 128:])


def near_tangent_kernel(high, low, d0, d1, out):
    acc = nn(high[:, :512], d0[:512]) + nn(low[:, :512], d0[:512])
    out[...] = acc + nn(high[:, 512:1024], d1[:512]) + nn(low[:, 512:1024], d1[:512])


def far_tangent_kernel(near, high, low, d0, d1, d2, d3, slope, tangent, pushed_a, pushed_b):
    acc = near[...] + nn(high[:, 1024:1536], d2[:512]) + nn(low[:, 1024:1536], d2[:512])
    acc = acc + nn(high[:, 1536:], d3[:512]) + nn(low[:, 1536:], d3[:512])
    tangent[...] = acc
    pushed_a[:256, :] = (slope[:256] * acc[:256]).astype(BF)
    pushed_b[...] = (slope[256:] * acc[256:]).astype(BF)
    rows = d0[512:].astype(F32) + d1[512:].astype(F32) + d2[512:].astype(F32) + d3[512:].astype(F32)
    pushed_a[256:, :] = digits(undigit(rows), 512)


def near_image_kernel(r0, r1, d0, d1, out):
    out[...] = nn(r0[...], d0[:512]) + nn(r1[...], d1[:512])


def far_image_kernel(near, r2, r3, d2, d3, out):
    out[...] = near[...] + nn(r2[...], d2[:512]) + nn(r3[...], d3[:512])


def last_image_kernel(near, r2, r3, d2, d3, sums, out, block):
    acc = near[...] + nn(r2[...], d2[...]) + nn(r3[...], d3[...])
    out[...] = acc
    index = lax.broadcasted_iota(jnp.int32, (8, 128), 0)
    block[...] = jnp.where(index == 3, jnp.broadcast_to(total(acc * acc), (8, 128)), sums[...])


def final_kernel(got, scalars, start, image_one, image_two, out, coefficients):
    acc = got[0]
    for i in range(1, 128):
        acc = acc + got[i]
    ss, sw, scale = scalars[0:1], scalars[1:2], scalars[2:3]
    ww, uz, wz, zz = acc[0:1], acc[1:2], acc[2:3], acc[3:4]
    norm_sq = ss + EPS
    norm = jnp.sqrt(norm_sq)
    alpha_one = sw / norm_sq
    one_one = ss / norm_sq
    resid_sq = jnp.maximum(ww / norm_sq - alpha_one * alpha_one * (2.0 - one_one), 0.0)
    beta_one = jnp.sqrt(resid_sq + EPS)
    second = 1.0 / (norm * beta_one)
    image = second / scale
    alpha_two = image * second * (wz - alpha_one * uz)
    cross = image * uz / norm
    two_two = resid_sq / (resid_sq + EPS)
    one_two = alpha_one * (1.0 - one_one) / beta_one
    last_sq = (
        image * image * zz
        - alpha_two * alpha_two * (2.0 - two_two)
        - cross * cross * (2.0 - one_one)
        + 2.0 * alpha_two * cross * one_two
    )
    beta_two = jnp.sqrt(jnp.maximum(last_sq, 0.0) + EPS)
    for i, v in enumerate((alpha_one, beta_one, alpha_two, beta_two)):
        coefficients[i] = v[0, 0]
    f_two = image / beta_two
    f_one = -alpha_two * second / beta_two
    f_start = (alpha_two * alpha_one / beta_one - cross) / (norm * beta_two)
    for k in range(4):
        cols = slice(k * 128, (k + 1) * 128)
        out[:, cols] = f_two * image_two[:, cols] + f_one * image_one[:, cols] + f_start * start[:, cols]


def shards(tokens, gate_weight, up_weight, down_weight, curvature, start):
    yh, c, x, z, yl = [lax.axis_index(n).astype(jnp.int32) for n in NAMES]
    dp = yh * 2 + c
    quarter_of = lax.rem(x + 2 * z, 4)
    pos = jnp.stack(
        [x, z, yl, dp, dp, yh * 2 + 1 - c, (1 - yh) * 2 + c, (1 - yh) * 2 + 1 - c, c, quarter_of, yh]
    )

    other = shift(tokens, "yl", 1)
    start_b, squares = call(cast_kernel, "cast_start", [((1024, 512), BF), ((8, 512), F32)], start)
    other, start_b = lax.optimization_barrier((other, start_b))
    far_start = shift(start_b, "yh", 1)
    starts = [start_b, shift(start_b, "c", 1), far_start, shift(far_start, "c", 1)]
    pair = jnp.where(
        yl == 0, jnp.concatenate([tokens, other], axis=1), jnp.concatenate([other, tokens], axis=1)
    )
    keep, send = call(
        split_kernel,
        "split_down",
        [((512, 2048), BF), ((256, 2048), BF)],
        pos, after(down_weight, pair), up_weight,
    )
    pieces, send = gather(pair, send)
    recv = from_y(after(send, far_start))
    recv, pieces = lax.optimization_barrier((recv, pieces))
    half = ((256, 512), BF)
    square = ((512, 512), F32)
    feats, slope, tan_start, pushed_a = call(
        front_first_kernel,
        "front_first",
        [((512, D), BF), square, square, half],
        pos, *pieces, gate_weight, up_weight, *starts,
        mib=16,
    )
    slope, tan_start, pushed_b = call(
        front_second_kernel,
        "front_second",
        [square, square, half],
        pos, feats, gate_weight, up_weight, *starts, slope, tan_start,
        aliases={8: 0, 9: 1},
    )
    pushed = [pushed_a, pushed_b]
    recv = call(join_kernel, "join", [((512, 2048), BF)], pos, recv, shift(recv, "c", 1))
    row, block = (4, 512, 128), (512, 128)

    other = [shift(v, "yl", 1) for v in pushed]
    feats_c = shift(after(feats, recv), "c", 1)
    own_gram = call(own_gram_kernel, "own_gram", [((512, 512), F32)], after(feats, pushed))
    quarter = call(quarter_kernel, "quarter", [((128, D), BF)], pos, after(feats, *pushed))
    other[0], own_gram, feats_c, quarter = lax.optimization_barrier((other[0], own_gram, feats_c, quarter))
    parts = push_down(pos, pushed, other, keep, recv, row, block)
    quarter = shift(after(quarter, parts[0]), "yh", 1)
    parts = scatter(parts)
    moved, weighted = call(
        weigh_first_kernel, "weigh", [((512, 128), F32), ((512, 128), BF)], *parts, curvature
    )
    quarter, weighted = lax.optimization_barrier((quarter, weighted))
    pieces, quarter_c = gather(weighted, shift(quarter, "c", 1))
    far_gram = call(far_gram_kernel, "far_gram", [((512, 256), F32)], feats, quarter, quarter_c)
    recv_one, far_gram = lax.optimization_barrier((recv, far_gram))
    full, *send = call(
        back_kernel, "back_other", [((512, 2048), BF), ((256, 512), BF), ((256, 512), BF)], pos, *pieces, recv_one
    )
    got = [shift(v, "yl", 1) for v in send]
    far_gram = after(far_gram, *send)
    far_grams = [far_gram, shift(far_gram, "x", 1), shift(far_gram, "z", 1), shift(far_gram, "x", 3)]
    own = call(own_back_kernel, "back_own", [((512, 512), F32)], full, keep)
    got, far_grams = lax.optimization_barrier((got, far_grams))
    delta = call(delta_first_kernel, "delta", [((528, 512), BF)], own, *got, slope, tan_start, squares)
    deltas = [delta, shift(delta, "c", 1)]
    far_delta = shift(delta, "yh", 1)
    core_gram = call(core_gram_kernel, "core_gram", [((512, 512), F32)], after(feats, delta), feats_c)
    high, low = call(
        gram_split_kernel,
        "gram_split",
        [((512, 2048), BF)] * 2,
        pos, after(own_gram, delta), core_gram, *far_grams,
    )
    near = call(near_tangent_kernel, "near_tangent", [((512, 512), F32)], high, low, *deltas)
    far_delta, near = lax.optimization_barrier((far_delta, near))
    deltas += [far_delta, shift(far_delta, "c", 1)]
    tan_image, *pushed = call(
        far_tangent_kernel,
        "far_tangent",
        [((512, 512), F32), ((272, 512), BF), ((256, 512), BF)],
        near, high, low, *deltas, slope,
    )

    row, block = (4, 528, 128), (528, 128)
    other = [shift(v, "yl", 1) for v in pushed]
    first_deltas = deltas
    rows = [call(rows_kernel, "rows", [((1024, 512), BF)], pos, after(f, *pushed)) for f in (feats, feats_c)]
    near_one = call(near_image_kernel, "near_image", [((1024, 512), F32)], *rows, *first_deltas[:2])
    theirs = call(their_rows_kernel, "their_rows", [((512, 2048), BF)], pos, after(feats, *pushed))
    other[0], near_one, theirs = lax.optimization_barrier((other[0], near_one, theirs))
    parts = push_down(pos, pushed, other, keep, recv, row, block)
    far_rows = shift(after(theirs, parts[0]), "yh", 1)
    parts = scatter(parts)
    weighted, scalars = call(
        weigh_second_kernel, "weigh", [((512, 128), BF), ((8, 128), F32)], *parts, curvature, moved
    )
    pieces, _ = gather(weighted)
    full, *send = call(
        back_kernel, "back_other", [((512, 2048), BF), ((256, 512), BF), ((256, 512), BF)], pos, *pieces, recv
    )
    got = [shift(v, "yl", 1) for v in send]
    own = call(own_back_kernel, "back_own", [((512, 512), F32)], full, keep)
    mine, theirs = call(far_rows_kernel, "far_rows", [((1024, 512), BF)] * 2, pos, after(far_rows, *send))
    got, mine, theirs = lax.optimization_barrier((got, mine, theirs))
    rows += [mine, shift(theirs, "c", 1)]
    delta, sums = call(
        delta_second_kernel,
        "delta",
        [((512, 512), BF), ((8, 128), F32)],
        own, *got, slope, tan_start, tan_image, delta,
    )
    deltas = [delta, shift(delta, "c", 1)]
    far_delta = shift(delta, "yh", 1)
    image_one = call(
        far_image_kernel, "far_image", [((1024, 512), F32)], after(near_one, delta), *rows[2:], *first_deltas[2:]
    )
    near = call(near_image_kernel, "near_image", [((1024, 512), F32)], *rows[:2], *deltas)
    far_delta, near, image_one = lax.optimization_barrier((far_delta, near, image_one))
    deltas += [far_delta, shift(far_delta, "c", 1)]
    image_two, block = call(
        last_image_kernel, "last_image", [((1024, 512), F32), ((8, 128), F32)], near, *rows[2:], *deltas[2:], sums
    )
    got = lax.all_to_all(jnp.broadcast_to(block[None], (128, 8, 128)), NAMES, 0, 0, tiled=True)
    whole = lambda *s: pl.BlockSpec(s, lambda i: (0,) * len(s))
    band = pl.BlockSpec((256, 512), lambda i: (i, 0))
    next_vector, coefficients = pl.pallas_call(
        final_kernel,
        grid=(4,),
        out_shape=[jax.ShapeDtypeStruct((1024, 512), F32), jax.ShapeDtypeStruct((4,), F32)],
        in_specs=[whole(128, 8, 128), whole(8, 128), band, band, band],
        out_specs=[band, SM],
        compiler_params=pltpu.CompilerParams(vmem_limit_bytes=16 * MIB),
        name="final",
    )(got, scalars, start, image_one, image_two)
    return (coefficients, next_vector)


def solution(mesh):
    inner = Mesh(mesh.devices.reshape([n for _, n in AXES]), NAMES)
    dp, fsdp = ("yh", "c"), ("x", "z", "yl")
    in_specs = (P(dp, fsdp), P(None, fsdp), P(None, fsdp), P(fsdp, None), P(dp, fsdp), P(dp, fsdp))
    out_specs = (P(), P(dp, fsdp))
    return jax.shard_map(shards, mesh=inner, in_specs=in_specs, out_specs=out_specs, check_vma=False)
```

```python
import jax
import jax.numpy as jnp
from jax import lax
from jax.experimental import pallas as pl
from jax.experimental.pallas import tpu as pltpu
from jax.sharding import Mesh
from jax.sharding import PartitionSpec as P

D = 4096
FF = 16384
EPS = 1e-06
TOKENS = 2048
SCALE_INV = 1.0 / (D * FF)
AXES = (("yh", 2), ("c", 2), ("x", 4), ("z", 4), ("yl", 2))
NAMES = tuple(name for name, _ in AXES)
SIZES = dict(AXES)
BF = jnp.bfloat16
F32 = jnp.float32
MIB = 1024 * 1024
VM = pl.BlockSpec(memory_space=pltpu.VMEM)
SM = pl.BlockSpec(memory_space=pltpu.SMEM)


def shift(value, axis, by):
    n = SIZES[axis]
    return lax.ppermute(value, axis, [((i + by) % n, i) for i in range(n)])


def from_y(v):
    pairs = []
    for y in range(4):
        for c in range(2):
            src = (y + (1 if c == 0 else 3)) % 4
            pairs.append(((src // 2 * 2 + c) * 2 + src % 2, (y // 2 * 2 + c) * 2 + y % 2))
    return lax.ppermute(v, ("yh", "c", "yl"), pairs)


def line(v, a):
    return [v, shift(v, a, 1), shift(v, a, 2), shift(v, a, 3)]


def after(value, *others):
    return lax.optimization_barrier((value, *others))[0]


def call(kernel, name, out, *operands, mib=12, scratch=(), aliases={}):
    specs = [SM if v.dtype == jnp.int32 else VM for v in operands]
    shapes = [jax.ShapeDtypeStruct(s, t) for s, t in out]
    got = pl.pallas_call(
        kernel,
        out_shape=shapes,
        in_specs=specs,
        out_specs=[VM] * len(shapes),
        scratch_shapes=[pltpu.VMEM(s, t) for s, t in scratch],
        input_output_aliases=aliases,
        compiler_params=pltpu.CompilerParams(vmem_limit_bytes=mib * MIB),
        name=name,
    )(*operands)
    return got if len(got) > 1 else got[0]


def gather(v, later=()):
    here, far, later = lax.optimization_barrier((line(v, "x"), shift(v, "z", 2), later))
    here = jnp.stack(here)
    return [here, shift(here, "z", 1), *line(far, "x"), shift(here, "z", 3)], later


def scatter(parts):
    row0, row1, row3, f0, f1, f2, f3 = parts
    up, down = shift(row1, "z", 3), shift(row3, "z", 1)
    far = [f0, shift(f1, "x", 3), shift(f2, "x", 2), shift(f3, "x", 1)]
    block = (f0.shape, BF)
    r0, r1, r2, r3, far = call(add_kernel, "add", [block] * 5, row0, up, down, *far)
    return [r0, shift(r1, "x", 3), shift(r2, "x", 2), shift(r3, "x", 1), shift(far, "z", 2)]


def add_up(*blocks):
    acc = blocks[0].astype(F32)
    for b in blocks[1:]:
        acc = acc + b.astype(F32)
    return acc[:512], undigit(acc[512:]) if acc.shape[0] > 512 else None


def add_kernel(row0, up, down, f0, f1, f2, f3, r0, r1, r2, r3, far):
    def put(out, *blocks):
        acc, sums = add_up(*blocks)
        out[:512, :] = acc.astype(BF)
        if sums is not None:
            out[512:, :] = digits(sums, 128)

    put(far, f0[...], f1[...], f2[...], f3[...])
    for i, r in enumerate((r0, r1, r2, r3)):
        put(r, row0[i], up[i], down[i])


def blocks(pos, refs, width):
    here, nxt, f0, f1, f2, f3, prev = refs
    for i, f in enumerate((f0, f1, f2, f3)):
        yield place(pos, i, 0, width), here[i]
        yield place(pos, i, 1, width), nxt[i]
        yield place(pos, i, 2, width), f[...]
        yield place(pos, i, 3, width), prev[i]


def nt(a, b):
    return lax.dot_general(a, b, (((1,), (1,)), ((), ())), preferred_element_type=F32)


def nn(a, b):
    return jnp.dot(a, b, preferred_element_type=F32)


def place(pos, i, j, width):
    return pl.multiple_of((lax.rem(pos[0] + i, 4) * 4 + lax.rem(pos[1] + j, 4)) * width, width)


def total(v):
    return jnp.sum(v, axis=(0, 1), keepdims=True) * SCALE_INV


def row_of(values, rows, width):
    index = lax.broadcasted_iota(jnp.int32, (rows, width), 0)
    out = jnp.zeros((rows, width), F32)
    for i, v in enumerate(values):
        out = jnp.where(index == i, jnp.broadcast_to(v, (rows, width)), out)
    return out


def digits(values, width):
    rows = []
    for v in values:
        for _ in range(3):
            d = v.astype(BF).astype(F32)
            rows.append(d)
            v = v - d
    return row_of(rows, 16, width).astype(BF)


def undigit(rows):
    return [rows[3 * i:3 * i + 1] + rows[3 * i + 1:3 * i + 2] + rows[3 * i + 2:3 * i + 3] for i in range(3)]


def cast_kernel(start, out, squares):
    acc = jnp.zeros((8, 512), F32)
    for i in range(0, 1024, 8):
        v = start[i:i + 8, :]
        acc = acc + v * v
    out[...] = start[...].astype(BF)
    squares[...] = acc


def split_kernel(pos, down, near, keep, send):
    del near
    yl = pos[2]
    mine = pl.ds(pl.multiple_of(pos[8] * 256, 256), 256)
    for b in range(16):
        keep[:, b * 128:(b + 1) * 128] = down[:, pl.ds(pl.multiple_of((2 * b + yl) * 128, 128), 128)]
        send[:, b * 128:(b + 1) * 128] = down[mine, pl.ds(pl.multiple_of((2 * b + 1 - yl) * 128, 128), 128)]


def join_kernel(pos, mine, theirs, out):
    out[pl.ds(pl.multiple_of(pos[8] * 256, 256), 256), :] = mine[...]
    out[pl.ds(pl.multiple_of((1 - pos[8]) * 256, 256), 256), :] = theirs[...]


def front_half(pos, rows, feats, gate_w, up_w, starts, slope, tangent, pushed):
    acc = jnp.zeros((256, 512), F32)
    for k in range(4):
        cols = pl.multiple_of(pos[4 + k] * 1024, 1024)
        acc = acc + nn(feats[rows, pl.ds(cols, 1024)], starts[k][...])
    tangent[rows] = acc
    gate = nn(feats[rows], gate_w[...])
    sigma = 1.0 / (1.0 + jnp.exp(-gate))
    slope[rows] = sigma * (1.0 + gate * (1.0 - sigma)) * nn(feats[rows], up_w[...])
    pushed[...] = (slope[rows] * acc).astype(BF)


def front_first_kernel(pos, *refs):
    gate_w, up_w = refs[7:9]
    starts = refs[9:13]
    feats, slope, tangent, pushed = refs[13:]
    for col, block in blocks(pos, refs[:7], 256):
        feats[:, pl.ds(col, 256)] = block
    front_half(pos, slice(0, 256), feats, gate_w, up_w, starts, slope, tangent, pushed)


def front_second_kernel(pos, feats, gate_w, up_w, s0, s1, s2, s3, slope_in, tangent_in, slope, tangent, pushed):
    front_half(pos, slice(256, 512), feats, gate_w, up_w, (s0, s1, s2, s3), slope, tangent, pushed)


def push_half(pos, rows, own, other, keep, recv, row0, row1, row3, fars, strip):
    x, z = pos[0], pos[1]
    for i, f in enumerate(fars):
        cols = pl.ds(pl.multiple_of(lax.rem(x + i, 4) * 512, 512), 512)
        strip[...] = (nn(own[:256], keep[:, cols]) + nn(other[:256], recv[:, cols])).astype(BF)
        for j, out in enumerate((row0.at[i], row1.at[i], f, row3.at[i])):
            out[rows] = strip[:, pl.ds(pl.multiple_of(lax.rem(z + j, 4) * 128, 128), 128)]


def push_first_kernel(pos, own, other, keep, recv, row0, row1, row3, f0, f1, f2, f3, strip):
    push_half(pos, slice(0, 256), own, other, keep, recv, row0, row1, row3, (f0, f1, f2, f3), strip)
    if own.shape[0] > 256:
        extra = digits(undigit(own[256:].astype(F32) + other[256:].astype(F32)), 512)[:, :128]
        for i in range(4):
            for out in (row0, row1, row3):
                out[i, 512:] = extra
        for f in (f0, f1, f2, f3):
            f[512:] = extra


def push_second_kernel(pos, own, other, keep, recv, *refs):
    row0, row1, row3, f0, f1, f2, f3, strip = refs[7:]
    push_half(pos, slice(256, 512), own, other, keep, recv, row0, row1, row3, (f0, f1, f2, f3), strip)


def push_down(pos, pushed, other, keep, recv, row, block):
    out = [(row, BF)] * 3 + [(block, BF)] * 4
    scratch = [((256, 512), BF)]
    parts = call(push_first_kernel, "push_first", out, pos, pushed[0], other[0], keep, recv, scratch=scratch)
    return call(
        push_second_kernel,
        "push_second",
        out,
        pos, pushed[1], other[1], keep, recv, *parts,
        scratch=scratch,
        aliases={5 + i: i for i in range(7)},
    )


def weigh_first_kernel(b0, b1, b2, b3, b4, curvature, moved, weighted):
    acc, _ = add_up(b0[...], b1[...], b2[...], b3[...], b4[...])
    moved[...] = acc
    weighted[...] = (curvature[...] * acc / TOKENS).astype(BF)


def weigh_second_kernel(b0, b1, b2, b3, b4, curvature, moved, weighted, scalars):
    acc, (ss, sw, dd) = add_up(b0[...], b1[...], b2[...], b3[...], b4[...])
    alpha = sw / (ss + EPS)
    scale = lax.rsqrt(dd + 1e-30) * (1.0 / 1024.0)
    weighted[...] = (curvature[...] * ((acc - alpha * moved[...]) * scale) / TOKENS).astype(BF)
    scalars[...] = row_of([ss, sw, scale], 8, 128)


def back_kernel(pos, *refs):
    recv, full, send_a, send_b = refs[7:]
    for col, block in blocks(pos, refs[:7], 128):
        full[:, pl.ds(col, 128)] = block
    send = nt(full[...], recv[...]).astype(BF)
    send_a[...] = send[:256]
    send_b[...] = send[256:]


def own_back_kernel(full, keep, out):
    out[...] = nt(full[...], keep[...])


def delta_first_kernel(own, got_a, got_b, slope, tangent, squares, out):
    out[:256, :] = ((own[:256] + got_a[...].astype(F32)) * slope[:256]).astype(BF)
    out[256:512, :] = ((own[256:] + got_b[...].astype(F32)) * slope[256:]).astype(BF)
    delta = out[:512, :].astype(F32)
    sums = [total(squares[...]), total(tangent[...] * delta), total(delta * (delta * 1.0))]
    out[512:, :] = digits([jnp.broadcast_to(v, (1, 512)) for v in sums], 512)


def delta_second_kernel(own, got_a, got_b, slope, tan_start, tan_image, delta_one, out, sums):
    out[:256, :] = ((own[:256] + got_a[...].astype(F32)) * slope[:256]).astype(BF)
    out[256:, :] = ((own[256:] + got_b[...].astype(F32)) * slope[256:]).astype(BF)
    delta = out[...].astype(F32)
    ww = total(tan_image[...] * delta_one[:512].astype(F32))
    sums[...] = row_of([ww, total(tan_start[...] * delta), total(tan_image[...] * delta)], 8, 128)


def own_gram_kernel(feats, out):
    out[...] = nt(feats[...], feats[...])


def quarter_kernel(pos, feats, out):
    out[...] = feats[pl.ds(pl.multiple_of(pos[9] * 128, 128), 128), :]


def their_rows_kernel(pos, feats, out):
    out[...] = feats[:, pl.ds(pl.multiple_of((1 - pos[10]) * 2048, 2048), 2048)]


def core_gram_kernel(feats, one, out):
    out[...] = nt(feats[...], one[...])


def far_gram_kernel(feats, one, two, out):
    out[:, :128] = nt(feats[...], one[...])
    out[:, 128:] = nt(feats[...], two[...])


def rows_kernel(pos, feats, out):
    out[...] = feats[:, pl.ds(pl.multiple_of(pos[3] * 1024, 1024), 1024)].T


def far_rows_kernel(pos, feats, out, other):
    c = pos[8]
    out[...] = feats[:, pl.ds(pl.multiple_of(c * 1024, 1024), 1024)].T
    other[...] = feats[:, pl.ds(pl.multiple_of((1 - c) * 1024, 1024), 1024)].T


def gram_split_kernel(pos, own, core, p0, p1, p2, p3, high, low):
    def put(cols, v):
        top = v.astype(BF)
        high[:, cols] = top
        low[:, cols] = (v - top.astype(F32)).astype(BF)

    put(slice(0, 512), own[...])
    put(slice(512, 1024), core[...])
    for i, p in enumerate((p0, p1, p2, p3)):
        q = lax.rem(pos[9] + i, 4) * 128
        put(pl.ds(pl.multiple_of(1024 + q, 128), 128), p[:, :128])
        put(pl.ds(pl.multiple_of(1536 + q, 128), 128), p[:, 128:])


def near_tangent_kernel(high, low, d0, d1, out):
    acc = nn(high[:, :512], d0[:512]) + nn(low[:, :512], d0[:512])
    out[...] = acc + nn(high[:, 512:1024], d1[:512]) + nn(low[:, 512:1024], d1[:512])


def middle_tangent_kernel(near, high, low, d2, out):
    out[...] = near[...] + nn(high[:, 1024:1536], d2[:512]) + nn(low[:, 1024:1536], d2[:512])


def far_tangent_kernel(near, high, low, d0, d1, d2, d3, slope, tangent, pushed_a, pushed_b):
    acc = near[...] + nn(high[:, 1536:], d3[:512]) + nn(low[:, 1536:], d3[:512])
    tangent[...] = acc
    pushed_a[:256, :] = (slope[:256] * acc[:256]).astype(BF)
    pushed_b[...] = (slope[256:] * acc[256:]).astype(BF)
    rows = d0[512:].astype(F32) + d1[512:].astype(F32) + d2[512:].astype(F32) + d3[512:].astype(F32)
    pushed_a[256:, :] = digits(undigit(rows), 512)


def near_image_kernel(r0, r1, d0, d1, out):
    out[...] = nn(r0[...], d0[:512]) + nn(r1[...], d1[:512])


def far_image_kernel(near, r2, r3, d2, d3, out):
    out[...] = near[...] + nn(r2[...], d2[:512]) + nn(r3[...], d3[:512])


def middle_image_kernel(near, r2, d2, out):
    out[...] = near[...] + nn(r2[...], d2[...])


def last_image_kernel(near, r3, d3, sums, out, block):
    acc = near[...] + nn(r3[...], d3[...])
    out[...] = acc
    index = lax.broadcasted_iota(jnp.int32, (8, 128), 0)
    block[...] = jnp.where(index == 3, jnp.broadcast_to(total(acc * acc), (8, 128)), sums[...])


def final_kernel(got, scalars, start, image_one, image_two, out, coefficients):
    acc = got[0]
    for i in range(1, 128):
        acc = acc + got[i]
    ss, sw, scale = scalars[0:1], scalars[1:2], scalars[2:3]
    ww, uz, wz, zz = acc[0:1], acc[1:2], acc[2:3], acc[3:4]
    norm_sq = ss + EPS
    norm = jnp.sqrt(norm_sq)
    alpha_one = sw / norm_sq
    one_one = ss / norm_sq
    resid_sq = jnp.maximum(ww / norm_sq - alpha_one * alpha_one * (2.0 - one_one), 0.0)
    beta_one = jnp.sqrt(resid_sq + EPS)
    second = 1.0 / (norm * beta_one)
    image = second / scale
    alpha_two = image * second * (wz - alpha_one * uz)
    cross = image * uz / norm
    two_two = resid_sq / (resid_sq + EPS)
    one_two = alpha_one * (1.0 - one_one) / beta_one
    last_sq = (
        image * image * zz
        - alpha_two * alpha_two * (2.0 - two_two)
        - cross * cross * (2.0 - one_one)
        + 2.0 * alpha_two * cross * one_two
    )
    beta_two = jnp.sqrt(jnp.maximum(last_sq, 0.0) + EPS)
    for i, v in enumerate((alpha_one, beta_one, alpha_two, beta_two)):
        coefficients[i] = v[0, 0]
    f_two = image / beta_two
    f_one = -alpha_two * second / beta_two
    f_start = (alpha_two * alpha_one / beta_one - cross) / (norm * beta_two)
    for k in range(4):
        cols = slice(k * 128, (k + 1) * 128)
        out[:, cols] = f_two * image_two[:, cols] + f_one * image_one[:, cols] + f_start * start[:, cols]


def shards(tokens, gate_weight, up_weight, down_weight, curvature, start):
    yh, c, x, z, yl = [lax.axis_index(n).astype(jnp.int32) for n in NAMES]
    dp = yh * 2 + c
    quarter_of = lax.rem(x + 2 * z, 4)
    pos = jnp.stack(
        [x, z, yl, dp, dp, yh * 2 + 1 - c, (1 - yh) * 2 + c, (1 - yh) * 2 + 1 - c, c, quarter_of, yh]
    )

    other = shift(tokens, "yl", 1)
    start_b, squares = call(cast_kernel, "cast_start", [((1024, 512), BF), ((8, 512), F32)], start)
    other, start_b = lax.optimization_barrier((other, start_b))
    far_start = shift(start_b, "yh", 1)
    starts = [start_b, shift(start_b, "c", 1), far_start, shift(far_start, "c", 1)]
    pair = jnp.where(
        yl == 0, jnp.concatenate([tokens, other], axis=1), jnp.concatenate([other, tokens], axis=1)
    )
    keep, send = call(
        split_kernel,
        "split_down",
        [((512, 2048), BF), ((256, 2048), BF)],
        pos, after(down_weight, pair), up_weight,
    )
    pieces, send = gather(pair, send)
    recv = from_y(after(send, far_start))
    recv, pieces = lax.optimization_barrier((recv, pieces))
    half = ((256, 512), BF)
    square = ((512, 512), F32)
    feats, slope, tan_start, pushed_a = call(
        front_first_kernel,
        "front_first",
        [((512, D), BF), square, square, half],
        pos, *pieces, gate_weight, up_weight, *starts,
        mib=16,
    )
    slope, tan_start, pushed_b = call(
        front_second_kernel,
        "front_second",
        [square, square, half],
        pos, feats, gate_weight, up_weight, *starts, slope, tan_start,
        aliases={8: 0, 9: 1},
    )
    pushed = [pushed_a, pushed_b]
    recv = call(join_kernel, "join", [((512, 2048), BF)], pos, recv, shift(recv, "c", 1))
    row, block = (4, 512, 128), (512, 128)

    other = [shift(v, "yl", 1) for v in pushed]
    feats_c = shift(after(feats, recv), "c", 1)
    own_gram = call(own_gram_kernel, "own_gram", [((512, 512), F32)], after(feats, pushed))
    quarter = call(quarter_kernel, "quarter", [((128, D), BF)], pos, after(feats, *pushed))
    other[0], own_gram, feats_c, quarter = lax.optimization_barrier((other[0], own_gram, feats_c, quarter))
    parts = push_down(pos, pushed, other, keep, recv, row, block)
    quarter = shift(after(quarter, parts[0]), "yh", 1)
    parts = scatter(parts)
    moved, weighted = call(
        weigh_first_kernel, "weigh", [((512, 128), F32), ((512, 128), BF)], *parts, curvature
    )
    quarter, weighted = lax.optimization_barrier((quarter, weighted))
    pieces, quarter_c = gather(weighted, shift(quarter, "c", 1))
    far_gram = call(far_gram_kernel, "far_gram", [((512, 256), F32)], feats, quarter, quarter_c)
    recv_one, far_gram = lax.optimization_barrier((recv, far_gram))
    full, *send = call(
        back_kernel, "back_other", [((512, 2048), BF), ((256, 512), BF), ((256, 512), BF)], pos, *pieces, recv_one
    )
    got = [shift(v, "yl", 1) for v in send]
    far_gram = after(far_gram, *send)
    far_grams = [far_gram, shift(far_gram, "x", 1), shift(far_gram, "z", 1), shift(far_gram, "x", 3)]
    own = call(own_back_kernel, "back_own", [((512, 512), F32)], full, keep)
    got, far_grams = lax.optimization_barrier((got, far_grams))
    delta = call(delta_first_kernel, "delta", [((528, 512), BF)], own, *got, slope, tan_start, squares)
    deltas = [delta, shift(delta, "c", 1)]
    far_delta = shift(delta, "yh", 1)
    core_gram = call(core_gram_kernel, "core_gram", [((512, 512), F32)], after(feats, delta), feats_c)
    high, low = call(
        gram_split_kernel,
        "gram_split",
        [((512, 2048), BF)] * 2,
        pos, after(own_gram, delta), core_gram, *far_grams,
    )
    near = call(near_tangent_kernel, "near_tangent", [((512, 512), F32)], high, low, *deltas)
    far_delta, near = lax.optimization_barrier((far_delta, near))
    deltas += [far_delta, shift(far_delta, "c", 1)]
    near = call(middle_tangent_kernel, "middle_tangent", [((512, 512), F32)], near, high, low, far_delta)
    tan_image, *pushed = call(
        far_tangent_kernel,
        "far_tangent",
        [((512, 512), F32), ((272, 512), BF), ((256, 512), BF)],
        near, high, low, *deltas, slope,
    )

    row, block = (4, 528, 128), (528, 128)
    other = [shift(v, "yl", 1) for v in pushed]
    first_deltas = deltas
    rows = [call(rows_kernel, "rows", [((1024, 512), BF)], pos, after(f, *pushed)) for f in (feats, feats_c)]
    near_one = call(near_image_kernel, "near_image", [((1024, 512), F32)], *rows, *first_deltas[:2])
    theirs = call(their_rows_kernel, "their_rows", [((512, 2048), BF)], pos, after(feats, *pushed))
    other[0], near_one, theirs = lax.optimization_barrier((other[0], near_one, theirs))
    parts = push_down(pos, pushed, other, keep, recv, row, block)
    far_rows = shift(after(theirs, parts[0]), "yh", 1)
    parts = scatter(parts)
    weighted, scalars = call(
        weigh_second_kernel, "weigh", [((512, 128), BF), ((8, 128), F32)], *parts, curvature, moved
    )
    pieces, _ = gather(weighted)
    full, *send = call(
        back_kernel, "back_other", [((512, 2048), BF), ((256, 512), BF), ((256, 512), BF)], pos, *pieces, recv
    )
    got = [shift(v, "yl", 1) for v in send]
    own = call(own_back_kernel, "back_own", [((512, 512), F32)], full, keep)
    mine, theirs = call(far_rows_kernel, "far_rows", [((1024, 512), BF)] * 2, pos, after(far_rows, *send))
    got, mine, theirs = lax.optimization_barrier((got, mine, theirs))
    rows += [mine, shift(theirs, "c", 1)]
    delta, sums = call(
        delta_second_kernel,
        "delta",
        [((512, 512), BF), ((8, 128), F32)],
        own, *got, slope, tan_start, tan_image, delta,
    )
    deltas = [delta, shift(delta, "c", 1)]
    far_delta = shift(delta, "yh", 1)
    image_one = call(
        far_image_kernel, "far_image", [((1024, 512), F32)], after(near_one, delta), *rows[2:], *first_deltas[2:]
    )
    near = call(near_image_kernel, "near_image", [((1024, 512), F32)], *rows[:2], *deltas)
    far_delta, near, image_one = lax.optimization_barrier((far_delta, near, image_one))
    deltas += [far_delta, shift(far_delta, "c", 1)]
    near = call(middle_image_kernel, "middle_image", [((1024, 512), F32)], near, rows[2], far_delta)
    image_two, block = call(
        last_image_kernel, "last_image", [((1024, 512), F32), ((8, 128), F32)], near, rows[3], deltas[3], sums
    )
    got = lax.all_to_all(jnp.broadcast_to(block[None], (128, 8, 128)), NAMES, 0, 0, tiled=True)
    whole = lambda *s: pl.BlockSpec(s, lambda i: (0,) * len(s))
    band = pl.BlockSpec((256, 512), lambda i: (i, 0))
    next_vector, coefficients = pl.pallas_call(
        final_kernel,
        grid=(4,),
        out_shape=[jax.ShapeDtypeStruct((1024, 512), F32), jax.ShapeDtypeStruct((4,), F32)],
        in_specs=[whole(128, 8, 128), whole(8, 128), band, band, band],
        out_specs=[band, SM],
        compiler_params=pltpu.CompilerParams(vmem_limit_bytes=16 * MIB),
        name="final",
    )(got, scalars, start, image_one, image_two)
    return (coefficients, next_vector)


def solution(mesh):
    inner = Mesh(mesh.devices.reshape([n for _, n in AXES]), NAMES)
    dp, fsdp = ("yh", "c"), ("x", "z", "yl")
    in_specs = (P(dp, fsdp), P(None, fsdp), P(None, fsdp), P(fsdp, None), P(dp, fsdp), P(dp, fsdp))
    out_specs = (P(), P(dp, fsdp))
    return jax.shard_map(shards, mesh=inner, in_specs=in_specs, out_specs=out_specs, check_vma=False)
```
